128 devices in a mesh: expert: 64 (over x, z, y), tensor: 2 (over core).
Axes of the slice: x: 4, y: 4, z: 4, core: 2. Of those that a mesh axis runs over, the one named last changes fastest.
Arguments:
- tokens: bfloat16 [16384, 768], P('expert'), may hold values from -6 to 6
- cotangent: bfloat16 [16384, 768], P('expert'), may hold values from -6 to 6
- segment_ids: int32 [16384], P('expert'), may hold values from 0 to 5, as said below
- expert_ids: int32 [16384, 2], P('expert'), may hold values from 0 to 63, all different within a row; in each aligned block of 256 rows (0 to 255, 256 to 511, ...) at most 12 rows name the same one
- attention: bfloat16 [2, 768, 3, 768], P(None, 'expert', None, 'tensor'), may hold values from -0.21875 to 0.21875
- combiner: bfloat16 [2, 768, 768], P(None, 'tensor', 'expert'), may hold values from -0.625 to 0.625
- expander: bfloat16 [768, 2, 3072], P('expert', None, 'tensor'), may hold values from -0.21875 to 0.21875
- reducer: bfloat16 [3072, 768], P('tensor', 'expert'), may hold values from -0.109375 to 0.109375
- router: bfloat16 [768, 64], P('expert'), may hold values from -0.15625 to 0.15625
- widener: bfloat16 [64, 768, 2, 3072], P('expert', None, None, 'tensor'), may hold values from -0.21875 to 0.21875
- narrower: bfloat16 [64, 3072, 768], P('expert', 'tensor'), may hold values from -0.109375 to 0.109375
- norm_gains: bfloat16 [4, 768], P(None, 'expert'), may hold values from 0.5 to 1.5
- rel_bias: bfloat16 [64, 12], P('expert', 'tensor'), may hold values from -3 to 3
Outputs:
- layer_out: float32 [16384, 768], P('expert')
- tokens_grad: float32 [16384, 768], P('expert')
- attention_grad: float32 [2, 768, 3, 768], P(None, 'expert', None, 'tensor')
- combiner_grad: float32 [2, 768, 768], P(None, 'tensor', 'expert')
- expander_grad: float32 [768, 2, 3072], P('expert', None, 'tensor')
- reducer_grad: float32 [3072, 768], P('tensor', 'expert')
- router_grad: float32 [768, 64], P('expert')
- widener_grad: float32 [64, 768, 2, 3072], P('expert', None, None, 'tensor')
- narrower_grad: float32 [64, 3072, 768], P('expert', 'tensor')
- gains_grad: float32 [4, 768], P(None, 'expert')
- bias_grad: float32 [64, 12], P('expert', 'tensor')
The draws below stay inside these ranges and needn't reach their ends.
Inputs may be any that keep to these rules, and one draw needn't show every extreme that they name: `segment_ids`: within each aligned block of 256 rows (the rows of one index of expert) the ids start at 0, never fall and rise by one at each of at most five places; rows with one id in a block form one sequence in order. Some block is one sequence of 256 rows and some block holds six sequences. `expert_ids`: the two ids of a row differ. Within each aligned block of 256 rows no expert is named by more than 12 rows.
All inputs are finite; a program needn't handle non-finite values.
Results may differ from the reference program's by a relative error of at most 0.035.
Values may be sent and summed in bfloat16 or wider, within the bound.
A program may use at most 256 MiB of HBM per device.

```python
import math
import jax
import jax.numpy as jnp
import numpy as np
from jax import lax

D = 768
HEADS = 12
HEAD_DIM = 64
FF = 3072
BUCKETS = 32
EXPERTS = 64
ROWS = 256
CAP = 12
TOKENS = 16384


def draw_segment_ids(key, part):
    blocks = TOKENS // ROWS
    key_cuts, key_counts, key_pick = jax.random.split(key, 3)
    block_keys = jax.random.split(key_cuts, blocks)
    cut_rows = jax.vmap(lambda one_key: jax.random.permutation(one_key, ROWS - 1)[:5] + 1)(block_keys)
    counts = jax.random.randint(key_counts, (blocks,), 1, 6)
    chosen = jax.random.permutation(key_pick, blocks)
    counts = counts.at[chosen[0]].set(0).at[chosen[1]].set(5)
    active = jnp.arange(5)[None, :] < counts[:, None]
    position = jnp.arange(ROWS)
    crossed = (cut_rows[:, None, :] <= position[None, :, None]) & active[:, None, :]
    return jnp.sum(crossed.astype(jnp.int32), axis=2).reshape(TOKENS).astype(jnp.int32)


def steps_of(key, extent, cuts, least, high):
    def one(dim, blocks):
        heights = jax.random.uniform(jax.random.fold_in(jax.random.fold_in(key, 6), dim), (blocks,), jnp.float32, least / len(cuts), high / len(cuts))
        return jnp.repeat(jnp.exp(heights), extent[dim] // blocks).reshape((-1,) + (1,) * (len(extent) - dim - 1))

    level = one(*cuts[0])
    for cut in cuts[1:]:
        level = level * one(*cut)
    return level


def routed_block(stream_key, own, number, rows, amount, top, reach, lean):
    sequence = jax.random.permutation(stream_key, amount)
    packed, usual = load_shares(amount, rows * top, reach, lean, True), load_shares(amount, rows * top, reach, lean, False)
    places = jnp.arange(amount)

    def named(tallies, rotation):
        used = int((tallies > 0).sum())
        fixed = max(1, used // 4)
        shifted = fixed + (places - fixed + rotation * (used - fixed)) % max(1, amount - fixed)
        return jnp.zeros((amount,), jnp.int32).at[sequence[jnp.where(places < fixed, places, shifted)]].set(jnp.asarray(tallies, jnp.int32))

    tallies = jnp.where(number % 4 == 0, named(packed, number // 4), named(usual, number - number // 4 - 1))
    mixed = jax.random.permutation(jax.random.fold_in(own, 3), amount)
    donor, sink = mixed[0:amount // 2 * 2:2], mixed[1:amount // 2 * 2:2]
    room = jnp.minimum(tallies[donor] - 1, reach - tallies[sink]) // 2
    room = jnp.where((donor == sequence[0]) | (sink == sequence[0]) | (tallies[sink] == 0), 0, jnp.maximum(room, 0))
    shifted = jax.random.randint(jax.random.fold_in(own, 4), (amount // 2,), 0, 1 << 20) % (room + 1)
    tallies = tallies.at[donor].add(-shifted).at[sink].add(shifted)
    items = jnp.searchsorted(jnp.cumsum(tallies), jnp.arange(rows * top), side="right").astype(jnp.int32)
    table = items.reshape(top, rows).T
    table = table[jax.random.permutation(jax.random.fold_in(own, 1), rows)]
    rotation = jax.random.randint(jax.random.fold_in(own, 2), (rows, 1), 0, top)
    return jnp.take_along_axis(table, (jnp.arange(top)[None, :] + rotation) % top, axis=1)


def load_shares(count, total, bound, slope, full):
    portions = [(1 << 20) // math.isqrt(rank ** slope) + 1 for rank in range(1, count + 1)]
    largest = bound if full else min(bound, max(-(-total // count), total * portions[0] // sum(portions)))
    least = 1 if total - largest >= count - 1 else 0
    holding, surplus = [largest] + [least] * (count - 1), total - largest - least * (count - 1)
    while surplus > 0:
        candidates = [i for i in range(1, count) if holding[i] < largest] or [i for i in range(1, count) if holding[i] < bound]
        pool, left = sum([portions[i] for i in candidates]), surplus
        for i in candidates:
            more = min(bound - holding[i], max(1, left * portions[i] // pool), surplus)
            holding[i] = holding[i] + more
            surplus = surplus - more
    return np.array(holding)


def noise(own_key, extent, width, bound, cuts=(), held_as=jnp.bfloat16):
    array = jax.random.normal(own_key, extent, jnp.float32) * width
    if len(cuts) > 0:
        array = steps_of(own_key, extent, cuts, -0.22, 0.18) * array
    return jnp.clip(array, min=-bound, max=bound).astype(held_as)


def setup_inputs(seed: int = 0) -> dict:
    splits = jax.random.split(jax.random.key(seed), 14)
    tokens = noise(splits[0], (TOKENS, D), 1.0, 6.0, ((0, 64),))
    cotangent = noise(splits[1], (TOKENS, D), 1.0, 6.0, ((0, 64),))
    segment_ids = draw_segment_ids(jax.random.fold_in(splits[13], 71), 0)
    expert_ids_keys = jax.random.split(jax.random.fold_in(splits[3], 1), TOKENS // ROWS)
    expert_ids_turns = jax.random.permutation(jax.random.fold_in(splits[3], 3), TOKENS // ROWS)
    expert_ids = jax.vmap(lambda own, number: routed_block(jax.random.fold_in(splits[3], 2), own, number, ROWS, EXPERTS, 2, CAP, 2))(expert_ids_keys, expert_ids_turns).reshape((TOKENS, 2))
    attention = noise(splits[4], (2, D, 3, HEADS * HEAD_DIM), D ** -0.5, 0.21875, ((1, 64), (3, 2)))
    combiner = noise(splits[5], (2, HEADS * HEAD_DIM, D), (HEADS * HEAD_DIM // 8) ** -0.5, 0.625, ((1, 2), (2, 64)))
    expander = noise(splits[6], (D, 2, FF), D ** -0.5, 0.21875, ((0, 64), (2, 2)))
    reducer = noise(splits[7], (FF, D), FF ** -0.5, 0.109375, ((0, 2), (1, 64)))
    router = noise(splits[8], (D, EXPERTS), (2 * D) ** -0.5, 0.15625, ((0, 64),))
    widener = noise(splits[9], (EXPERTS, D, 2, FF), D ** -0.5, 0.21875, ((0, 64), (3, 2)))
    narrower = noise(splits[10], (EXPERTS, FF, D), FF ** -0.5, 0.109375, ((0, 64), (1, 2)))
    norm_gains = jnp.clip(1.0 + 0.1 * jax.random.normal(splits[11], (4, D), jnp.float32), 0.5, 1.5).astype(jnp.bfloat16)
    rel_bias = noise(splits[12], (2 * BUCKETS, HEADS), 0.5, 3.0, ((0, 64), (1, 2)))
    return {"tokens": tokens, "cotangent": cotangent, "segment_ids": segment_ids, "expert_ids": expert_ids, "attention": attention, "combiner": combiner, "expander": expander, "reducer": reducer, "router": router, "widener": widener, "narrower": narrower, "norm_gains": norm_gains, "rel_bias": rel_bias}


EPSILON = 1e-06
NEG_FILL = -1000000000.0
REACH_RATIO = 8.0
GELU_COEF = 0.7978845608028654
HIGH_PREC = lax.Precision.HIGHEST

@jax.custom_vjp
def low(v):
    return lax.optimization_barrier(v.astype(jnp.bfloat16)).astype(jnp.float32)

@jax.custom_vjp
def low_back(v):
    return v

def low_keep(v):
    return (low(v), None)

def low_pass(kept, grad):
    return (grad,)

def back_keep(v):
    return (v, None)

def back_low(kept, grad):
    return (low(grad),)
low.defvjp(low_keep, low_pass)
low_back.defvjp(back_keep, back_low)

def bucket_onehot(length, buckets):
    offsets = np.maximum(np.arange(length)[:, None] - np.arange(length)[None, :], 0)
    exact_span = buckets // 2
    levels = np.arange(1, buckets - exact_span)
    bounds = exact_span * REACH_RATIO ** (levels / exact_span)
    far_bucket = exact_span + np.sum(offsets[:, :, None] >= bounds[None, None, :], axis=2)
    bucket_index = np.where(offsets < exact_span, offsets, far_bucket)
    return (bucket_index[:, :, None] == np.arange(buckets)[None, None, :]).astype(np.float32)

def gated_gelu(gate_up):
    gate_part = gate_up[..., 0, :]
    up_part = gate_up[..., 1, :]
    inner_arg = GELU_COEF * (gate_part + 0.044715 * gate_part * gate_part * gate_part)
    return 0.5 * gate_part * (1.0 + jnp.tanh(inner_arg)) * up_part

def rms_norm(hidden, gain_row):
    factor = lax.rsqrt(lax.optimization_barrier(jnp.mean(hidden * hidden, axis=-1, keepdims=True)) + EPSILON)
    return hidden * factor * gain_row

def attend_group(normed, segments, weight_qkv, bias_table, onehot):
    row_count = normed.shape[0]
    heads_all = bias_table.shape[1]
    projected = low_back(low(jnp.einsum('rd,dkf->rkf', normed, weight_qkv, precision=HIGH_PREC)))
    by_head = projected.reshape(row_count, 3, heads_all, HEAD_DIM)
    position = jnp.arange(row_count)
    allowed = (segments[:, None] == segments[None, :]) & (position[:, None] >= position[None, :])
    rel_terms = jnp.einsum('ijb,bh->hij', onehot, bias_table, precision=HIGH_PREC)
    raw_scores = jnp.einsum('ihd,jhd->hij', by_head[:, 0], by_head[:, 1], precision=HIGH_PREC) * HEAD_DIM ** (-0.5)
    scores = low_back(raw_scores + rel_terms)
    scores = jnp.where(allowed[None], scores, NEG_FILL)
    row_peak = lax.optimization_barrier(jnp.max(scores, axis=-1, keepdims=True))
    raised = jnp.exp(scores - row_peak)
    attn_probs = low(raised / lax.optimization_barrier(jnp.sum(raised, axis=-1, keepdims=True)))
    mixed_rows = low_back(low(jnp.einsum('hij,jhd->ihd', attn_probs, by_head[:, 2], precision=HIGH_PREC)))
    return mixed_rows.reshape(row_count, heads_all * HEAD_DIM)

def experts_branch(normed, router, widener, narrower, expert_ids, groups):
    logits = low_back(jnp.dot(normed, router, precision=HIGH_PREC, preferred_element_type=jnp.float32))
    choose = (expert_ids[:, :, None] == jnp.arange(EXPERTS)[None, None, :]).astype(jnp.float32)
    picked = lax.optimization_barrier(jnp.sum(choose * logits[:, None, :], axis=2))
    margin = picked[:, 0] - picked[:, 1]
    gate_pair = jnp.stack([1.0 / (1.0 + jnp.exp(-margin)), 1.0 / (1.0 + jnp.exp(margin))], axis=1)
    pair_ids = expert_ids.reshape(groups, 2 * ROWS)
    onehot_ids = (pair_ids[:, :, None] == jnp.arange(EXPERTS)[None, None, :]).astype(jnp.int32)
    earlier = jnp.cumsum(onehot_ids, axis=1) - onehot_ids
    slot_rank = lax.optimization_barrier(jnp.sum(earlier * onehot_ids, axis=2)).astype(jnp.int32)
    target = (pair_ids * CAP + slot_rank).astype(jnp.int32)
    source = jnp.repeat(normed.reshape(groups, ROWS, D), 2, axis=1)

    def place_block(block_source, block_target):
        return jnp.zeros((EXPERTS * CAP, D), jnp.float32).at[block_target].add(block_source)
    buffer = low_back(jax.vmap(place_block)(source, target))
    received = buffer.reshape(groups, EXPERTS, CAP, D).transpose(1, 0, 2, 3).reshape(EXPERTS, groups * CAP, D)

    def one_expert(triple):
        expert_rows, weight_in, weight_out = triple
        gate_up = low_back(jnp.einsum('rd,dkf->rkf', expert_rows, weight_in, precision=HIGH_PREC))
        hidden = low(gated_gelu(gate_up))
        return low_back(low(jnp.dot(hidden, weight_out, precision=HIGH_PREC, preferred_element_type=jnp.float32)))
    produced = lax.map(jax.checkpoint(one_expert), (received, widener, narrower))
    returned = produced.reshape(EXPERTS, groups, CAP, D).transpose(1, 0, 2, 3).reshape(groups, EXPERTS * CAP, D)

    def pick_block(slot_block, slot_index):
        return slot_block[slot_index]
    chosen = jax.vmap(pick_block)(returned, target).reshape(TOKENS, 2, D)
    return lax.optimization_barrier(jnp.sum(gate_pair[:, :, None] * chosen, axis=1))

def forward(tok_values, attention, combiner, expander, reducer, router, widener, narrower, norm_gains, rel_bias, segment_ids, expert_ids):
    groups = TOKENS // ROWS
    onehot = jnp.asarray(bucket_onehot(ROWS, BUCKETS))
    seg_blocks = segment_ids.reshape(groups, ROWS)
    residual = tok_values
    for layer_index in range(2):
        bias_table = rel_bias[layer_index * BUCKETS:(layer_index + 1) * BUCKETS]
        weight_qkv = attention[layer_index]
        normed = low(rms_norm(residual, norm_gains[2 * layer_index]))

        def one_group(group_pair):
            return attend_group(group_pair[0], group_pair[1], weight_qkv, bias_table, onehot)
        mixed_rows = lax.map(jax.checkpoint(one_group), (normed.reshape(groups, ROWS, D), seg_blocks))
        mixed_rows = mixed_rows.reshape(TOKENS, HEADS * HEAD_DIM)
        residual = residual + low_back(jnp.dot(mixed_rows, combiner[layer_index], precision=HIGH_PREC, preferred_element_type=jnp.float32))
        normed = low(rms_norm(residual, norm_gains[2 * layer_index + 1]))
        if layer_index == 0:
            gate_up = low_back(jnp.einsum('rd,dkf->rkf', normed, expander, precision=HIGH_PREC))
            hidden = low(gated_gelu(gate_up))
            residual = residual + low_back(jnp.dot(hidden, reducer, precision=HIGH_PREC, preferred_element_type=jnp.float32))
        else:
            residual = residual + experts_branch(normed, router, widener, narrower, expert_ids, groups)
    return residual

def reference(tokens, cotangent, segment_ids, expert_ids, attention, combiner, expander, reducer, router, widener, narrower, norm_gains, rel_bias):

    def wrapped(tok_values, attn_values, comb_values, expand_values, reduce_values, router_values, widen_values, narrow_values, gain_values, bias_values):
        return forward(tok_values, attn_values, comb_values, expand_values, reduce_values, router_values, widen_values, narrow_values, gain_values, bias_values, segment_ids, expert_ids)
    result, pullback = jax.vjp(wrapped, tokens.astype(jnp.float32), attention.astype(jnp.float32), combiner.astype(jnp.float32), expander.astype(jnp.float32), reducer.astype(jnp.float32), router.astype(jnp.float32), widener.astype(jnp.float32), narrower.astype(jnp.float32), norm_gains.astype(jnp.float32), rel_bias.astype(jnp.float32))
    gradients = pullback(cotangent.astype(jnp.float32))
    return (result, gradients[0], gradients[1], gradients[2], gradients[3], gradients[4], gradients[5], gradients[6], gradients[7], gradients[8], gradients[9])
```

```python
import functools

import jax
import jax.numpy as jnp
import numpy as np
from jax import lax
from jax.experimental import pallas as pl
from jax.experimental.pallas import tpu as pltpu
from jax.sharding import PartitionSpec as P

HEAD_DIM = 64
EPSILON = 1e-06
NEG_FILL = -1000000000.0
REACH_RATIO = 8.0
GELU_COEF = 0.7978845608028654

MESH = pl.DeviceIdType.MESH
RING = 4
LANES = 128
BF = jnp.bfloat16
F32 = jnp.float32


def places():
    e = lax.axis_index("expert")
    return e // 16, (e // 4) % 4, e % 4


def neighbours():
    x, z, y = places()
    up, down = lambda v: (v + 1) % RING, lambda v: (v + 3) % RING
    at = lambda a, b, c: a * 16 + b * 4 + c
    return {
        "x": (at(up(x), z, y), at(down(x), z, y)),
        "z": (at(x, up(z), y), at(x, down(z), y)),
        "y": (at(x, z, up(y)), at(x, z, down(y))),
    }


def greet(near):
    barrier = pltpu.get_barrier_semaphore()
    for axis in "xzy":
        for peer in near[axis]:
            pl.semaphore_signal(barrier, inc=1, device_id={"expert": peer}, device_id_type=MESH)
    pl.semaphore_wait(barrier, 6)


def gather_kernel(split, cols, own, out, ring, block, sends, recvs, local_sem):
    near = neighbours()
    x, z, y = places()
    greet(near)

    def copy(k, src, dst, peer):
        return pltpu.make_async_remote_copy(
            src_ref=src, dst_ref=dst, send_sem=sends.at[k], recv_sem=recvs.at[k],
            device_id={"expert": peer}, device_id_type=MESH)

    def both_ways(k, axis, src, at, lo, mid, hi):
        m = {"x": x, "z": z, "y": y}[axis]
        up, down = near[axis]
        prev, nxt = (m + 3) % RING, (m + 1) % RING
        left, right, full = pl.ds(lo, mid - lo), pl.ds(mid, hi - mid), pl.ds(lo, hi - lo)
        first = copy(k, src, at(m, full), up)
        second = copy(k + 1, src, at(m, full), down)
        third = copy(k + 2, at(prev, left), at(prev, left), up)
        fourth = copy(k + 3, at(nxt, right), at(nxt, right), down)

        def start():
            first.start()
            second.start()

        def relay():
            first.wait_recv()
            third.start()
            second.wait_recv()
            fourth.start()

        def finish():
            third.wait_recv()
            fourth.wait_recv()
            for c in (first, second, third, fourth):
                c.wait_send()

        return start, relay, finish

    mid = cols // 2 // LANES * LANES
    start, relay, finish = both_ways(0, "y", own, lambda i, c: ring.at[i, :, c], 0, mid, cols)
    start()
    relay()
    ring[y] = own[...]
    finish()

    def assemble(t, carry):
        c = pl.ds(pl.multiple_of(t * LANES, LANES), LANES)
        parts = [ring[i, :, c].astype(F32)[:12] for i in range(RING)]
        block[:, c] = jnp.concatenate(parts, axis=0).astype(BF)
        return carry

    lax.fori_loop(0, cols // LANES, assemble, 0)
    keep = pltpu.make_async_copy(block, out.at[x, z], local_sem)
    keep.start()

    mid_a = split // 2 // LANES * LANES
    mid_b = (split + cols) // 2 // LANES * LANES
    a_cols, b_cols = pl.ds(0, split), pl.ds(split, cols - split)
    az = both_ways(4, "z", block.at[:, a_cols], lambda i, c: out.at[x, i, :, c], 0, mid_a, split)
    bx = both_ways(8, "x", block.at[:, b_cols], lambda i, c: out.at[i, z, :, c], split, mid_b, cols)
    az[0]()
    bx[0]()
    az[1]()
    bx[1]()
    keep.wait()
    az[2]()
    bx[2]()
    ax = both_ways(12, "x", out.at[x, :, :, a_cols], lambda i, c: out.at[i, :, :, c], 0, mid_a, split)
    bz = both_ways(16, "z", out.at[:, z, :, b_cols], lambda i, c: out.at[:, i, :, c], split, mid_b, cols)
    ax[0]()
    bz[0]()
    ax[1]()
    bz[1]()
    ax[2]()
    bz[2]()


def gather_rows(own):
    cols = own.shape[1]
    split = cols // 2 // LANES * LANES
    out = pl.pallas_call(
        functools.partial(gather_kernel, split, cols),
        out_shape=jax.ShapeDtypeStruct((RING, RING, 48, cols), BF),
        in_specs=[pl.BlockSpec(memory_space=pltpu.VMEM)],
        out_specs=pl.BlockSpec(memory_space=pltpu.HBM),
        scratch_shapes=[
            pltpu.VMEM((RING, 16, cols), BF),
            pltpu.VMEM((48, cols), BF),
            pltpu.SemaphoreType.DMA((20,)),
            pltpu.SemaphoreType.DMA((20,)),
            pltpu.SemaphoreType.DMA,
        ],
        compiler_params=pltpu.CompilerParams(
            collective_id=0, has_side_effects=True, vmem_limit_bytes=40 << 20),
    )(own)
    return out.reshape(768, cols)


def scatter_kernel(split, cols, grads, out, ra1, rb1, fa1, fb1, sa, sb, ra2, rb2, fa2, fb2,
                   sy, ry, fy, sends, recvs):
    near = neighbours()
    x, z, y = places()
    greet(near)

    def copy(k, src, dst, peer):
        return pltpu.make_async_remote_copy(
            src_ref=src, dst_ref=dst, send_sem=sends.at[k], recv_sem=recvs.at[k],
            device_id={"expert": peer}, device_id_type=MESH)

    def ring_sum(k, axis, at, load, relay_buf, final_buf, lead, lo, hi, store):
        width = hi - lo
        half = width // 2 // LANES * LANES
        m = {"x": x, "z": z, "y": y}[axis]
        up, down = near[axis]
        p, q, o = (m + 1) % RING, (m + 3) % RING, (m + 2) % RING
        left, right = pl.ds(0, half), pl.ds(half, width - half)
        g_left, g_right = pl.ds(lo, half), pl.ds(lo + half, width - half)
        c = [
            copy(k, at(o, g_left), relay_buf.at[..., left], up),
            copy(k + 1, at(o, g_right), relay_buf.at[..., right], down),
            copy(k + 2, at(p, g_right), final_buf.at[0, ..., right], up),
            copy(k + 3, at(q, g_left), final_buf.at[1, ..., left], down),
            copy(k + 4, relay_buf.at[..., left], final_buf.at[0, ..., left], up),
            copy(k + 5, relay_buf.at[..., right], final_buf.at[1, ..., right], down),
        ]

        def tiles(first, count, dest):
            def body(t, carry):
                off = pl.multiple_of(first + t * LANES, LANES)
                here, there = pl.ds(off, LANES), pl.ds(pl.multiple_of(lo + off, LANES), LANES)
                for i in range(lead or 1):
                    ix = (i,) if lead else ()
                    relay_buf[(*ix, slice(None), here)] = (
                        relay_buf[(*ix, slice(None), here)].astype(F32)
                        + load(dest, i, there).astype(F32)).astype(BF)
                return carry
            lax.fori_loop(0, count, body, 0)

        def start():
            for j in range(4):
                c[j].start()

        def relay():
            c[0].wait_recv()
            tiles(0, half // LANES, p)
            c[4].start()
            c[1].wait_recv()
            tiles(half, (width - half) // LANES, q)
            c[5].start()

        def finish():
            for j in range(2, 6):
                c[j].wait_recv()

            def body(t, carry):
                here = pl.ds(pl.multiple_of(t * LANES, LANES), LANES)
                there = pl.ds(pl.multiple_of(lo + t * LANES, LANES), LANES)
                for i in range(lead or 1):
                    ix = (i,) if lead else ()
                    total = (load(m, i, there).astype(F32)
                             + final_buf[(0, *ix, slice(None), here)].astype(F32)
                             + final_buf[(1, *ix, slice(None), here)].astype(F32))
                    store(i, here, there, total)
                return carry
            lax.fori_loop(0, width // LANES, body, 0)
            for j in range(6):
                c[j].wait_send()

        return start, relay, finish

    def store_to(ref):
        def store(i, here, there, total):
            ref[i, :, here] = total.astype(BF)
        return store

    def store_parts(i, here, there, total):
        for k in range(RING):
            part = total[12 * k:12 * k + 12]
            sy[k, :, there] = jnp.concatenate([part, jnp.zeros((4, LANES), F32)], axis=0).astype(BF)

    def store_out(i, here, there, total):
        out[:, there] = total

    a1 = ring_sum(0, "x", lambda i, c: grads.at[i, :, :, c], lambda d, i, c: grads[d, i, :, c],
                  ra1, fa1, RING, 0, split, store_to(sa))
    b1 = ring_sum(6, "z", lambda i, c: grads.at[:, i, :, c], lambda d, i, c: grads[i, d, :, c],
                  rb1, fb1, RING, split, cols, store_to(sb))
    for step in range(3):
        a1[step]()
        b1[step]()

    a2 = ring_sum(12, "z", lambda i, c: sa.at[i, :, c], lambda d, i, c: sa[d, :, c],
                  ra2, fa2, 0, 0, split, store_parts)

    def sb_at(i, c):
        return sb.at[i, :, pl.ds(c.start - split, c.size)]

    def sb_load(d, i, c):
        return sb[d, :, pl.ds(pl.multiple_of(c.start - split, LANES), LANES)]

    b2 = ring_sum(18, "x", sb_at, sb_load, rb2, fb2, 0, split, cols, store_parts)
    for step in range(3):
        a2[step]()
        b2[step]()
    last = ring_sum(24, "y", lambda i, c: sy.at[i, :, c], lambda d, i, c: sy[d, :, c],
                    ry, fy, 0, 0, cols, store_out)
    for step in range(3):
        last[step]()


def scatter_rows(grads):
    cols = grads.shape[1]
    split = cols // 2 // LANES * LANES
    rest = cols - split
    vm = lambda *shape: pltpu.VMEM(shape, BF)
    return pl.pallas_call(
        functools.partial(scatter_kernel, split, cols),
        out_shape=jax.ShapeDtypeStruct((16, cols), F32),
        in_specs=[pl.BlockSpec(memory_space=pltpu.VMEM)],
        out_specs=pl.BlockSpec(memory_space=pltpu.VMEM),
        scratch_shapes=[
            vm(RING, 48, split), vm(RING, 48, rest), vm(2, RING, 48, split), vm(2, RING, 48, rest),
            vm(RING, 48, split), vm(RING, 48, rest),
            vm(48, split), vm(48, rest), vm(2, 48, split), vm(2, 48, rest),
            vm(RING, 16, cols), vm(16, cols), vm(2, 16, cols),
            pltpu.SemaphoreType.DMA((30,)),
            pltpu.SemaphoreType.DMA((30,)),
        ],
        compiler_params=pltpu.CompilerParams(
            collective_id=1, has_side_effects=True, vmem_limit_bytes=56 << 20),
    )(grads.reshape(RING, RING, 48, cols))


ROWS = 256
WIDTH = 768
HALF = 384
HEADS = 6
COLS = 7808
CHUNKS = 6
SLOTS = 768
CAPACITY = 12
EXPERTS = 64
BUCKETS = 32
VMEM_BYTES = 56 << 20


def matmul(a, b):
    return jnp.dot(a, b, preferred_element_type=F32)


def matmul_nt(a, b):
    return lax.dot_general(a, b, (((1,), (1,)), ((), ())), preferred_element_type=F32)


def matmul_tn(a, b):
    return lax.dot_general(a, b, (((0,), (0,)), ((), ())), preferred_element_type=F32)


def norm_factor(v):
    return lax.rsqrt(jnp.mean(v * v, axis=-1, keepdims=True) + EPSILON)


def norm_back(v, gain, du):
    r = norm_factor(v)
    inner = jnp.sum(du * gain * v, axis=-1, keepdims=True) / WIDTH
    dgain = jnp.sum(du * v * r, axis=0, keepdims=True)
    return r * gain * du - v * (r * r * r) * inner, dgain


def pair_sum(own, recv):
    return own[...].astype(F32) + recv[...].astype(F32)


def gelu_parts(g):
    t = jnp.tanh(GELU_COEF * (g + 0.044715 * g * g * g))
    value = 0.5 * g * (1.0 + t)
    slope = 0.5 * (1.0 + t) + 0.5 * g * (1.0 - t * t) * GELU_COEF * (1.0 + 3 * 0.044715 * g * g)
    return value, slope


def swap_kernel(pick, mine, theirs, send, recv):
    t = lax.axis_index("tensor")
    peer = {"tensor": 1 - t}
    barrier = pltpu.get_barrier_semaphore()
    pl.semaphore_signal(barrier, inc=1, device_id=peer, device_id_type=MESH)
    pl.semaphore_wait(barrier, 1)
    move = pltpu.make_async_remote_copy(
        src_ref=mine.at[1 - t] if pick else mine, dst_ref=theirs, send_sem=send, recv_sem=recv,
        device_id=peer, device_id_type=MESH)
    move.start()
    move.wait()


def swap(mine, number, pick=False):
    shape = mine.shape[1:] if pick else mine.shape
    return pl.pallas_call(
        functools.partial(swap_kernel, pick),
        out_shape=jax.ShapeDtypeStruct(shape, mine.dtype),
        in_specs=[pl.BlockSpec(memory_space=pltpu.VMEM)],
        out_specs=pl.BlockSpec(memory_space=pltpu.VMEM),
        scratch_shapes=[pltpu.SemaphoreType.DMA, pltpu.SemaphoreType.DMA],
        compiler_params=pltpu.CompilerParams(collective_id=number, has_side_effects=True),
    )(mine)


def vm():
    return pl.BlockSpec(memory_space=pltpu.VMEM)


def full(shape):
    return pl.BlockSpec(shape, lambda *_: (0,) * len(shape))


def shaped(shape, dtype):
    return jax.ShapeDtypeStruct(shape, dtype)


def params():
    return pltpu.CompilerParams(vmem_limit_bytes=VMEM_BYTES)


def attend_kernel(layer, summed, *refs):
    if summed:
        base, own, recv, weights, sides, lookup, seg_col, seg_row, x_out, na, qkv, probs, mixed, part = refs
        x = base[...] + pair_sum(own, recv)
    else:
        base, weights, sides, lookup, seg_col, seg_row, x_out, na, qkv, probs, mixed, part = refs
        x = base[...].astype(F32)
    x_out[...] = x
    gain = sides[64 + 2 * layer:65 + 2 * layer, :].astype(F32)
    normed = (x * norm_factor(x) * gain).astype(BF)
    na[...] = normed
    qkv[...] = matmul(normed, weights[:, :1152]).astype(BF)
    offsets = matmul_nt(sides[...], lookup[...])
    row = lax.broadcasted_iota(jnp.int32, (ROWS, ROWS), 0)
    col = lax.broadcasted_iota(jnp.int32, (ROWS, ROWS), 1)
    allowed = (seg_col[...] == seg_row[...]) & (col <= row)
    outs = []
    for h in range(HEADS):
        at = h * HEAD_DIM
        q = qkv[:, at:at + HEAD_DIM]
        k = qkv[:, HALF + at:HALF + at + HEAD_DIM]
        v = qkv[:, 2 * HALF + at:2 * HALF + at + HEAD_DIM]
        rel = pltpu.roll(jnp.broadcast_to(offsets[68 + h:69 + h, :], (ROWS, ROWS)), 0, 1,
                         stride=1, stride_axis=0)
        s = jnp.where(allowed, matmul_nt(q, k) * HEAD_DIM ** (-0.5) + rel, NEG_FILL)
        e = jnp.exp(s - jnp.max(s, axis=-1, keepdims=True))
        p = (e / jnp.sum(e, axis=-1, keepdims=True)).astype(BF)
        probs[h] = p
        outs.append(matmul(p, v))
    o = jnp.concatenate(outs, axis=1).astype(BF)
    mixed[...] = o
    part[...] = matmul_nt(o, weights[:, 1152:]).astype(BF)


def attend(layer, base, pair, whole, sides, lookup, seg_col, seg_row):
    n_in = 1 + len(pair)
    return pl.pallas_call(
        functools.partial(attend_kernel, layer, len(pair) > 0),
        grid=(1,),
        out_shape=(
            shaped((ROWS, WIDTH), F32), shaped((ROWS, WIDTH), BF), shaped((ROWS, 1152), BF),
            shaped((HEADS, ROWS, ROWS), BF), shaped((ROWS, HALF), BF), shaped((ROWS, WIDTH), BF)),
        in_specs=[full((ROWS, WIDTH))] * n_in + [
            pl.BlockSpec((WIDTH, 1536), lambda i: (0, 3 + layer)), full((128, WIDTH)),
            full((ROWS, WIDTH)), full((ROWS, 1)), full((1, ROWS))],
        out_specs=(
            full((ROWS, WIDTH)), full((ROWS, WIDTH)), full((ROWS, 1152)),
            full((HEADS, ROWS, ROWS)), full((ROWS, HALF)), full((ROWS, WIDTH))),
        compiler_params=params(),
    )(base, *pair, whole, sides, lookup, seg_col, seg_row)


def dense_kernel(base, own, recv, weights, sides, x_out, normed_out, gate_up, hidden, part, acc):
    c = pl.program_id(0)

    @pl.when(c == 0)
    def _():
        x = base[...] + pair_sum(own, recv)
        x_out[...] = x
        normed_out[...] = (x * norm_factor(x) * sides[65:66, :].astype(F32)).astype(BF)
        acc[...] = jnp.zeros_like(acc)

    gu = matmul(normed_out[...], weights[:, :512])
    gate_up[...] = gu.astype(BF)
    g, u = gu[:, :256], gu[:, 256:]
    t = jnp.tanh(GELU_COEF * (g + 0.044715 * g * g * g))
    hid = (0.5 * g * (1.0 + t) * u).astype(BF)
    hidden[...] = hid
    acc[...] += matmul_nt(hid, weights[:, 512:])

    @pl.when(c == CHUNKS - 1)
    def _():
        part[...] = acc[...].astype(BF)


def dense(base, own, recv, whole, sides):
    return pl.pallas_call(
        dense_kernel,
        grid=(CHUNKS,),
        out_shape=(
            shaped((ROWS, WIDTH), F32), shaped((ROWS, WIDTH), BF), shaped((ROWS, 3072), BF),
            shaped((ROWS, 1536), BF), shaped((ROWS, WIDTH), BF)),
        in_specs=[full((ROWS, WIDTH))] * 3 + [
            pl.BlockSpec((WIDTH, WIDTH), lambda c: (0, c)), full((128, WIDTH))],
        out_specs=(
            full((ROWS, WIDTH)), full((ROWS, WIDTH)),
            pl.BlockSpec((ROWS, 512), lambda c: (0, c)), pl.BlockSpec((ROWS, 256), lambda c: (0, c)),
            full((ROWS, WIDTH))),
        scratch_shapes=[pltpu.VMEM((ROWS, WIDTH), F32)],
        compiler_params=params(),
    )(base, own, recv, whole, sides)


def route_kernel(base, own, recv, sides, ids_col, ids_row, cot, x_out, normed_out, first, second,
                 weights_out, packed):
    t = lax.axis_index("tensor")
    x = base[...] + pair_sum(own, recv)
    x_out[...] = x
    normed = (x * norm_factor(x) * sides[67:68, :].astype(F32)).astype(BF)
    normed_out[...] = normed
    logits = matmul_nt(normed, sides[:64, :])
    experts_col = lax.broadcasted_iota(jnp.int32, (ROWS, EXPERTS), 1)
    one, two = ids_col[:, 0:1] == experts_col, ids_col[:, 1:2] == experts_col
    pick = lambda mask, v: jnp.sum(jnp.where(mask, v, 0.0), axis=1, keepdims=True)
    margin = pick(one, logits) - pick(two, logits)
    w1 = 1.0 / (1.0 + jnp.exp(-margin))
    w2 = 1.0 / (1.0 + jnp.exp(margin))
    weights_out[...] = jnp.concatenate([w1, w2], axis=1)
    row = lax.broadcasted_iota(jnp.int32, (ROWS, ROWS), 0)
    col = lax.broadcasted_iota(jnp.int32, (ROWS, ROWS), 1)
    as_low = lambda mask: jnp.where(mask, 1.0, 0.0).astype(BF)
    counts = matmul(as_low(col < row), as_low(one | two))
    slots_col = lax.broadcasted_iota(jnp.int32, (ROWS, SLOTS), 1)
    for k, (mask, out) in enumerate(((one, first), (two, second))):
        target = ids_col[:, k:k + 1] * CAPACITY + pick(mask, counts).astype(jnp.int32)
        out[...] = as_low(target == slots_col)
    experts_row = lax.broadcasted_iota(jnp.int32, (EXPERTS, ROWS), 0)
    one, two = ids_row[0:1, :] == experts_row, ids_row[1:2, :] == experts_row
    counts = matmul(as_low(one | two), as_low(row < col))
    slots_row = lax.broadcasted_iota(jnp.int32, (SLOTS, ROWS), 0)
    half = pl.ds(pl.multiple_of(t * HALF, HALF), HALF)
    g4 = cot[:, half].astype(F32)
    take, back = None, 0.0
    for k, (mask, w) in enumerate(((one, w1), (two, w2))):
        seen = jnp.sum(jnp.where(mask, counts, 0.0), axis=0, keepdims=True).astype(jnp.int32)
        target = ids_row[k:k + 1, :] * CAPACITY + seen
        here = target == slots_row
        take = here if take is None else take | here
        back = back + matmul(as_low(here), (w * g4).astype(BF))
    packed[:, :HALF] = matmul(as_low(take), normed_out[:, half]).astype(BF)
    packed[:, HALF:] = back.astype(BF)


def route(base, own, recv, sides, ids_col, ids_row, cot):
    return pl.pallas_call(
        route_kernel,
        out_shape=(
            shaped((ROWS, WIDTH), F32), shaped((ROWS, WIDTH), BF), shaped((ROWS, SLOTS), BF),
            shaped((ROWS, SLOTS), BF), shaped((ROWS, 2), F32), shaped((SLOTS, WIDTH), BF)),
        in_specs=[vm()] * 7,
        out_specs=(vm(),) * 6,
        compiler_params=params(),
    )(base, own, recv, sides, ids_col, ids_row, cot)


def expert_kernel(own, recv, wide_gate, wide_up, narrow, wide_grad, narrow_grad, back, xin, dy, x_turned, y_acc, dx_acc):
    c = pl.program_id(0)
    t = lax.axis_index("tensor")

    @pl.when(c == 0)
    def _():
        low = jnp.where(t == 0, own[...], recv[...])
        high = jnp.where(t == 0, recv[...], own[...])
        xin[:, :HALF] = low[:, :HALF]
        xin[:, HALF:] = high[:, :HALF]
        dy[:, :HALF] = low[:, HALF:]
        dy[:, HALF:] = high[:, HALF:]
        x_turned[...] = xin[...].T
        y_acc[...] = jnp.zeros_like(y_acc)
        dx_acc[...] = jnp.zeros_like(dx_acc)

    g, u = matmul(xin[...], wide_gate[...]), matmul(xin[...], wide_up[...])
    value, slope = gelu_parts(g)
    hid = (value * u).astype(BF)
    y_acc[...] += matmul(hid, narrow[...])
    narrow_grad[...] = matmul_tn(hid, dy[...])
    dh = matmul_nt(dy[...], narrow[...])
    dg, du = (dh * u * slope).astype(BF), (dh * value).astype(BF)
    dx_acc[...] += matmul_nt(dg, wide_gate[...]) + matmul_nt(du, wide_up[...])
    wide_grad[:, 0, :] = matmul(x_turned[...], dg)
    wide_grad[:, 1, :] = matmul(x_turned[...], du)

    @pl.when(c == CHUNKS - 1)
    def _():
        for h in range(2):
            back[h, :, :HALF] = y_acc[:, h * HALF:(h + 1) * HALF].astype(BF)
            back[h, :, HALF:] = dx_acc[:, h * HALF:(h + 1) * HALF].astype(BF)


def expert(own, recv, wide, narrow):
    return pl.pallas_call(
        expert_kernel,
        grid=(CHUNKS,),
        out_shape=(
            shaped((WIDTH, 2, 1536), F32), shaped((1536, WIDTH), F32), shaped((2, SLOTS, WIDTH), BF)),
        in_specs=[full((SLOTS, WIDTH)), full((SLOTS, WIDTH)),
                  pl.BlockSpec((WIDTH, 256), lambda c: (0, c)),
                  pl.BlockSpec((WIDTH, 256), lambda c: (0, CHUNKS + c)),
                  pl.BlockSpec((256, WIDTH), lambda c: (c, 0))],
        out_specs=(pl.BlockSpec((WIDTH, 2, 256), lambda c: (0, 0, c)), pl.BlockSpec((256, WIDTH), lambda c: (c, 0)),
                   full((2, SLOTS, WIDTH))),
        scratch_shapes=[pltpu.VMEM((SLOTS, WIDTH), BF), pltpu.VMEM((SLOTS, WIDTH), BF),
                        pltpu.VMEM((WIDTH, SLOTS), BF), pltpu.VMEM((SLOTS, WIDTH), F32),
                        pltpu.VMEM((SLOTS, WIDTH), F32)],
        compiler_params=params(),
    )(own, recv, wide, wide, narrow)


def combine_kernel(own, recv, first, second, weights, x, normed, cot, ids_col, sides,
                   out, g3, dgain, router_back):
    t = lax.axis_index("tensor")
    low = jnp.where(t == 0, own[...], recv[...])
    high = jnp.where(t == 0, recv[...], own[...])
    y = jnp.concatenate([low[:, :HALF], high[:, :HALF]], axis=1)
    dx = jnp.concatenate([low[:, HALF:], high[:, HALF:]], axis=1)
    g4 = cot[...].astype(F32)
    y1, y2 = matmul(first[...], y), matmul(second[...], y)
    w1, w2 = weights[:, 0:1], weights[:, 1:2]
    v = x[...]
    out[...] = v + (w1 * y1 + w2 * y2)
    dot = lambda a: jnp.sum(a * g4, axis=1, keepdims=True)
    dm = w1 * w2 * (dot(y1) - dot(y2))
    experts = lax.broadcasted_iota(jnp.int32, (ROWS, EXPERTS), 1)
    signs = (jnp.where(ids_col[:, 0:1] == experts, 1.0, 0.0)
             - jnp.where(ids_col[:, 1:2] == experts, 1.0, 0.0))
    dlogits = (dm * signs).astype(BF)
    router_back[...] = matmul_tn(dlogits, normed[...])
    dn = matmul(dlogits, sides[:64, :]) + matmul(first[...] + second[...], dx)
    dv, dg = norm_back(v, sides[67:68, :].astype(F32), dn)
    g3[...] = g4 + dv
    dgain[...] = dg


def combine(*operands):
    return pl.pallas_call(
        combine_kernel,
        out_shape=(shaped((ROWS, WIDTH), F32), shaped((ROWS, WIDTH), F32), shaped((1, WIDTH), F32),
                   shaped((EXPERTS, WIDTH), F32)),
        in_specs=[vm()] * len(operands),
        out_specs=(vm(),) * 4,
        compiler_params=params(),
    )(*operands)


def attend_back_kernel(layer, summed, *refs):
    if summed:
        (grad, own, recv, x, held, weights, sides, lookup, na, qkv, probs, mixed,
         held_out, part, bias_back, g_out, dgain) = refs
        dv, dg = norm_back(x[...], sides[65:66, :].astype(F32), pair_sum(own, recv))
        g = grad[...] + dv
        g_out[...] = g
        dgain[...] = dg
    else:
        grad, weights, sides, lookup, na, qkv, probs, mixed, held_out, part, bias_back = refs
        g = grad[...]
    db = g.astype(BF)
    held_out[:, 1152:] = matmul_tn(db, mixed[...]).astype(BF)
    back = matmul(db, weights[:, 1152:]).astype(BF)
    row = lax.broadcasted_iota(jnp.int32, (ROWS, ROWS), 0)
    col = lax.broadcasted_iota(jnp.int32, (ROWS, ROWS), 1)
    reverse = jnp.where(row + col == ROWS - 1, 1.0, 0.0).astype(BF)
    dq, dk, dv, sums = [], [], [], []
    for h in range(HEADS):
        at = h * HEAD_DIM
        q = qkv[:, at:at + HEAD_DIM]
        k = qkv[:, HALF + at:HALF + at + HEAD_DIM]
        v = qkv[:, 2 * HALF + at:2 * HALF + at + HEAD_DIM]
        d = back[:, at:at + HEAD_DIM]
        low = probs[h]
        p = low.astype(F32)
        dp = matmul_nt(d, v)
        ds = (p * (dp - jnp.sum(p * dp, axis=-1, keepdims=True))).astype(BF)
        turned = pltpu.roll(matmul(reverse, ds), 1, 1, stride=1, stride_axis=0)
        sums.append(jnp.sum(turned, axis=0, keepdims=True))
        dq.append(matmul(ds, k) * HEAD_DIM ** (-0.5))
        dk.append(matmul_tn(ds, q) * HEAD_DIM ** (-0.5))
        dv.append(matmul_tn(low, d))
    sums = jnp.concatenate(sums + [jnp.zeros((2, ROWS), F32)], axis=0)
    high = sums.astype(BF)
    rest = (sums - high.astype(F32)).astype(BF)
    bias_back[...] = matmul(high, lookup[...]) + matmul(rest, lookup[...])
    dqkv = jnp.concatenate(dq + dk + dv, axis=1).astype(BF)
    held_out[:, :1152] = matmul_tn(na[...], dqkv).astype(BF)
    part[...] = matmul_nt(dqkv, weights[:, :1152]).astype(BF)


def attend_back(layer, grad, extra, held, whole, sides, lookup, na, qkv, probs, mixed):
    summed = len(extra) > 0
    block = pl.BlockSpec((WIDTH, 1536), lambda i: (0, 3 + layer))
    rows = full((ROWS, WIDTH))
    in_specs = [rows] * (1 + len(extra))
    operands = [grad, *extra]
    aliases = {}
    if summed:
        aliases = {len(operands): 0}
        in_specs.append(pl.BlockSpec(memory_space=pl.ANY))
        operands.append(held)
    in_specs += [block, full((128, WIDTH)), full((ROWS, WIDTH)), rows, full((ROWS, 1152)),
                 full((HEADS, ROWS, ROWS)), full((ROWS, HALF))]
    operands += [whole, sides, lookup, na, qkv, probs, mixed]
    out_shape = [shaped((WIDTH, COLS), BF), shaped((ROWS, WIDTH), BF), shaped((8, WIDTH), F32)]
    out_specs = [block, rows, full((8, WIDTH))]
    if summed:
        out_shape += [shaped((ROWS, WIDTH), F32), shaped((1, WIDTH), F32)]
        out_specs += [rows, full((1, WIDTH))]
    return pl.pallas_call(
        functools.partial(attend_back_kernel, layer, summed),
        grid=(1,), out_shape=tuple(out_shape), in_specs=in_specs, out_specs=tuple(out_specs),
        input_output_aliases=aliases, compiler_params=params(),
    )(*operands)


def dense_back_kernel(grad, own, recv, x, held, weights, sides, normed, gate_up, hidden,
                      held_out, part, g_out, dgain, low, low_turned, normed_turned, acc):
    c = pl.program_id(0)

    @pl.when(c == 0)
    def _():
        dv, dg = norm_back(x[...], sides[66:67, :].astype(F32), pair_sum(own, recv))
        g = grad[...] + dv
        g_out[...] = g
        dgain[...] = dg
        low[...] = g.astype(BF)
        low_turned[...] = low[...].T
        normed_turned[...] = normed[...].T
        acc[...] = jnp.zeros_like(acc)

    held_out[:, 512:] = matmul(low_turned[...], hidden[...]).astype(BF)
    dh = matmul(low[...], weights[:, 512:])
    gu = gate_up[...].astype(F32)
    g, u = gu[:, :256], gu[:, 256:]
    value, slope = gelu_parts(g)
    dgu = jnp.concatenate([(dh * u * slope).astype(BF), (dh * value).astype(BF)], axis=1)
    held_out[:, :512] = matmul(normed_turned[...], dgu).astype(BF)
    acc[...] += matmul_nt(dgu, weights[:, :512])

    @pl.when(c == CHUNKS - 1)
    def _():
        part[...] = acc[...].astype(BF)


def dense_back(grad, own, recv, x, held, whole, sides, normed, gate_up, hidden):
    rows = full((ROWS, WIDTH))
    block = pl.BlockSpec((WIDTH, WIDTH), lambda c: (0, c))
    return pl.pallas_call(
        dense_back_kernel,
        grid=(CHUNKS,),
        out_shape=(shaped((WIDTH, COLS), BF), shaped((ROWS, WIDTH), BF), shaped((ROWS, WIDTH), F32),
                   shaped((1, WIDTH), F32)),
        in_specs=[rows, rows, rows, rows, pl.BlockSpec(memory_space=pl.ANY), block,
                  full((128, WIDTH)), rows, pl.BlockSpec((ROWS, 512), lambda c: (0, c)),
                  pl.BlockSpec((ROWS, 256), lambda c: (0, c))],
        out_specs=(block, rows, rows, full((1, WIDTH))),
        scratch_shapes=[pltpu.VMEM((ROWS, WIDTH), BF), pltpu.VMEM((WIDTH, ROWS), BF),
                        pltpu.VMEM((WIDTH, ROWS), BF), pltpu.VMEM((ROWS, WIDTH), F32)],
        input_output_aliases={4: 0},
        compiler_params=params(),
    )(grad, own, recv, x, held, whole, sides, normed, gate_up, hidden)


def finish_kernel(grad, own, recv, x, held, sides, router_back, gain1, gain2, gain3, bias1, bias2,
                  held_out, g_out, turned):
    dv, dg = norm_back(x[...].astype(F32), sides[64:65, :].astype(F32), pair_sum(own, recv))
    g_out[...] = grad[...] + dv
    turned[:64, :] = router_back[...]
    turned[64:68, :] = jnp.concatenate([dg, gain1[...], gain2[...], gain3[...]], axis=0)
    turned[68:76, :] = bias1[...] + bias2[...]
    turned[76:, :] = jnp.zeros((52, WIDTH), F32)
    held_out[...] = turned[...].T.astype(BF)


def finish(grad, own, recv, x, held, *rest):
    rows = full((ROWS, WIDTH))
    return pl.pallas_call(
        finish_kernel,
        grid=(1,),
        out_shape=(shaped((WIDTH, COLS), BF), shaped((ROWS, WIDTH), F32)),
        in_specs=[rows, rows, rows, rows, pl.BlockSpec(memory_space=pl.ANY)]
        + [full(r.shape) for r in rest],
        out_specs=(pl.BlockSpec((WIDTH, 128), lambda i: (0, 60)), rows),
        scratch_shapes=[pltpu.VMEM((128, WIDTH), F32)],
        input_output_aliases={4: 0},
        compiler_params=params(),
    )(grad, own, recv, x, held, *rest)


def bucket_lookup(layer):
    distance = (-np.arange(ROWS)) % ROWS
    exact = BUCKETS // 2
    levels = np.arange(1, BUCKETS - exact)
    bounds = exact * REACH_RATIO ** (levels / exact)
    far = exact + np.sum(distance[:, None] >= bounds[None, :], axis=1)
    bucket = np.where(distance < exact, distance, far)
    place = (layer * BUCKETS + bucket) * 12
    return jnp.asarray(place[:, None] == np.arange(WIDTH)[None, :], BF)


def across(packed):
    moved = lax.all_to_all(packed.reshape(EXPERTS, CAPACITY, WIDTH), "expert", 0, 0, tiled=True)
    return moved.reshape(SLOTS, WIDTH)


def chunked(a):
    return a.reshape(a.shape[0], 2, CHUNKS, 256).transpose(0, 2, 1, 3)


def local(tokens, cotangent, segment_ids, expert_ids, attention, combiner, expander, reducer,
          router, widener, narrower, norm_gains, rel_bias):
    feed = jnp.concatenate([chunked(expander), reducer.T.reshape(12, CHUNKS, 1, 256)], axis=2)
    small = jnp.concatenate(
        [router, norm_gains.T, jnp.pad(rel_bias, ((0, 11), (0, 0))), jnp.zeros((12, 54), BF)], axis=1)
    own = jnp.concatenate(
        [feed.reshape(12, -1), attention[0].reshape(12, -1), combiner[0].T,
         attention[1].reshape(12, -1), combiner[1].T, small], axis=1)
    whole = gather_rows(jnp.pad(own, ((0, 4), (0, 0))))
    sides = whole[:, 7680:].T
    seg_col, seg_row = segment_ids[:, None], segment_ids[None, :]
    ids_row = expert_ids.T
    look1, look2 = bucket_lookup(0), bucket_lookup(1)
    wide = widener[0].reshape(WIDTH, -1)

    x0, na1, qkv1, probs1, mixed1, part = attend(0, tokens, (), whole, sides, look1, seg_col, seg_row)
    x1, n2, gate_up, hidden, part2 = dense(x0, part, swap(part, 2), whole, sides)
    x2, na2, qkv2, probs2, mixed2, part = attend(
        1, x1, (part2, swap(part2, 2)), whole, sides, look2, seg_col, seg_row)
    x3, n4, first, second, weights, packed = route(
        x2, part, swap(part, 2), sides, expert_ids, ids_row, cotangent)
    arrived = across(packed)
    wide_grad, narrow_grad, back = expert(arrived, swap(arrived, 3), wide, narrower[0])
    t = lax.axis_index("tensor")
    mine = lax.dynamic_index_in_dim(back, t, 0, keepdims=False).astype(F32)
    total = (mine + swap(back, 4, pick=True).astype(F32)).astype(BF)
    returned = across(total)
    layer_out, g3, gain3, router_back = combine(
        returned, swap(returned, 3), first, second, weights, x3, n4, cotangent, expert_ids, sides)
    held, part, bias2 = attend_back(1, g3, (), None, whole, sides, look2, na2, qkv2, probs2, mixed2)
    held, part2, g2, gain2 = dense_back(
        g3, part, swap(part, 2), x2, held, whole, sides, n2, gate_up, hidden)
    held, part, bias1, g1, gain1 = attend_back(
        0, g2, (part2, swap(part2, 2), x1), held, whole, sides, look1, na1, qkv1, probs1, mixed1)
    held, g0 = finish(
        g1, part, swap(part, 2), x0, held, sides, router_back, gain1, gain2, gain3, bias1, bias2)
    summed = scatter_rows(held)[:12]
    feed = summed[:, :4608].reshape(12, CHUNKS, 3, 256)
    return (
        layer_out,
        g0,
        jnp.stack([summed[:, 4608:5760], summed[:, 6144:7296]]).reshape(2, 12, 3, HALF),
        jnp.stack([summed[:, 5760:6144].T, summed[:, 7296:7680].T]),
        feed[:, :, :2].transpose(0, 2, 1, 3).reshape(12, 2, 1536),
        feed[:, :, 2].reshape(12, 1536).T,
        summed[:, 7680:7744],
        wide_grad[None],
        narrow_grad[None],
        summed[:, 7744:7748].T,
        summed[:1, 7748:7754],
    )


def solution(mesh):
    in_specs = (
        P("expert", None),
        P("expert", None),
        P("expert"),
        P("expert", None),
        P(None, "expert", None, "tensor"),
        P(None, "tensor", "expert"),
        P("expert", None, "tensor"),
        P("tensor", "expert"),
        P("expert", None),
        P("expert", None, None, "tensor"),
        P("expert", "tensor", None),
        P(None, "expert"),
        P("expert", "tensor"),
    )
    out_specs = (
        P("expert", None),
        P("expert", None),
        P(None, "expert", None, "tensor"),
        P(None, "tensor", "expert"),
        P("expert", None, "tensor"),
        P("tensor", "expert"),
        P("expert", None),
        P("expert", None, None, "tensor"),
        P("expert", "tensor", None),
        P(None, "expert"),
        P("expert", "tensor"),
    )
    return jax.shard_map(local, mesh=mesh, in_specs=in_specs, out_specs=out_specs, check_vma=False)
```

```python
import functools

import jax
import jax.numpy as jnp
import numpy as np
from jax import lax
from jax.experimental import pallas as pl
from jax.experimental.pallas import tpu as pltpu
from jax.sharding import PartitionSpec as P

HEAD_DIM = 64
EPSILON = 1e-06
NEG_FILL = -1000000000.0
REACH_RATIO = 8.0
GELU_COEF = 0.7978845608028654

MESH = pl.DeviceIdType.MESH
RING = 4
LANES = 128
BF = jnp.bfloat16
F32 = jnp.float32


def places():
    e = lax.axis_index("expert")
    return e // 16, (e // 4) % 4, e % 4


def neighbours():
    x, z, y = places()
    up, down = lambda v: (v + 1) % RING, lambda v: (v + 3) % RING
    at = lambda a, b, c: a * 16 + b * 4 + c
    return {
        "x": (at(up(x), z, y), at(down(x), z, y)),
        "z": (at(x, up(z), y), at(x, down(z), y)),
        "y": (at(x, z, up(y)), at(x, z, down(y))),
    }


def greet(near):
    barrier = pltpu.get_barrier_semaphore()
    for axis in "xzy":
        for peer in near[axis]:
            pl.semaphore_signal(barrier, inc=1, device_id={"expert": peer}, device_id_type=MESH)
    pl.semaphore_wait(barrier, 6)


FOLDED = 2560
QUARTER = FOLDED // RING
SPLIT = 5120


def tile_at(t, base=0):
    return pl.ds(pl.multiple_of(base + t * LANES, LANES), LANES)


def gather_kernel(cols, own, out, ring, block, folded, whole_c, stage, sends, recvs, locals_):
    near = neighbours()
    x, z, y = places()
    greet(near)

    def copy(k, src, dst, peer):
        return pltpu.make_async_remote_copy(
            src_ref=src, dst_ref=dst, send_sem=sends.at[k], recv_sem=recvs.at[k],
            device_id={"expert": peer}, device_id_type=MESH)

    def both_ways(k, axis, src, at, lo, hi):
        m = {"x": x, "z": z, "y": y}[axis]
        up, down = near[axis]
        prev, nxt = (m + 3) % RING, (m + 1) % RING
        mid = (lo + hi) // 2 // LANES * LANES
        left, right, full = pl.ds(lo, mid - lo), pl.ds(mid, hi - mid), pl.ds(lo, hi - lo)
        first = copy(k, src, at(m, full), up)
        second = copy(k + 1, src, at(m, full), down)
        third = copy(k + 2, at(prev, left), at(prev, left), up)
        fourth = copy(k + 3, at(nxt, right), at(nxt, right), down)

        def start():
            first.start()
            second.start()

        def relay():
            first.wait_recv()
            third.start()
            second.wait_recv()
            fourth.start()

        def finish():
            third.wait_recv()
            fourth.wait_recv()
            for c in (first, second, third, fourth):
                c.wait_send()

        return start, relay, finish

    def run(*streams):
        for step in range(3):
            for stream in streams:
                stream[step]()

    ab_y = both_ways(0, "y", own.at[:, pl.ds(FOLDED, cols - FOLDED)],
                     lambda i, c: ring.at[i, :, c], 0, cols - FOLDED)
    ab_y[0]()
    for t in range(QUARTER // LANES):
        parts = [own[:, pl.ds(q * QUARTER + t * LANES, LANES)].astype(F32)[:12] for q in range(RING)]
        folded[:, pl.ds(t * LANES, LANES)] = jnp.concatenate(parts, axis=0).astype(BF)
    c_z = both_ways(4, "z", folded, lambda i, c: whole_c.at[x, i, y, :, c], 0, QUARTER)
    c_z[0]()
    whole_c[x, z, y] = folded[...]
    ring[y] = own[:, FOLDED:]
    ab_y[1]()
    c_z[1]()
    ab_y[2]()

    def assemble(t, carry):
        parts = [ring[i, :, tile_at(t)].astype(F32)[:12] for i in range(RING)]
        block[:, tile_at(t)] = jnp.concatenate(parts, axis=0).astype(BF)
        return carry

    lax.fori_loop(0, (cols - FOLDED) // LANES, assemble, 0)
    keep = pltpu.make_async_copy(block, out.at[x, z, :, pl.ds(FOLDED, cols - FOLDED)], locals_.at[2])
    keep.start()
    a_cols, b_cols = pl.ds(FOLDED, SPLIT - FOLDED), pl.ds(SPLIT, cols - SPLIT)
    a_z = both_ways(8, "z", block.at[:, pl.ds(0, SPLIT - FOLDED)], lambda i, c: out.at[x, i, :, c], FOLDED, SPLIT)
    b_x = both_ways(12, "x", block.at[:, pl.ds(SPLIT - FOLDED, cols - SPLIT)], lambda i, c: out.at[i, z, :, c],
                    SPLIT, cols)
    a_z[0]()
    b_x[0]()
    c_z[2]()
    c_x = both_ways(16, "x", whole_c.at[x, :, y], lambda i, c: whole_c.at[i, :, y, :, c], 0, QUARTER)
    c_x[0]()
    a_z[1]()
    b_x[1]()
    c_x[1]()
    keep.wait()
    a_z[2]()
    a_x = both_ways(20, "x", out.at[x, :, :, a_cols], lambda i, c: out.at[i, :, :, c], FOLDED, SPLIT)
    a_x[0]()
    b_x[2]()
    b_z = both_ways(24, "z", out.at[:, z, :, b_cols], lambda i, c: out.at[:, i, :, c], SPLIT, cols)
    b_z[0]()
    c_x[2]()
    c_y = both_ways(28, "y", whole_c.at[:, :, y], lambda i, c: whole_c.at[:, :, i, :, c], 0, QUARTER)
    c_y[0]()
    a_x[1]()
    b_z[1]()
    c_y[1]()
    c_y[2]()

    def unfold(n, slot):
        def one(t, carry):
            got = [whole_c[n // RING, n % RING, i, :, tile_at(t)].astype(F32) for i in range(RING)]
            for q in range(RING):
                parts = [g[12 * q:12 * q + 12] for g in got]
                stage[slot, :, tile_at(t, q * QUARTER)] = jnp.concatenate(parts, axis=0).astype(BF)
            return carry
        lax.fori_loop(0, QUARTER // LANES, one, 0)

    def write(n, slot):
        return pltpu.make_async_copy(
            stage.at[slot], out.at[n // RING, n % RING, :, pl.ds(0, FOLDED)], locals_.at[slot])

    def pair(j, carry):
        for slot in range(2):
            n = 2 * j + slot

            @pl.when(j > 0)
            def _():
                write(n, slot).wait()

            unfold(n, slot)
            write(n, slot).start()
        return carry

    lax.fori_loop(0, RING * RING // 2, pair, 0)
    for slot in range(2):
        write(slot, slot).wait()
    a_x[2]()
    b_z[2]()


def gather_rows(own):
    cols = own.shape[1]
    out = pl.pallas_call(
        functools.partial(gather_kernel, cols),
        out_shape=jax.ShapeDtypeStruct((RING, RING, 48, cols), BF),
        in_specs=[pl.BlockSpec(memory_space=pltpu.VMEM)],
        out_specs=pl.BlockSpec(memory_space=pltpu.HBM),
        scratch_shapes=[
            pltpu.VMEM((RING, 16, cols - FOLDED), BF),
            pltpu.VMEM((48, cols - FOLDED), BF),
            pltpu.VMEM((48, QUARTER), BF),
            pltpu.VMEM((RING, RING, RING, 48, QUARTER), BF),
            pltpu.VMEM((2, 48, FOLDED), BF),
            pltpu.SemaphoreType.DMA((32,)),
            pltpu.SemaphoreType.DMA((32,)),
            pltpu.SemaphoreType.DMA((3,)),
        ],
        compiler_params=pltpu.CompilerParams(
            collective_id=0, has_side_effects=True, vmem_limit_bytes=60 << 20),
    )(own)
    return out.reshape(768, cols)


def scatter_kernel(cols, grads, out, out_c, ra1, rb1, fa1, fb1, sa, sb, ra2, rb2, fa2, fb2,
                   sy, ry, fy, cf, rc1, fc1, sc1, rc2, fc2, sc2, rc3, fc3, sends, recvs):
    near = neighbours()
    x, z, y = places()
    greet(near)

    def copy(k, src, dst, peer):
        return pltpu.make_async_remote_copy(
            src_ref=src, dst_ref=dst, send_sem=sends.at[k], recv_sem=recvs.at[k],
            device_id={"expert": peer}, device_id_type=MESH)

    def ring_sum(k, axis, at, load, relay_buf, final_buf, lead, lo, hi, store):
        width = hi - lo
        half = width // 2 // LANES * LANES
        m = {"x": x, "z": z, "y": y}[axis]
        up, down = near[axis]
        p, q, o = (m + 1) % RING, (m + 3) % RING, (m + 2) % RING
        left, right = pl.ds(0, half), pl.ds(half, width - half)
        g_left, g_right = pl.ds(lo, half), pl.ds(lo + half, width - half)
        c = [
            copy(k, at(o, g_left), relay_buf.at[..., left], up),
            copy(k + 1, at(o, g_right), relay_buf.at[..., right], down),
            copy(k + 2, at(p, g_right), final_buf.at[0, ..., right], up),
            copy(k + 3, at(q, g_left), final_buf.at[1, ..., left], down),
            copy(k + 4, relay_buf.at[..., left], final_buf.at[0, ..., left], up),
            copy(k + 5, relay_buf.at[..., right], final_buf.at[1, ..., right], down),
        ]

        def tiles(first, count, dest):
            def body(t, carry):
                off = pl.multiple_of(first + t * LANES, LANES)
                here, there = pl.ds(off, LANES), pl.ds(pl.multiple_of(lo + off, LANES), LANES)
                for i in range(lead or 1):
                    ix = (i,) if lead else ()
                    relay_buf[(*ix, slice(None), here)] = (
                        relay_buf[(*ix, slice(None), here)].astype(F32)
                        + load(dest, i, there).astype(F32)).astype(BF)
                return carry
            lax.fori_loop(0, count, body, 0)

        def start():
            for j in range(4):
                c[j].start()

        def relay():
            c[0].wait_recv()
            tiles(0, half // LANES, p)
            c[4].start()
            c[1].wait_recv()
            tiles(half, (width - half) // LANES, q)
            c[5].start()

        def finish():
            for j in range(2, 6):
                c[j].wait_recv()

            def body(t, carry):
                here = pl.ds(pl.multiple_of(t * LANES, LANES), LANES)
                there = pl.ds(pl.multiple_of(lo + t * LANES, LANES), LANES)
                for i in range(lead or 1):
                    ix = (i,) if lead else ()
                    total = (load(m, i, there).astype(F32)
                             + final_buf[(0, *ix, slice(None), here)].astype(F32)
                             + final_buf[(1, *ix, slice(None), here)].astype(F32))
                    store(i, here, there, total)
                return carry
            lax.fori_loop(0, width // LANES, body, 0)
            for j in range(6):
                c[j].wait_send()

        return start, relay, finish

    def store_to(ref):
        def store(i, here, there, total):
            ref[i, :, here] = total.astype(BF)
        return store

    def store_parts_at(base):
        def store(i, here, there, total):
            spot = pl.ds(pl.multiple_of(there.start - base, LANES), LANES)
            for k in range(RING):
                part = total[12 * k:12 * k + 12]
                sy[k, :, spot] = jnp.concatenate([part, jnp.zeros((4, LANES), F32)], axis=0).astype(BF)
        return store

    def store_out(i, here, there, total):
        out[:, there] = total

    def store_c(i, here, there, total):
        out_c[:, here] = total

    a1 = ring_sum(0, "x", lambda i, c: grads.at[i, :, :, c], lambda d, i, c: grads[d, i, :, c],
                  ra1, fa1, RING, FOLDED, SPLIT, store_to(sa))
    b1 = ring_sum(6, "z", lambda i, c: grads.at[:, i, :, c], lambda d, i, c: grads[i, d, :, c],
                  rb1, fb1, RING, SPLIT, cols, store_to(sb))
    c1 = ring_sum(12, "y", lambda i, c: cf.at[i, :, :, c], lambda d, i, c: cf[d, i, :, c],
                  rc1, fc1, RING * RING, 0, QUARTER, store_to(sc1))
    a1[0]()
    b1[0]()

    def fold(n, carry):
        for t in range(QUARTER // LANES):
            got = [grads[n // RING, n % RING, :, pl.ds(q * QUARTER + t * LANES, LANES)].astype(F32)
                   for q in range(RING)]
            for i in range(RING):
                parts = [g[12 * i:12 * i + 12] for g in got]
                cf[i, n, :, pl.ds(t * LANES, LANES)] = jnp.concatenate(parts, axis=0).astype(BF)
        return carry

    lax.fori_loop(0, RING * RING, fold, 0)
    c1[0]()
    for step in (1, 2):
        a1[step]()
        b1[step]()
        if step == 2:
            a2 = ring_sum(18, "z", lambda i, c: sa.at[i, :, pl.ds(c.start - FOLDED, c.size)],
                          lambda d, i, c: sa[d, :, pl.ds(pl.multiple_of(c.start - FOLDED, LANES), LANES)],
                          ra2, fa2, 0, FOLDED, SPLIT, store_parts_at(FOLDED))
            b2 = ring_sum(24, "x", lambda i, c: sb.at[i, :, pl.ds(c.start - SPLIT, c.size)],
                          lambda d, i, c: sb[d, :, pl.ds(pl.multiple_of(c.start - SPLIT, LANES), LANES)],
                          rb2, fb2, 0, SPLIT, cols, store_parts_at(FOLDED))
            a2[0]()
            b2[0]()
        c1[step]()
    c2 = ring_sum(30, "x", lambda i, c: sc1.at[pl.ds(i * RING, RING), :, c],
                  lambda d, i, c: sc1[d * RING + i, :, c],
                  rc2, fc2, RING, 0, QUARTER, store_to(sc2))
    c2[0]()
    for step in (1, 2):
        a2[step]()
        b2[step]()
        c2[step]()
    c3 = ring_sum(36, "z", lambda i, c: sc2.at[i, :, c], lambda d, i, c: sc2[d, :, c],
                  rc3, fc3, 0, 0, QUARTER, store_c)
    last = ring_sum(42, "y", lambda i, c: sy.at[i, :, c], lambda d, i, c: sy[d, :, c],
                    ry, fy, 0, 0, cols - FOLDED, store_out)
    for step in range(3):
        last[step]()
        c3[step]()


def scatter_rows(grads):
    cols = grads.shape[1]
    wa, wb, wy = SPLIT - FOLDED, cols - SPLIT, cols - FOLDED
    vm = lambda *shape: pltpu.VMEM(shape, BF)
    return pl.pallas_call(
        functools.partial(scatter_kernel, cols),
        out_shape=(jax.ShapeDtypeStruct((16, wy), F32), jax.ShapeDtypeStruct((48, QUARTER), F32)),
        in_specs=[pl.BlockSpec(memory_space=pltpu.VMEM)],
        out_specs=(pl.BlockSpec(memory_space=pltpu.VMEM),) * 2,
        scratch_shapes=[
            vm(RING, 48, wa), vm(RING, 48, wb), vm(2, RING, 48, wa), vm(2, RING, 48, wb),
            vm(RING, 48, wa), vm(RING, 48, wb),
            vm(48, wa), vm(48, wb), vm(2, 48, wa), vm(2, 48, wb),
            vm(RING, 16, wy), vm(16, wy), vm(2, 16, wy),
            vm(RING, RING * RING, 48, QUARTER), vm(RING * RING, 48, QUARTER), vm(2, RING * RING, 48, QUARTER),
            vm(RING * RING, 48, QUARTER), vm(RING, 48, QUARTER), vm(2, RING, 48, QUARTER),
            vm(RING, 48, QUARTER), vm(48, QUARTER), vm(2, 48, QUARTER),
            pltpu.SemaphoreType.DMA((48,)),
            pltpu.SemaphoreType.DMA((48,)),
        ],
        compiler_params=pltpu.CompilerParams(
            collective_id=1, has_side_effects=True, vmem_limit_bytes=56 << 20),
    )(grads.reshape(RING, RING, 48, cols))


ROWS = 256
WIDTH = 768
HALF = 384
HEADS = 6
COLS = 7808
CHUNKS = 6
SLOTS = 768
CAPACITY = 12
EXPERTS = 64
BUCKETS = 32
VMEM_BYTES = 56 << 20


def matmul(a, b):
    return jnp.dot(a, b, preferred_element_type=F32)


def matmul_nt(a, b):
    return lax.dot_general(a, b, (((1,), (1,)), ((), ())), preferred_element_type=F32)


def matmul_tn(a, b):
    return lax.dot_general(a, b, (((0,), (0,)), ((), ())), preferred_element_type=F32)


def norm_factor(v):
    return lax.rsqrt(jnp.mean(v * v, axis=-1, keepdims=True) + EPSILON)


def norm_back(v, gain, du):
    r = norm_factor(v)
    inner = jnp.sum(du * gain * v, axis=-1, keepdims=True) / WIDTH
    dgain = jnp.sum(du * v * r, axis=0, keepdims=True)
    return r * gain * du - v * (r * r * r) * inner, dgain


def greet_pair():
    barrier = pltpu.get_barrier_semaphore()
    peer = {"tensor": 1 - lax.axis_index("tensor")}
    pl.semaphore_signal(barrier, inc=1, device_id=peer, device_id_type=MESH)


def to_pair(src, dst, sems):
    return pltpu.make_async_remote_copy(
        src_ref=src, dst_ref=dst, send_sem=sems.at[0], recv_sem=sems.at[1],
        device_id={"tensor": 1 - lax.axis_index("tensor")}, device_id_type=MESH)


def pair_total(value, mine, theirs, sems):
    mine[...] = value.astype(BF)
    pl.semaphore_wait(pltpu.get_barrier_semaphore(), 1)
    move = to_pair(mine, theirs, sems)
    move.start()
    move.wait()
    return mine[...].astype(F32) + theirs[...].astype(F32)


def pair_scratch():
    return [pltpu.VMEM((ROWS, WIDTH), BF), pltpu.VMEM((ROWS, WIDTH), BF), pltpu.SemaphoreType.DMA((2,))]


def joint(number):
    return pltpu.CompilerParams(
        collective_id=number, has_side_effects=True, vmem_limit_bytes=VMEM_BYTES)


def gelu_parts(g):
    t = jnp.tanh(GELU_COEF * (g + 0.044715 * g * g * g))
    value = 0.5 * g * (1.0 + t)
    slope = 0.5 * (1.0 + t) + 0.5 * g * (1.0 - t * t) * GELU_COEF * (1.0 + 3 * 0.044715 * g * g)
    return value, slope


def swap_kernel(pick, mine, theirs, send, recv):
    t = lax.axis_index("tensor")
    peer = {"tensor": 1 - t}
    barrier = pltpu.get_barrier_semaphore()
    pl.semaphore_signal(barrier, inc=1, device_id=peer, device_id_type=MESH)
    pl.semaphore_wait(barrier, 1)
    move = pltpu.make_async_remote_copy(
        src_ref=mine.at[1 - t] if pick else mine, dst_ref=theirs, send_sem=send, recv_sem=recv,
        device_id=peer, device_id_type=MESH)
    move.start()
    move.wait()


def swap(mine, number, pick=False):
    shape = mine.shape[1:] if pick else mine.shape
    return pl.pallas_call(
        functools.partial(swap_kernel, pick),
        out_shape=jax.ShapeDtypeStruct(shape, mine.dtype),
        in_specs=[pl.BlockSpec(memory_space=pltpu.VMEM)],
        out_specs=pl.BlockSpec(memory_space=pltpu.VMEM),
        scratch_shapes=[pltpu.SemaphoreType.DMA, pltpu.SemaphoreType.DMA],
        compiler_params=pltpu.CompilerParams(collective_id=number, has_side_effects=True),
    )(mine)


def vm():
    return pl.BlockSpec(memory_space=pltpu.VMEM)


def full(shape):
    return pl.BlockSpec(shape, lambda *_: (0,) * len(shape))


def shaped(shape, dtype):
    return jax.ShapeDtypeStruct(shape, dtype)


def params():
    return pltpu.CompilerParams(vmem_limit_bytes=VMEM_BYTES)


def attend_kernel(layer, base, weights, sides, lookup, seg_col, seg_row, next_out, na, qkv, probs,
                  mixed, mine, theirs, sems):
    greet_pair()
    x = base[...].astype(F32)
    gain = sides[64 + 2 * layer:65 + 2 * layer, :].astype(F32)
    normed = (x * norm_factor(x) * gain).astype(BF)
    na[...] = normed
    qkv[...] = matmul(normed, weights[:, :1152]).astype(BF)
    offsets = matmul_nt(sides[...], lookup[...])
    row = lax.broadcasted_iota(jnp.int32, (ROWS, ROWS), 0)
    col = lax.broadcasted_iota(jnp.int32, (ROWS, ROWS), 1)
    allowed = (seg_col[...] == seg_row[...]) & (col <= row)
    outs = []
    for h in range(HEADS):
        at = h * HEAD_DIM
        q = qkv[:, at:at + HEAD_DIM]
        k = qkv[:, HALF + at:HALF + at + HEAD_DIM]
        v = qkv[:, 2 * HALF + at:2 * HALF + at + HEAD_DIM]
        rel = pltpu.roll(jnp.broadcast_to(offsets[68 + h:69 + h, :], (ROWS, ROWS)), 0, 1,
                         stride=1, stride_axis=0)
        s = jnp.where(allowed, matmul_nt(q, k) * HEAD_DIM ** (-0.5) + rel, NEG_FILL)
        e = jnp.exp(s - jnp.max(s, axis=-1, keepdims=True))
        p = (e / jnp.sum(e, axis=-1, keepdims=True)).astype(BF)
        probs[h] = p
        outs.append(matmul(p, v))
    o = jnp.concatenate(outs, axis=1).astype(BF)
    mixed[...] = o
    next_out[...] = x + pair_total(matmul_nt(o, weights[:, 1152:]), mine, theirs, sems)


def attend(layer, base, whole, sides, lookup, seg_col, seg_row):
    return pl.pallas_call(
        functools.partial(attend_kernel, layer),
        grid=(1,),
        out_shape=(
            shaped((ROWS, WIDTH), F32), shaped((ROWS, WIDTH), BF), shaped((ROWS, 1152), BF),
            shaped((HEADS, ROWS, ROWS), BF), shaped((ROWS, HALF), BF)),
        in_specs=[
            full((ROWS, WIDTH)), pl.BlockSpec((WIDTH, 1536), lambda i: (0, 3 + layer)),
            full((128, WIDTH)), full((ROWS, WIDTH)), full((ROWS, 1)), full((1, ROWS))],
        out_specs=(
            full((ROWS, WIDTH)), full((ROWS, WIDTH)), full((ROWS, 1152)),
            full((HEADS, ROWS, ROWS)), full((ROWS, HALF))),
        scratch_shapes=pair_scratch(),
        compiler_params=joint(2 + layer),
    )(base, whole, sides, lookup, seg_col, seg_row)


def dense_kernel(base, weights, sides, next_out, normed_out, gate_up, hidden, acc, mine, theirs, sems):
    c = pl.program_id(0)

    @pl.when(c == 0)
    def _():
        greet_pair()
        x = base[...]
        normed_out[...] = (x * norm_factor(x) * sides[65:66, :].astype(F32)).astype(BF)
        acc[...] = jnp.zeros_like(acc)

    gu = matmul(normed_out[...], weights[:, :512])
    gate_up[...] = gu.astype(BF)
    g, u = gu[:, :256], gu[:, 256:]
    t = jnp.tanh(GELU_COEF * (g + 0.044715 * g * g * g))
    hid = (0.5 * g * (1.0 + t) * u).astype(BF)
    hidden[...] = hid
    acc[...] += matmul_nt(hid, weights[:, 512:])

    @pl.when(c == CHUNKS - 1)
    def _():
        next_out[...] = base[...] + pair_total(acc[...], mine, theirs, sems)


def dense(base, whole, sides):
    return pl.pallas_call(
        dense_kernel,
        grid=(CHUNKS,),
        out_shape=(
            shaped((ROWS, WIDTH), F32), shaped((ROWS, WIDTH), BF), shaped((ROWS, 3072), BF),
            shaped((ROWS, 1536), BF)),
        in_specs=[
            full((ROWS, WIDTH)), pl.BlockSpec((WIDTH, WIDTH), lambda c: (0, c)), full((128, WIDTH))],
        out_specs=(
            full((ROWS, WIDTH)), full((ROWS, WIDTH)),
            pl.BlockSpec((ROWS, 512), lambda c: (0, c)), pl.BlockSpec((ROWS, 256), lambda c: (0, c))),
        scratch_shapes=[pltpu.VMEM((ROWS, WIDTH), F32), *pair_scratch()],
        compiler_params=joint(4),
    )(base, whole, sides)


def route_kernel(base, sides, ids_col, ids_row, cot, normed_out, first, second,
                 weights_out, packed):
    t = lax.axis_index("tensor")
    x = base[...]
    normed = (x * norm_factor(x) * sides[67:68, :].astype(F32)).astype(BF)
    normed_out[...] = normed
    logits = matmul_nt(normed, sides[:64, :])
    experts_col = lax.broadcasted_iota(jnp.int32, (ROWS, EXPERTS), 1)
    one, two = ids_col[:, 0:1] == experts_col, ids_col[:, 1:2] == experts_col
    pick = lambda mask, v: jnp.sum(jnp.where(mask, v, 0.0), axis=1, keepdims=True)
    margin = pick(one, logits) - pick(two, logits)
    w1 = 1.0 / (1.0 + jnp.exp(-margin))
    w2 = 1.0 / (1.0 + jnp.exp(margin))
    weights_out[...] = jnp.concatenate([w1, w2], axis=1)
    row = lax.broadcasted_iota(jnp.int32, (ROWS, ROWS), 0)
    col = lax.broadcasted_iota(jnp.int32, (ROWS, ROWS), 1)
    as_low = lambda mask: jnp.where(mask, 1.0, 0.0).astype(BF)
    counts = matmul(as_low(col < row), as_low(one | two))
    slots_col = lax.broadcasted_iota(jnp.int32, (ROWS, SLOTS), 1)
    for k, (mask, out) in enumerate(((one, first), (two, second))):
        target = ids_col[:, k:k + 1] * CAPACITY + pick(mask, counts).astype(jnp.int32)
        out[...] = as_low(target == slots_col)
    experts_row = lax.broadcasted_iota(jnp.int32, (EXPERTS, ROWS), 0)
    one, two = ids_row[0:1, :] == experts_row, ids_row[1:2, :] == experts_row
    counts = matmul(as_low(one | two), as_low(row < col))
    slots_row = lax.broadcasted_iota(jnp.int32, (SLOTS, ROWS), 0)
    half = pl.ds(pl.multiple_of(t * HALF, HALF), HALF)
    g4 = cot[:, half].astype(F32)
    take, back = None, 0.0
    for k, (mask, w) in enumerate(((one, w1), (two, w2))):
        seen = jnp.sum(jnp.where(mask, counts, 0.0), axis=0, keepdims=True).astype(jnp.int32)
        target = ids_row[k:k + 1, :] * CAPACITY + seen
        here = target == slots_row
        take = here if take is None else take | here
        back = back + matmul(as_low(here), (w * g4).astype(BF))
    packed[:, :HALF] = matmul(as_low(take), normed_out[:, half]).astype(BF)
    packed[:, HALF:] = back.astype(BF)


def route(*operands):
    return pl.pallas_call(
        route_kernel,
        out_shape=(
            shaped((ROWS, WIDTH), BF), shaped((ROWS, SLOTS), BF),
            shaped((ROWS, SLOTS), BF), shaped((ROWS, 2), F32), shaped((SLOTS, WIDTH), BF)),
        in_specs=[vm()] * 5,
        out_specs=(vm(),) * 5,
        compiler_params=params(),
    )(*operands)


def expert_kernel(own, recv, wide_gate, wide_up, narrow, wide_grad, narrow_grad, back, xin, dy, x_turned, y_acc, dx_acc):
    c = pl.program_id(0)
    t = lax.axis_index("tensor")

    @pl.when(c == 0)
    def _():
        low = jnp.where(t == 0, own[...], recv[...])
        high = jnp.where(t == 0, recv[...], own[...])
        xin[:, :HALF] = low[:, :HALF]
        xin[:, HALF:] = high[:, :HALF]
        dy[:, :HALF] = low[:, HALF:]
        dy[:, HALF:] = high[:, HALF:]
        x_turned[...] = xin[...].T
        y_acc[...] = jnp.zeros_like(y_acc)
        dx_acc[...] = jnp.zeros_like(dx_acc)

    g, u = matmul(xin[...], wide_gate[...]), matmul(xin[...], wide_up[...])
    value, slope = gelu_parts(g)
    hid = (value * u).astype(BF)
    y_acc[...] += matmul(hid, narrow[...])
    narrow_grad[...] = matmul_tn(hid, dy[...])
    dh = matmul_nt(dy[...], narrow[...])
    dg, du = (dh * u * slope).astype(BF), (dh * value).astype(BF)
    dx_acc[...] += matmul_nt(dg, wide_gate[...]) + matmul_nt(du, wide_up[...])
    wide_grad[:, 0, :] = matmul(x_turned[...], dg)
    wide_grad[:, 1, :] = matmul(x_turned[...], du)

    @pl.when(c == CHUNKS - 1)
    def _():
        for h in range(2):
            back[h, :, :HALF] = y_acc[:, h * HALF:(h + 1) * HALF].astype(BF)
            back[h, :, HALF:] = dx_acc[:, h * HALF:(h + 1) * HALF].astype(BF)


def expert(own, recv, wide, narrow):
    return pl.pallas_call(
        expert_kernel,
        grid=(CHUNKS,),
        out_shape=(
            shaped((WIDTH, 2, 1536), F32), shaped((1536, WIDTH), F32), shaped((2, SLOTS, WIDTH), BF)),
        in_specs=[full((SLOTS, WIDTH)), full((SLOTS, WIDTH)),
                  pl.BlockSpec((WIDTH, 256), lambda c: (0, c)),
                  pl.BlockSpec((WIDTH, 256), lambda c: (0, CHUNKS + c)),
                  pl.BlockSpec((256, WIDTH), lambda c: (c, 0))],
        out_specs=(pl.BlockSpec((WIDTH, 2, 256), lambda c: (0, 0, c)), pl.BlockSpec((256, WIDTH), lambda c: (c, 0)),
                   full((2, SLOTS, WIDTH))),
        scratch_shapes=[pltpu.VMEM((SLOTS, WIDTH), BF), pltpu.VMEM((SLOTS, WIDTH), BF),
                        pltpu.VMEM((WIDTH, SLOTS), BF), pltpu.VMEM((SLOTS, WIDTH), F32),
                        pltpu.VMEM((SLOTS, WIDTH), F32)],
        compiler_params=params(),
    )(own, recv, wide, wide, narrow)


def combine_kernel(own, first, second, weights, x, normed, cot, ids_col, sides,
                   out, g3, dgain, router_back, recv, sems):
    t = lax.axis_index("tensor")
    greet_pair()
    pl.semaphore_wait(pltpu.get_barrier_semaphore(), 1)
    move = to_pair(own, recv, sems)
    move.start()
    move.wait()
    low = jnp.where(t == 0, own[...], recv[...])
    high = jnp.where(t == 0, recv[...], own[...])
    y = jnp.concatenate([low[:, :HALF], high[:, :HALF]], axis=1)
    dx = jnp.concatenate([low[:, HALF:], high[:, HALF:]], axis=1)
    g4 = cot[...].astype(F32)
    y1, y2 = matmul(first[...], y), matmul(second[...], y)
    w1, w2 = weights[:, 0:1], weights[:, 1:2]
    v = x[...]
    out[...] = v + (w1 * y1 + w2 * y2)
    dot = lambda a: jnp.sum(a * g4, axis=1, keepdims=True)
    dm = w1 * w2 * (dot(y1) - dot(y2))
    experts = lax.broadcasted_iota(jnp.int32, (ROWS, EXPERTS), 1)
    signs = (jnp.where(ids_col[:, 0:1] == experts, 1.0, 0.0)
             - jnp.where(ids_col[:, 1:2] == experts, 1.0, 0.0))
    dlogits = (dm * signs).astype(BF)
    router_back[...] = matmul_tn(dlogits, normed[...])
    dn = matmul(dlogits, sides[:64, :]) + matmul(first[...] + second[...], dx)
    dv, dg = norm_back(v, sides[67:68, :].astype(F32), dn)
    g3[...] = g4 + dv
    dgain[...] = dg


def combine(*operands):
    return pl.pallas_call(
        combine_kernel,
        out_shape=(shaped((ROWS, WIDTH), F32), shaped((ROWS, WIDTH), F32), shaped((1, WIDTH), F32),
                   shaped((EXPERTS, WIDTH), F32)),
        in_specs=[vm()] * len(operands),
        out_specs=(vm(),) * 4,
        scratch_shapes=[pltpu.VMEM((SLOTS, WIDTH), BF), pltpu.SemaphoreType.DMA((2,))],
        compiler_params=joint(5),
    )(*operands)


def attend_back_kernel(layer, grad, x, held, weights, sides, lookup, na, qkv, probs, mixed,
                       held_out, bias_back, g_out, dgain, mine, theirs, sems):
    greet_pair()
    g = grad[...]
    db = g.astype(BF)
    held_out[:, 1152:] = matmul_tn(db, mixed[...]).astype(BF)
    back = matmul(db, weights[:, 1152:]).astype(BF)
    row = lax.broadcasted_iota(jnp.int32, (ROWS, ROWS), 0)
    col = lax.broadcasted_iota(jnp.int32, (ROWS, ROWS), 1)
    reverse = jnp.where(row + col == ROWS - 1, 1.0, 0.0).astype(BF)
    dq, dk, dv, sums = [], [], [], []
    for h in range(HEADS):
        at = h * HEAD_DIM
        q = qkv[:, at:at + HEAD_DIM]
        k = qkv[:, HALF + at:HALF + at + HEAD_DIM]
        v = qkv[:, 2 * HALF + at:2 * HALF + at + HEAD_DIM]
        d = back[:, at:at + HEAD_DIM]
        low = probs[h]
        p = low.astype(F32)
        dp = matmul_nt(d, v)
        ds = (p * (dp - jnp.sum(p * dp, axis=-1, keepdims=True))).astype(BF)
        turned = pltpu.roll(matmul(reverse, ds), 1, 1, stride=1, stride_axis=0)
        sums.append(jnp.sum(turned, axis=0, keepdims=True))
        dq.append(matmul(ds, k) * HEAD_DIM ** (-0.5))
        dk.append(matmul_tn(ds, q) * HEAD_DIM ** (-0.5))
        dv.append(matmul_tn(low, d))
    sums = jnp.concatenate(sums + [jnp.zeros((2, ROWS), F32)], axis=0)
    high = sums.astype(BF)
    rest = (sums - high.astype(F32)).astype(BF)
    bias_back[...] = matmul(high, lookup[...]) + matmul(rest, lookup[...])
    dqkv = jnp.concatenate(dq + dk + dv, axis=1).astype(BF)
    held_out[:, :1152] = matmul_tn(na[...], dqkv).astype(BF)
    total = pair_total(matmul_nt(dqkv, weights[:, :1152]), mine, theirs, sems)
    back, dg = norm_back(x[...].astype(F32), sides[64 + 2 * layer:65 + 2 * layer, :].astype(F32), total)
    g_out[...] = g + back
    dgain[...] = dg


def attend_back(layer, grad, x, held, whole, sides, lookup, na, qkv, probs, mixed):
    block = pl.BlockSpec((WIDTH, 1536), lambda i: (0, 3 + layer))
    rows = full((ROWS, WIDTH))
    return pl.pallas_call(
        functools.partial(attend_back_kernel, layer),
        grid=(1,),
        out_shape=(shaped((WIDTH, COLS), BF), shaped((8, WIDTH), F32), shaped((ROWS, WIDTH), F32),
                   shaped((1, WIDTH), F32)),
        in_specs=[rows, rows, pl.BlockSpec(memory_space=pl.ANY), block, full((128, WIDTH)), rows, rows,
                  full((ROWS, 1152)), full((HEADS, ROWS, ROWS)), full((ROWS, HALF))],
        out_specs=(block, full((8, WIDTH)), rows, full((1, WIDTH))),
        scratch_shapes=pair_scratch(),
        input_output_aliases={2: 0},
        compiler_params=joint(6 + layer),
    )(grad, x, held, whole, sides, lookup, na, qkv, probs, mixed)


def dense_back_kernel(grad, x, held, weights, sides, normed, gate_up, hidden,
                      held_out, g_out, dgain, low, low_turned, normed_turned, acc, mine, theirs, sems):
    c = pl.program_id(0)

    @pl.when(c == 0)
    def _():
        greet_pair()
        low[...] = grad[...].astype(BF)
        low_turned[...] = low[...].T
        normed_turned[...] = normed[...].T
        acc[...] = jnp.zeros_like(acc)

    held_out[:, 512:] = matmul(low_turned[...], hidden[...]).astype(BF)
    dh = matmul(low[...], weights[:, 512:])
    gu = gate_up[...].astype(F32)
    g, u = gu[:, :256], gu[:, 256:]
    value, slope = gelu_parts(g)
    dgu = jnp.concatenate([(dh * u * slope).astype(BF), (dh * value).astype(BF)], axis=1)
    held_out[:, :512] = matmul(normed_turned[...], dgu).astype(BF)
    acc[...] += matmul_nt(dgu, weights[:, :512])

    @pl.when(c == CHUNKS - 1)
    def _():
        total = pair_total(acc[...], mine, theirs, sems)
        dv, dg = norm_back(x[...], sides[65:66, :].astype(F32), total)
        g_out[...] = grad[...] + dv
        dgain[...] = dg


def dense_back(grad, x, held, whole, sides, normed, gate_up, hidden):
    rows = full((ROWS, WIDTH))
    block = pl.BlockSpec((WIDTH, WIDTH), lambda c: (0, c))
    return pl.pallas_call(
        dense_back_kernel,
        grid=(CHUNKS,),
        out_shape=(shaped((WIDTH, COLS), BF), shaped((ROWS, WIDTH), F32), shaped((1, WIDTH), F32)),
        in_specs=[rows, rows, pl.BlockSpec(memory_space=pl.ANY), block,
                  full((128, WIDTH)), rows, pl.BlockSpec((ROWS, 512), lambda c: (0, c)),
                  pl.BlockSpec((ROWS, 256), lambda c: (0, c))],
        out_specs=(block, rows, full((1, WIDTH))),
        scratch_shapes=[pltpu.VMEM((ROWS, WIDTH), BF), pltpu.VMEM((WIDTH, ROWS), BF),
                        pltpu.VMEM((WIDTH, ROWS), BF), pltpu.VMEM((ROWS, WIDTH), F32), *pair_scratch()],
        input_output_aliases={2: 0},
        compiler_params=joint(8),
    )(grad, x, held, whole, sides, normed, gate_up, hidden)


def finish_kernel(held, g, router_back, gain0, gain1, gain2, gain3, bias1, bias2, held_out, g_out, turned):
    g_out[...] = g[...]
    turned[:64, :] = router_back[...]
    turned[64:68, :] = jnp.concatenate([gain0[...], gain1[...], gain2[...], gain3[...]], axis=0)
    turned[68:76, :] = bias1[...] + bias2[...]
    turned[76:, :] = jnp.zeros((52, WIDTH), F32)
    held_out[...] = turned[...].T.astype(BF)


def finish(held, *rest):
    return pl.pallas_call(
        finish_kernel,
        grid=(1,),
        out_shape=(shaped((WIDTH, COLS), BF), shaped((ROWS, WIDTH), F32)),
        in_specs=[pl.BlockSpec(memory_space=pl.ANY)] + [full(r.shape) for r in rest],
        out_specs=(pl.BlockSpec((WIDTH, 128), lambda i: (0, 60)), full((ROWS, WIDTH))),
        scratch_shapes=[pltpu.VMEM((128, WIDTH), F32)],
        input_output_aliases={0: 0},
        compiler_params=params(),
    )(held, *rest)


def blank_kernel(out):
    pass


def blank():
    return pl.pallas_call(
        blank_kernel,
        out_shape=shaped((WIDTH, COLS), BF),
        out_specs=pl.BlockSpec(memory_space=pl.ANY),
    )()


def bucket_lookup(layer):
    distance = (-np.arange(ROWS)) % ROWS
    exact = BUCKETS // 2
    levels = np.arange(1, BUCKETS - exact)
    bounds = exact * REACH_RATIO ** (levels / exact)
    far = exact + np.sum(distance[:, None] >= bounds[None, :], axis=1)
    bucket = np.where(distance < exact, distance, far)
    place = (layer * BUCKETS + bucket) * 12
    return jnp.asarray(place[:, None] == np.arange(WIDTH)[None, :], BF)


def across(packed):
    moved = lax.all_to_all(packed.reshape(EXPERTS, CAPACITY, WIDTH), "expert", 0, 0, tiled=True)
    return moved.reshape(SLOTS, WIDTH)


def chunked(a):
    return a.reshape(a.shape[0], 2, CHUNKS, 256).transpose(0, 2, 1, 3)


def local(tokens, cotangent, segment_ids, expert_ids, attention, combiner, expander, reducer,
          router, widener, narrower, norm_gains, rel_bias):
    feed = jnp.concatenate([chunked(expander), reducer.T.reshape(12, CHUNKS, 1, 256)], axis=2)
    small = jnp.concatenate(
        [router, norm_gains.T, jnp.pad(rel_bias, ((0, 11), (0, 0))), jnp.zeros((12, 54), BF)], axis=1)
    own = jnp.concatenate(
        [feed.reshape(12, -1), attention[0].reshape(12, -1), combiner[0].T,
         attention[1].reshape(12, -1), combiner[1].T, small], axis=1)
    whole = gather_rows(jnp.pad(own, ((0, 4), (0, 0))))
    sides = whole[:, 7680:].T
    seg_col, seg_row = segment_ids[:, None], segment_ids[None, :]
    ids_row = expert_ids.T
    look1, look2 = bucket_lookup(0), bucket_lookup(1)
    wide = widener[0].reshape(WIDTH, -1)

    x1, na1, qkv1, probs1, mixed1 = attend(0, tokens, whole, sides, look1, seg_col, seg_row)
    x2, n2, gate_up, hidden = dense(x1, whole, sides)
    x3, na2, qkv2, probs2, mixed2 = attend(1, x2, whole, sides, look2, seg_col, seg_row)
    n4, first, second, weights, packed = route(x3, sides, expert_ids, ids_row, cotangent)
    arrived = across(packed)
    wide_grad, narrow_grad, back = expert(arrived, swap(arrived, 9), wide, narrower[0])
    t = lax.axis_index("tensor")
    mine = lax.dynamic_index_in_dim(back, t, 0, keepdims=False).astype(F32)
    total = (mine + swap(back, 10, pick=True).astype(F32)).astype(BF)
    layer_out, g3, gain3, router_back = combine(
        across(total), first, second, weights, x3, n4, cotangent, expert_ids, sides)
    held, bias2, g2, gain2 = attend_back(
        1, g3, x2, blank(), whole, sides, look2, na2, qkv2, probs2, mixed2)
    held, g1, gain1 = dense_back(g2, x1, held, whole, sides, n2, gate_up, hidden)
    held, bias1, g0, gain0 = attend_back(
        0, g1, tokens, held, whole, sides, look1, na1, qkv1, probs1, mixed1)
    held, g0 = finish(held, g0, router_back, gain0, gain1, gain2, gain3, bias1, bias2)
    summed, folded = scatter_rows(held)
    folded = folded.reshape(RING, 12, QUARTER).transpose(1, 0, 2).reshape(12, FOLDED)
    summed = jnp.concatenate([folded, summed[:12]], axis=1)
    feed = summed[:, :4608].reshape(12, CHUNKS, 3, 256)
    return (
        layer_out,
        g0,
        jnp.stack([summed[:, 4608:5760], summed[:, 6144:7296]]).reshape(2, 12, 3, HALF),
        jnp.stack([summed[:, 5760:6144].T, summed[:, 7296:7680].T]),
        feed[:, :, :2].transpose(0, 2, 1, 3).reshape(12, 2, 1536),
        feed[:, :, 2].reshape(12, 1536).T,
        summed[:, 7680:7744],
        wide_grad[None],
        narrow_grad[None],
        summed[:, 7744:7748].T,
        summed[:1, 7748:7754],
    )


def solution(mesh):
    in_specs = (
        P("expert", None),
        P("expert", None),
        P("expert"),
        P("expert", None),
        P(None, "expert", None, "tensor"),
        P(None, "tensor", "expert"),
        P("expert", None, "tensor"),
        P("tensor", "expert"),
        P("expert", None),
        P("expert", None, None, "tensor"),
        P("expert", "tensor", None),
        P(None, "expert"),
        P("expert", "tensor"),
    )
    out_specs = (
        P("expert", None),
        P("expert", None),
        P(None, "expert", None, "tensor"),
        P(None, "tensor", "expert"),
        P("expert", None, "tensor"),
        P("tensor", "expert"),
        P("expert", None),
        P("expert", None, None, "tensor"),
        P("expert", "tensor", None),
        P(None, "expert"),
        P("expert", "tensor"),
    )
    return jax.shard_map(local, mesh=mesh, in_specs=in_specs, out_specs=out_specs, check_vma=False)
```

```python
import functools

import jax
import jax.numpy as jnp
import numpy as np
from jax import lax
from jax.experimental import pallas as pl
from jax.experimental.pallas import tpu as pltpu
from jax.sharding import PartitionSpec as P

HEAD_DIM = 64
EPSILON = 1e-06
NEG_FILL = -1000000000.0
REACH_RATIO = 8.0
GELU_COEF = 0.7978845608028654

MESH = pl.DeviceIdType.MESH
RING = 4
LANES = 128
BF = jnp.bfloat16
F32 = jnp.float32


def places():
    e = lax.axis_index("expert")
    return e // 16, (e // 4) % 4, e % 4


def neighbours():
    x, z, y = places()
    up, down = lambda v: (v + 1) % RING, lambda v: (v + 3) % RING
    at = lambda a, b, c: a * 16 + b * 4 + c
    return {
        "x": (at(up(x), z, y), at(down(x), z, y)),
        "z": (at(x, up(z), y), at(x, down(z), y)),
        "y": (at(x, z, up(y)), at(x, z, down(y))),
    }


def greet(near):
    barrier = pltpu.get_barrier_semaphore()
    for axis in "xzy":
        for peer in near[axis]:
            pl.semaphore_signal(barrier, inc=1, device_id={"expert": peer}, device_id_type=MESH)
    pl.semaphore_wait(barrier, 6)


FOLDED = 2560
QUARTER = FOLDED // RING
SPLIT = 5120


def tile_at(t, base=0):
    return pl.ds(pl.multiple_of(base + t * LANES, LANES), LANES)


def gather_kernel(cols, own, out, ring, block, folded, whole_c, stage, sends, recvs, locals_):
    near = neighbours()
    x, z, y = places()
    greet(near)

    def copy(k, src, dst, peer):
        return pltpu.make_async_remote_copy(
            src_ref=src, dst_ref=dst, send_sem=sends.at[k], recv_sem=recvs.at[k],
            device_id={"expert": peer}, device_id_type=MESH)

    def both_ways(k, axis, src, at, lo, hi):
        m = {"x": x, "z": z, "y": y}[axis]
        up, down = near[axis]
        prev, nxt = (m + 3) % RING, (m + 1) % RING
        mid = (lo + hi) // 2 // LANES * LANES
        left, right, full = pl.ds(lo, mid - lo), pl.ds(mid, hi - mid), pl.ds(lo, hi - lo)
        first = copy(k, src, at(m, full), up)
        second = copy(k + 1, src, at(m, full), down)
        third = copy(k + 2, at(prev, left), at(prev, left), up)
        fourth = copy(k + 3, at(nxt, right), at(nxt, right), down)

        def start():
            first.start()
            second.start()

        def relay():
            first.wait_recv()
            third.start()
            second.wait_recv()
            fourth.start()

        def finish():
            third.wait_recv()
            fourth.wait_recv()
            for c in (first, second, third, fourth):
                c.wait_send()

        return start, relay, finish

    def run(*streams):
        for step in range(3):
            for stream in streams:
                stream[step]()

    ab_y = both_ways(0, "y", own.at[:, pl.ds(FOLDED, cols - FOLDED)],
                     lambda i, c: ring.at[i, :, c], 0, cols - FOLDED)
    ab_y[0]()
    for t in range(QUARTER // LANES):
        parts = [own[:, pl.ds(q * QUARTER + t * LANES, LANES)].astype(F32)[:12] for q in range(RING)]
        folded[:, pl.ds(t * LANES, LANES)] = jnp.concatenate(parts, axis=0).astype(BF)
    c_z = both_ways(4, "z", folded, lambda i, c: whole_c.at[x, i, y, :, c], 0, QUARTER)
    c_z[0]()
    whole_c[x, z, y] = folded[...]
    ring[y] = own[:, FOLDED:]
    ab_y[1]()
    c_z[1]()
    ab_y[2]()

    def assemble(t, carry):
        parts = [ring[i, :, tile_at(t)].astype(F32)[:12] for i in range(RING)]
        block[:, tile_at(t)] = jnp.concatenate(parts, axis=0).astype(BF)
        return carry

    lax.fori_loop(0, (cols - FOLDED) // LANES, assemble, 0)
    keep = pltpu.make_async_copy(block, out.at[x, z, :, pl.ds(FOLDED, cols - FOLDED)], locals_.at[2])
    keep.start()
    a_cols, b_cols = pl.ds(FOLDED, SPLIT - FOLDED), pl.ds(SPLIT, cols - SPLIT)
    a_z = both_ways(8, "z", block.at[:, pl.ds(0, SPLIT - FOLDED)], lambda i, c: out.at[x, i, :, c], FOLDED, SPLIT)
    b_x = both_ways(12, "x", block.at[:, pl.ds(SPLIT - FOLDED, cols - SPLIT)], lambda i, c: out.at[i, z, :, c],
                    SPLIT, cols)
    a_z[0]()
    b_x[0]()
    c_z[2]()
    c_x = both_ways(16, "x", whole_c.at[x, :, y], lambda i, c: whole_c.at[i, :, y, :, c], 0, QUARTER)
    c_x[0]()
    a_z[1]()
    b_x[1]()
    c_x[1]()
    keep.wait()
    a_z[2]()
    a_x = both_ways(20, "x", out.at[x, :, :, a_cols], lambda i, c: out.at[i, :, :, c], FOLDED, SPLIT)
    a_x[0]()
    b_x[2]()
    b_z = both_ways(24, "z", out.at[:, z, :, b_cols], lambda i, c: out.at[:, i, :, c], SPLIT, cols)
    b_z[0]()
    c_x[2]()
    c_y = both_ways(28, "y", whole_c.at[:, :, y], lambda i, c: whole_c.at[:, :, i, :, c], 0, QUARTER)
    c_y[0]()
    a_x[1]()
    b_z[1]()
    c_y[1]()
    c_y[2]()

    def unfold(n, slot):
        def one(t, carry):
            got = [whole_c[n // RING, n % RING, i, :, tile_at(t)].astype(F32) for i in range(RING)]
            for q in range(RING):
                parts = [g[12 * q:12 * q + 12] for g in got]
                stage[slot, :, tile_at(t, q * QUARTER)] = jnp.concatenate(parts, axis=0).astype(BF)
            return carry
        lax.fori_loop(0, QUARTER // LANES, one, 0)

    def write(n, slot):
        return pltpu.make_async_copy(
            stage.at[slot], out.at[n // RING, n % RING, :, pl.ds(0, FOLDED)], locals_.at[slot])

    def pair(j, carry):
        for slot in range(2):
            n = 2 * j + slot

            @pl.when(j > 0)
            def _():
                write(n, slot).wait()

            unfold(n, slot)
            write(n, slot).start()
        return carry

    lax.fori_loop(0, RING * RING // 2, pair, 0)
    for slot in range(2):
        write(slot, slot).wait()
    a_x[2]()
    b_z[2]()


def gather_rows(own):
    cols = own.shape[1]
    out = pl.pallas_call(
        functools.partial(gather_kernel, cols),
        out_shape=jax.ShapeDtypeStruct((RING, RING, 48, cols), BF),
        in_specs=[pl.BlockSpec(memory_space=pltpu.VMEM)],
        out_specs=pl.BlockSpec(memory_space=pltpu.HBM),
        scratch_shapes=[
            pltpu.VMEM((RING, 16, cols - FOLDED), BF),
            pltpu.VMEM((48, cols - FOLDED), BF),
            pltpu.VMEM((48, QUARTER), BF),
            pltpu.VMEM((RING, RING, RING, 48, QUARTER), BF),
            pltpu.VMEM((2, 48, FOLDED), BF),
            pltpu.SemaphoreType.DMA((32,)),
            pltpu.SemaphoreType.DMA((32,)),
            pltpu.SemaphoreType.DMA((3,)),
        ],
        compiler_params=pltpu.CompilerParams(
            collective_id=0, has_side_effects=True, vmem_limit_bytes=60 << 20),
    )(own)
    return out.reshape(768, cols)


def scatter_kernel(cols, held, out, out_c, grads, ra1, rb1, fa1, fb1, sa, sb, ra2, rb2, fa2, fb2,
                   sy, ry, fy, cf, rc1, fc1, sc1, rc2, fc2, sc2, rc3, fc3, sends, recvs, loads):
    near = neighbours()
    x, z, y = places()
    loading = [pltpu.make_async_copy(held.at[:, :, :, c], grads.at[:, :, :, c], loads.at[n])
               for n, c in enumerate((pl.ds(0, FOLDED), pl.ds(FOLDED, SPLIT - FOLDED), pl.ds(SPLIT, cols - SPLIT)))]
    for load_part in loading:
        load_part.start()
    greet(near)

    def copy(k, src, dst, peer):
        return pltpu.make_async_remote_copy(
            src_ref=src, dst_ref=dst, send_sem=sends.at[k], recv_sem=recvs.at[k],
            device_id={"expert": peer}, device_id_type=MESH)

    def ring_sum(k, axis, at, load, relay_buf, final_buf, lead, lo, hi, store):
        width = hi - lo
        half = width // 2 // LANES * LANES
        m = {"x": x, "z": z, "y": y}[axis]
        up, down = near[axis]
        p, q, o = (m + 1) % RING, (m + 3) % RING, (m + 2) % RING
        left, right = pl.ds(0, half), pl.ds(half, width - half)
        g_left, g_right = pl.ds(lo, half), pl.ds(lo + half, width - half)
        c = [
            copy(k, at(o, g_left), relay_buf.at[..., left], up),
            copy(k + 1, at(o, g_right), relay_buf.at[..., right], down),
            copy(k + 2, at(p, g_right), final_buf.at[0, ..., right], up),
            copy(k + 3, at(q, g_left), final_buf.at[1, ..., left], down),
            copy(k + 4, relay_buf.at[..., left], final_buf.at[0, ..., left], up),
            copy(k + 5, relay_buf.at[..., right], final_buf.at[1, ..., right], down),
        ]

        def tiles(first, count, dest):
            def body(t, carry):
                off = pl.multiple_of(first + t * LANES, LANES)
                here, there = pl.ds(off, LANES), pl.ds(pl.multiple_of(lo + off, LANES), LANES)
                for i in range(lead or 1):
                    ix = (i,) if lead else ()
                    relay_buf[(*ix, slice(None), here)] = (
                        relay_buf[(*ix, slice(None), here)].astype(F32)
                        + load(dest, i, there).astype(F32)).astype(BF)
                return carry
            lax.fori_loop(0, count, body, 0)

        def start():
            for j in range(4):
                c[j].start()

        def relay():
            c[0].wait_recv()
            tiles(0, half // LANES, p)
            c[4].start()
            c[1].wait_recv()
            tiles(half, (width - half) // LANES, q)
            c[5].start()

        def finish():
            for j in range(2, 6):
                c[j].wait_recv()

            def body(t, carry):
                here = pl.ds(pl.multiple_of(t * LANES, LANES), LANES)
                there = pl.ds(pl.multiple_of(lo + t * LANES, LANES), LANES)
                for i in range(lead or 1):
                    ix = (i,) if lead else ()
                    total = (load(m, i, there).astype(F32)
                             + final_buf[(0, *ix, slice(None), here)].astype(F32)
                             + final_buf[(1, *ix, slice(None), here)].astype(F32))
                    store(i, here, there, total)
                return carry
            lax.fori_loop(0, width // LANES, body, 0)
            for j in range(6):
                c[j].wait_send()

        return start, relay, finish

    def store_to(ref):
        def store(i, here, there, total):
            ref[i, :, here] = total.astype(BF)
        return store

    def store_parts_at(base):
        def store(i, here, there, total):
            spot = pl.ds(pl.multiple_of(there.start - base, LANES), LANES)
            for k in range(RING):
                part = total[12 * k:12 * k + 12]
                sy[k, :, spot] = jnp.concatenate([part, jnp.zeros((4, LANES), F32)], axis=0).astype(BF)
        return store

    def store_out(i, here, there, total):
        out[:, there] = total

    def store_c(i, here, there, total):
        out_c[:, here] = total

    a1 = ring_sum(0, "x", lambda i, c: held.at[i, :, :, c], lambda d, i, c: grads[d, i, :, c],
                  ra1, fa1, RING, FOLDED, SPLIT, store_to(sa))
    b1 = ring_sum(6, "z", lambda i, c: held.at[:, i, :, c], lambda d, i, c: grads[i, d, :, c],
                  rb1, fb1, RING, SPLIT, cols, store_to(sb))
    c1 = ring_sum(12, "y", lambda i, c: cf.at[i, :, :, c], lambda d, i, c: cf[d, i, :, c],
                  rc1, fc1, RING * RING, 0, QUARTER, store_to(sc1))
    a1[0]()
    b1[0]()

    def fold(n, carry):
        for t in range(QUARTER // LANES):
            got = [grads[n // RING, n % RING, :, pl.ds(q * QUARTER + t * LANES, LANES)].astype(F32)
                   for q in range(RING)]
            for i in range(RING):
                parts = [g[12 * i:12 * i + 12] for g in got]
                cf[i, n, :, pl.ds(t * LANES, LANES)] = jnp.concatenate(parts, axis=0).astype(BF)
        return carry

    loading[0].wait()
    lax.fori_loop(0, RING * RING, fold, 0)
    c1[0]()
    loading[1].wait()
    loading[2].wait()
    for step in (1, 2):
        a1[step]()
        b1[step]()
        if step == 2:
            a2 = ring_sum(18, "z", lambda i, c: sa.at[i, :, pl.ds(c.start - FOLDED, c.size)],
                          lambda d, i, c: sa[d, :, pl.ds(pl.multiple_of(c.start - FOLDED, LANES), LANES)],
                          ra2, fa2, 0, FOLDED, SPLIT, store_parts_at(FOLDED))
            b2 = ring_sum(24, "x", lambda i, c: sb.at[i, :, pl.ds(c.start - SPLIT, c.size)],
                          lambda d, i, c: sb[d, :, pl.ds(pl.multiple_of(c.start - SPLIT, LANES), LANES)],
                          rb2, fb2, 0, SPLIT, cols, store_parts_at(FOLDED))
            a2[0]()
            b2[0]()
        c1[step]()
    c2 = ring_sum(30, "x", lambda i, c: sc1.at[pl.ds(i * RING, RING), :, c],
                  lambda d, i, c: sc1[d * RING + i, :, c],
                  rc2, fc2, RING, 0, QUARTER, store_to(sc2))
    c2[0]()
    for step in (1, 2):
        a2[step]()
        b2[step]()
        c2[step]()
    c3 = ring_sum(36, "z", lambda i, c: sc2.at[i, :, c], lambda d, i, c: sc2[d, :, c],
                  rc3, fc3, 0, 0, QUARTER, store_c)
    last = ring_sum(42, "y", lambda i, c: sy.at[i, :, c], lambda d, i, c: sy[d, :, c],
                    ry, fy, 0, 0, cols - FOLDED, store_out)
    for step in range(3):
        last[step]()
        c3[step]()


def scatter_rows(grads):
    cols = grads.shape[1]
    wa, wb, wy = SPLIT - FOLDED, cols - SPLIT, cols - FOLDED
    vm = lambda *shape: pltpu.VMEM(shape, BF)
    return pl.pallas_call(
        functools.partial(scatter_kernel, cols),
        out_shape=(jax.ShapeDtypeStruct((16, wy), F32), jax.ShapeDtypeStruct((48, QUARTER), F32)),
        in_specs=[pl.BlockSpec(memory_space=pl.ANY)],
        out_specs=(pl.BlockSpec(memory_space=pltpu.VMEM),) * 2,
        scratch_shapes=[
            vm(RING, RING, 48, cols),
            vm(RING, 48, wa), vm(RING, 48, wb), vm(2, RING, 48, wa), vm(2, RING, 48, wb),
            vm(RING, 48, wa), vm(RING, 48, wb),
            vm(48, wa), vm(48, wb), vm(2, 48, wa), vm(2, 48, wb),
            vm(RING, 16, wy), vm(16, wy), vm(2, 16, wy),
            vm(RING, RING * RING, 48, QUARTER), vm(RING * RING, 48, QUARTER), vm(2, RING * RING, 48, QUARTER),
            vm(RING * RING, 48, QUARTER), vm(RING, 48, QUARTER), vm(2, RING, 48, QUARTER),
            vm(RING, 48, QUARTER), vm(48, QUARTER), vm(2, 48, QUARTER),
            pltpu.SemaphoreType.DMA((48,)),
            pltpu.SemaphoreType.DMA((48,)),
            pltpu.SemaphoreType.DMA((3,)),
        ],
        compiler_params=pltpu.CompilerParams(
            collective_id=1, has_side_effects=True, vmem_limit_bytes=56 << 20),
    )(grads.reshape(RING, RING, 48, cols))


ROWS = 256
WIDTH = 768
HALF = 384
HEADS = 6
COLS = 7808
CHUNKS = 6
SLOTS = 768
CAPACITY = 12
EXPERTS = 64
BUCKETS = 32
VMEM_BYTES = 56 << 20


def matmul(a, b):
    return jnp.dot(a, b, preferred_element_type=F32)


def matmul_nt(a, b):
    return lax.dot_general(a, b, (((1,), (1,)), ((), ())), preferred_element_type=F32)


def matmul_tn(a, b):
    return lax.dot_general(a, b, (((0,), (0,)), ((), ())), preferred_element_type=F32)


def norm_factor(v):
    return lax.rsqrt(jnp.mean(v * v, axis=-1, keepdims=True) + EPSILON)


def norm_back(v, gain, du):
    r = norm_factor(v)
    inner = jnp.sum(du * gain * v, axis=-1, keepdims=True) / WIDTH
    dgain = jnp.sum(du * v * r, axis=0, keepdims=True)
    return r * gain * du - v * (r * r * r) * inner, dgain


def greet_pair():
    barrier = pltpu.get_barrier_semaphore()
    peer = {"tensor": 1 - lax.axis_index("tensor")}
    pl.semaphore_signal(barrier, inc=1, device_id=peer, device_id_type=MESH)


def to_pair(src, dst, sems):
    return pltpu.make_async_remote_copy(
        src_ref=src, dst_ref=dst, send_sem=sems.at[0], recv_sem=sems.at[1],
        device_id={"tensor": 1 - lax.axis_index("tensor")}, device_id_type=MESH)


def pair_total(value, mine, theirs, sems):
    mine[...] = value.astype(BF)
    pl.semaphore_wait(pltpu.get_barrier_semaphore(), 1)
    move = to_pair(mine, theirs, sems)
    move.start()
    move.wait()
    return mine[...].astype(F32) + theirs[...].astype(F32)


def pair_scratch():
    return [pltpu.VMEM((ROWS, WIDTH), BF), pltpu.VMEM((ROWS, WIDTH), BF), pltpu.SemaphoreType.DMA((2,))]


def joint(number):
    return pltpu.CompilerParams(
        collective_id=number, has_side_effects=True, vmem_limit_bytes=VMEM_BYTES)


def gelu_parts(g):
    t = jnp.tanh(GELU_COEF * (g + 0.044715 * g * g * g))
    value = 0.5 * g * (1.0 + t)
    slope = 0.5 * (1.0 + t) + 0.5 * g * (1.0 - t * t) * GELU_COEF * (1.0 + 3 * 0.044715 * g * g)
    return value, slope


def vm():
    return pl.BlockSpec(memory_space=pltpu.VMEM)


def full(shape):
    return pl.BlockSpec(shape, lambda *_: (0,) * len(shape))


def shaped(shape, dtype):
    return jax.ShapeDtypeStruct(shape, dtype)


def params():
    return pltpu.CompilerParams(vmem_limit_bytes=VMEM_BYTES)


def attend_kernel(layer, base, weights, sides, lookup, seg_col, seg_row, next_out, na, qkv, probs,
                  mixed, mine, theirs, sems):
    greet_pair()
    x = base[...].astype(F32)
    gain = sides[64 + 2 * layer:65 + 2 * layer, :].astype(F32)
    normed = (x * norm_factor(x) * gain).astype(BF)
    na[...] = normed
    qkv[...] = matmul(normed, weights[:, :1152]).astype(BF)
    offsets = matmul_nt(sides[...], lookup[...])
    row = lax.broadcasted_iota(jnp.int32, (ROWS, ROWS), 0)
    col = lax.broadcasted_iota(jnp.int32, (ROWS, ROWS), 1)
    allowed = (seg_col[...] == seg_row[...]) & (col <= row)
    outs = []
    for h in range(HEADS):
        at = h * HEAD_DIM
        q = qkv[:, at:at + HEAD_DIM]
        k = qkv[:, HALF + at:HALF + at + HEAD_DIM]
        v = qkv[:, 2 * HALF + at:2 * HALF + at + HEAD_DIM]
        rel = pltpu.roll(jnp.broadcast_to(offsets[68 + h:69 + h, :], (ROWS, ROWS)), 0, 1,
                         stride=1, stride_axis=0)
        s = jnp.where(allowed, matmul_nt(q, k) * HEAD_DIM ** (-0.5) + rel, NEG_FILL)
        e = jnp.exp(s - jnp.max(s, axis=-1, keepdims=True))
        p = (e / jnp.sum(e, axis=-1, keepdims=True)).astype(BF)
        probs[h] = p
        outs.append(matmul(p, v))
    o = jnp.concatenate(outs, axis=1).astype(BF)
    mixed[...] = o
    next_out[...] = x + pair_total(matmul_nt(o, weights[:, 1152:]), mine, theirs, sems)


def attend(layer, base, whole, sides, lookup, seg_col, seg_row):
    return pl.pallas_call(
        functools.partial(attend_kernel, layer),
        grid=(1,),
        out_shape=(
            shaped((ROWS, WIDTH), F32), shaped((ROWS, WIDTH), BF), shaped((ROWS, 1152), BF),
            shaped((HEADS, ROWS, ROWS), BF), shaped((ROWS, HALF), BF)),
        in_specs=[
            full((ROWS, WIDTH)), pl.BlockSpec((WIDTH, 1536), lambda i: (0, 3 + layer)),
            full((128, WIDTH)), full((ROWS, WIDTH)), full((ROWS, 1)), full((1, ROWS))],
        out_specs=(
            full((ROWS, WIDTH)), full((ROWS, WIDTH)), full((ROWS, 1152)),
            full((HEADS, ROWS, ROWS)), full((ROWS, HALF))),
        scratch_shapes=pair_scratch(),
        compiler_params=joint(2 + layer),
    )(base, whole, sides, lookup, seg_col, seg_row)


def dense_kernel(base, weights, sides, next_out, normed_out, gate_up, hidden, acc, mine, theirs, sems):
    c = pl.program_id(0)

    @pl.when(c == 0)
    def _():
        greet_pair()
        x = base[...]
        normed_out[...] = (x * norm_factor(x) * sides[65:66, :].astype(F32)).astype(BF)
        acc[...] = jnp.zeros_like(acc)

    gu = matmul(normed_out[...], weights[:, :512])
    gate_up[...] = gu.astype(BF)
    g, u = gu[:, :256], gu[:, 256:]
    t = jnp.tanh(GELU_COEF * (g + 0.044715 * g * g * g))
    hid = (0.5 * g * (1.0 + t) * u).astype(BF)
    hidden[...] = hid
    acc[...] += matmul_nt(hid, weights[:, 512:])

    @pl.when(c == CHUNKS - 1)
    def _():
        next_out[...] = base[...] + pair_total(acc[...], mine, theirs, sems)


def dense(base, whole, sides):
    return pl.pallas_call(
        dense_kernel,
        grid=(CHUNKS,),
        out_shape=(
            shaped((ROWS, WIDTH), F32), shaped((ROWS, WIDTH), BF), shaped((ROWS, 3072), BF),
            shaped((ROWS, 1536), BF)),
        in_specs=[
            full((ROWS, WIDTH)), pl.BlockSpec((WIDTH, WIDTH), lambda c: (0, c)), full((128, WIDTH))],
        out_specs=(
            full((ROWS, WIDTH)), full((ROWS, WIDTH)),
            pl.BlockSpec((ROWS, 512), lambda c: (0, c)), pl.BlockSpec((ROWS, 256), lambda c: (0, c))),
        scratch_shapes=[pltpu.VMEM((ROWS, WIDTH), F32), *pair_scratch()],
        compiler_params=joint(4),
    )(base, whole, sides)


def ordered(e, j):
    x, z, y = e >> 4, (e >> 2) & 3, e & 3
    first, second, third = ((x, z, y), (z, y, x), (y, x, z))[j]
    return first * 16 + second * 4 + third


def route_kernel(base, sides, ids_col, ids_row, cot, normed_out, first, second,
                 weights_out, packed):
    t = lax.axis_index("tensor")
    x = base[...]
    normed = (x * norm_factor(x) * sides[67:68, :].astype(F32)).astype(BF)
    normed_out[...] = normed
    logits = matmul_nt(normed, sides[:64, :])
    experts_col = lax.broadcasted_iota(jnp.int32, (ROWS, EXPERTS), 1)
    one, two = ids_col[:, 0:1] == experts_col, ids_col[:, 1:2] == experts_col
    pick = lambda mask, v: jnp.sum(jnp.where(mask, v, 0.0), axis=1, keepdims=True)
    margin = pick(one, logits) - pick(two, logits)
    w1 = 1.0 / (1.0 + jnp.exp(-margin))
    w2 = 1.0 / (1.0 + jnp.exp(margin))
    weights_out[...] = jnp.concatenate([w1, w2], axis=1)
    row = lax.broadcasted_iota(jnp.int32, (ROWS, ROWS), 0)
    col = lax.broadcasted_iota(jnp.int32, (ROWS, ROWS), 1)
    as_low = lambda mask: jnp.where(mask, 1.0, 0.0).astype(BF)
    counts = matmul(as_low(col < row), as_low(one | two))
    slots_col = lax.broadcasted_iota(jnp.int32, (ROWS, SLOTS), 1)
    for k, (mask, out) in enumerate(((one, first), (two, second))):
        seen = pick(mask, counts).astype(jnp.int32)
        for j in range(3):
            out[j] = as_low(ordered(ids_col[:, k:k + 1], j) * CAPACITY + seen == slots_col)
    experts_row = lax.broadcasted_iota(jnp.int32, (EXPERTS, ROWS), 0)
    one, two = ids_row[0:1, :] == experts_row, ids_row[1:2, :] == experts_row
    counts = matmul(as_low(one | two), as_low(row < col))
    slots_row = lax.broadcasted_iota(jnp.int32, (SLOTS, ROWS), 0)
    half = pl.ds(pl.multiple_of(t * HALF, HALF), HALF)
    g4 = cot[:, half].astype(F32)
    low = normed_out[:, half]
    scaled = [(w * g4).astype(BF) for w in (w1, w2)]
    seen = [jnp.sum(jnp.where(mask, counts, 0.0), axis=0, keepdims=True).astype(jnp.int32)
            for mask in (one, two)]
    for j in range(3):
        here = [as_low(ordered(ids_row[k:k + 1, :], j) * CAPACITY + seen[k] == slots_row) for k in range(2)]
        if j < 2:
            taken = matmul(here[0] + here[1], low[:, 256 * j:min(256 * j + 256, HALF)]).astype(BF)
            packed[j, :, :taken.shape[1]] = taken
        if j > 0:
            cut = slice(0, LANES) if j == 1 else slice(LANES, HALF)
            back = sum(matmul(here[k], scaled[k][:, cut]) for k in range(2)).astype(BF)
            packed[j, :, 256 - back.shape[1]:] = back


def route(*operands):
    return pl.pallas_call(
        route_kernel,
        out_shape=(
            shaped((ROWS, WIDTH), BF), shaped((3, ROWS, SLOTS), BF),
            shaped((3, ROWS, SLOTS), BF), shaped((ROWS, 2), F32), shaped((3, SLOTS, 256), BF)),
        in_specs=[vm()] * 5,
        out_specs=(vm(),) * 5,
        compiler_params=params(),
    )(*operands)


def expert_kernel(own, recv, wide_gate, wide_up, narrow, wide_grad, narrow_grad, back, xin, dy, x_turned, y_acc, dx_acc):
    c = pl.program_id(0)
    t = lax.axis_index("tensor")

    @pl.when(c == 0)
    def _():
        for h in range(2):
            part = [jnp.where(t == h, own[j], recv[j]) for j in range(3)]
            at = h * HALF
            xin[:, at:at + 256] = part[0]
            xin[:, at + 256:at + HALF] = part[1][:, :LANES]
            dy[:, at:at + LANES] = part[1][:, LANES:]
            dy[:, at + LANES:at + HALF] = part[2]
        x_turned[...] = xin[...].T
        y_acc[...] = jnp.zeros_like(y_acc)
        dx_acc[...] = jnp.zeros_like(dx_acc)

    g, u = matmul(xin[...], wide_gate[...]), matmul(xin[...], wide_up[...])
    value, slope = gelu_parts(g)
    hid = (value * u).astype(BF)
    y_acc[...] += matmul(hid, narrow[...])
    narrow_grad[...] = matmul_tn(hid, dy[...])
    dh = matmul_nt(dy[...], narrow[...])
    dg, du = (dh * u * slope).astype(BF), (dh * value).astype(BF)
    dx_acc[...] += matmul_nt(dg, wide_gate[...]) + matmul_nt(du, wide_up[...])
    wide_grad[:, 0, :] = matmul(x_turned[...], dg)
    wide_grad[:, 1, :] = matmul(x_turned[...], du)

    @pl.when(c == CHUNKS - 1)
    def _():
        for h in range(2):
            at = h * HALF
            back[h, 0] = y_acc[:, at:at + 256].astype(BF)
            back[h, 1, :, :LANES] = y_acc[:, at + 256:at + HALF].astype(BF)
            back[h, 1, :, LANES:] = dx_acc[:, at:at + LANES].astype(BF)
            back[h, 2] = dx_acc[:, at + LANES:at + HALF].astype(BF)


def expert(own, recv, wide, narrow):
    return pl.pallas_call(
        expert_kernel,
        grid=(CHUNKS,),
        out_shape=(
            shaped((WIDTH, 2, 1536), F32), shaped((1536, WIDTH), F32), shaped((2, 3, SLOTS, 256), BF)),
        in_specs=[full((3, SLOTS, 256)), full((3, SLOTS, 256)),
                  pl.BlockSpec((WIDTH, 256), lambda c: (0, c)),
                  pl.BlockSpec((WIDTH, 256), lambda c: (0, CHUNKS + c)),
                  pl.BlockSpec((256, WIDTH), lambda c: (c, 0))],
        out_specs=(pl.BlockSpec((WIDTH, 2, 256), lambda c: (0, 0, c)), pl.BlockSpec((256, WIDTH), lambda c: (c, 0)),
                   full((2, 3, SLOTS, 256))),
        scratch_shapes=[pltpu.VMEM((SLOTS, WIDTH), BF), pltpu.VMEM((SLOTS, WIDTH), BF),
                        pltpu.VMEM((WIDTH, SLOTS), BF), pltpu.VMEM((SLOTS, WIDTH), F32),
                        pltpu.VMEM((SLOTS, WIDTH), F32)],
        compiler_params=params(),
    )(own, recv, wide, wide, narrow)


def combine_kernel(own, recv, first, second, weights, x, normed, cot, ids_col, sides,
                   out, g3, dgain, router_back):
    t = lax.axis_index("tensor")
    ys, dxs = [[], []], []
    for h in range(2):
        part = [jnp.where(t == h, own[j], recv[j]) for j in range(3)]
        for k, chosen in enumerate((first, second)):
            ys[k] += [matmul(chosen[0], part[0]), matmul(chosen[1], part[1][:, :LANES])]
        dxs += [matmul(first[1] + second[1], part[1][:, LANES:]), matmul(first[2] + second[2], part[2])]
    y1, y2 = jnp.concatenate(ys[0], axis=1), jnp.concatenate(ys[1], axis=1)
    g4 = cot[...].astype(F32)
    w1, w2 = weights[:, 0:1], weights[:, 1:2]
    v = x[...]
    out[...] = v + (w1 * y1 + w2 * y2)
    dot = lambda a: jnp.sum(a * g4, axis=1, keepdims=True)
    dm = w1 * w2 * (dot(y1) - dot(y2))
    experts = lax.broadcasted_iota(jnp.int32, (ROWS, EXPERTS), 1)
    signs = (jnp.where(ids_col[:, 0:1] == experts, 1.0, 0.0)
             - jnp.where(ids_col[:, 1:2] == experts, 1.0, 0.0))
    dlogits = (dm * signs).astype(BF)
    router_back[...] = matmul_tn(dlogits, normed[...])
    dn = matmul(dlogits, sides[:64, :]) + jnp.concatenate(dxs, axis=1)
    dv, dg = norm_back(v, sides[67:68, :].astype(F32), dn)
    g3[...] = g4 + dv
    dgain[...] = dg


def combine(*operands):
    return pl.pallas_call(
        combine_kernel,
        out_shape=(shaped((ROWS, WIDTH), F32), shaped((ROWS, WIDTH), F32), shaped((1, WIDTH), F32),
                   shaped((EXPERTS, WIDTH), F32)),
        in_specs=[vm()] * len(operands),
        out_specs=(vm(),) * 4,
        compiler_params=params(),
    )(*operands)


def attend_back_kernel(layer, grad, x, held, weights, sides, lookup, na, qkv, probs, mixed,
                       held_out, bias_back, g_out, dgain, mine, theirs, sems):
    greet_pair()
    g = grad[...]
    db = g.astype(BF)
    held_out[:, 1152:] = matmul_tn(db, mixed[...]).astype(BF)
    back = matmul(db, weights[:, 1152:]).astype(BF)
    row = lax.broadcasted_iota(jnp.int32, (ROWS, ROWS), 0)
    col = lax.broadcasted_iota(jnp.int32, (ROWS, ROWS), 1)
    reverse = jnp.where(row + col == ROWS - 1, 1.0, 0.0).astype(BF)
    dq, dk, dv, sums = [], [], [], []
    for h in range(HEADS):
        at = h * HEAD_DIM
        q = qkv[:, at:at + HEAD_DIM]
        k = qkv[:, HALF + at:HALF + at + HEAD_DIM]
        v = qkv[:, 2 * HALF + at:2 * HALF + at + HEAD_DIM]
        d = back[:, at:at + HEAD_DIM]
        low = probs[h]
        p = low.astype(F32)
        dp = matmul_nt(d, v)
        ds = (p * (dp - jnp.sum(p * dp, axis=-1, keepdims=True))).astype(BF)
        turned = pltpu.roll(matmul(reverse, ds), 1, 1, stride=1, stride_axis=0)
        sums.append(jnp.sum(turned, axis=0, keepdims=True))
        dq.append(matmul(ds, k) * HEAD_DIM ** (-0.5))
        dk.append(matmul_tn(ds, q) * HEAD_DIM ** (-0.5))
        dv.append(matmul_tn(low, d))
    sums = jnp.concatenate(sums + [jnp.zeros((2, ROWS), F32)], axis=0)
    high = sums.astype(BF)
    rest = (sums - high.astype(F32)).astype(BF)
    bias_back[...] = matmul(high, lookup[...]) + matmul(rest, lookup[...])
    dqkv = jnp.concatenate(dq + dk + dv, axis=1).astype(BF)
    held_out[:, :1152] = matmul_tn(na[...], dqkv).astype(BF)
    total = pair_total(matmul_nt(dqkv, weights[:, :1152]), mine, theirs, sems)
    back, dg = norm_back(x[...].astype(F32), sides[64 + 2 * layer:65 + 2 * layer, :].astype(F32), total)
    g_out[...] = g + back
    dgain[...] = dg


def attend_back(layer, grad, x, held, whole, sides, lookup, na, qkv, probs, mixed):
    block = pl.BlockSpec((WIDTH, 1536), lambda i: (0, 3 + layer))
    rows = full((ROWS, WIDTH))
    return pl.pallas_call(
        functools.partial(attend_back_kernel, layer),
        grid=(1,),
        out_shape=(shaped((WIDTH, COLS), BF), shaped((8, WIDTH), F32), shaped((ROWS, WIDTH), F32),
                   shaped((1, WIDTH), F32)),
        in_specs=[rows, rows, pl.BlockSpec(memory_space=pl.ANY), block, full((128, WIDTH)), rows, rows,
                  full((ROWS, 1152)), full((HEADS, ROWS, ROWS)), full((ROWS, HALF))],
        out_specs=(block, full((8, WIDTH)), rows, full((1, WIDTH))),
        scratch_shapes=pair_scratch(),
        input_output_aliases={2: 0},
        compiler_params=joint(6 + layer),
    )(grad, x, held, whole, sides, lookup, na, qkv, probs, mixed)


def dense_back_kernel(grad, x, held, weights, sides, normed, gate_up, hidden,
                      held_out, g_out, dgain, low, low_turned, normed_turned, acc, mine, theirs, sems):
    c = pl.program_id(0)

    @pl.when(c == 0)
    def _():
        greet_pair()
        low[...] = grad[...].astype(BF)
        low_turned[...] = low[...].T
        normed_turned[...] = normed[...].T
        acc[...] = jnp.zeros_like(acc)

    held_out[:, 512:] = matmul(low_turned[...], hidden[...]).astype(BF)
    dh = matmul(low[...], weights[:, 512:])
    gu = gate_up[...].astype(F32)
    g, u = gu[:, :256], gu[:, 256:]
    value, slope = gelu_parts(g)
    dgu = jnp.concatenate([(dh * u * slope).astype(BF), (dh * value).astype(BF)], axis=1)
    held_out[:, :512] = matmul(normed_turned[...], dgu).astype(BF)
    acc[...] += matmul_nt(dgu, weights[:, :512])

    @pl.when(c == CHUNKS - 1)
    def _():
        total = pair_total(acc[...], mine, theirs, sems)
        dv, dg = norm_back(x[...], sides[65:66, :].astype(F32), total)
        g_out[...] = grad[...] + dv
        dgain[...] = dg


def dense_back(grad, x, held, whole, sides, normed, gate_up, hidden):
    rows = full((ROWS, WIDTH))
    block = pl.BlockSpec((WIDTH, WIDTH), lambda c: (0, c))
    return pl.pallas_call(
        dense_back_kernel,
        grid=(CHUNKS,),
        out_shape=(shaped((WIDTH, COLS), BF), shaped((ROWS, WIDTH), F32), shaped((1, WIDTH), F32)),
        in_specs=[rows, rows, pl.BlockSpec(memory_space=pl.ANY), block,
                  full((128, WIDTH)), rows, pl.BlockSpec((ROWS, 512), lambda c: (0, c)),
                  pl.BlockSpec((ROWS, 256), lambda c: (0, c))],
        out_specs=(block, rows, full((1, WIDTH))),
        scratch_shapes=[pltpu.VMEM((ROWS, WIDTH), BF), pltpu.VMEM((WIDTH, ROWS), BF),
                        pltpu.VMEM((WIDTH, ROWS), BF), pltpu.VMEM((ROWS, WIDTH), F32), *pair_scratch()],
        input_output_aliases={2: 0},
        compiler_params=joint(8),
    )(grad, x, held, whole, sides, normed, gate_up, hidden)


def finish_kernel(held, g, router_back, gain0, gain1, gain2, gain3, bias1, bias2, held_out, g_out, turned):
    g_out[...] = g[...]
    turned[:64, :] = router_back[...]
    turned[64:68, :] = jnp.concatenate([gain0[...], gain1[...], gain2[...], gain3[...]], axis=0)
    turned[68:76, :] = bias1[...] + bias2[...]
    turned[76:, :] = jnp.zeros((52, WIDTH), F32)
    held_out[...] = turned[...].T.astype(BF)


def finish(held, *rest):
    return pl.pallas_call(
        finish_kernel,
        grid=(1,),
        out_shape=(shaped((WIDTH, COLS), BF), shaped((ROWS, WIDTH), F32)),
        in_specs=[pl.BlockSpec(memory_space=pl.ANY)] + [full(r.shape) for r in rest],
        out_specs=(pl.BlockSpec((WIDTH, 128), lambda i: (0, 60)), full((ROWS, WIDTH))),
        scratch_shapes=[pltpu.VMEM((128, WIDTH), F32)],
        input_output_aliases={0: 0},
        compiler_params=params(),
    )(held, *rest)


def blank_kernel(out):
    pass


def blank():
    return pl.pallas_call(
        blank_kernel,
        out_shape=shaped((WIDTH, COLS), BF),
        out_specs=pl.BlockSpec(memory_space=pl.ANY),
    )()


def bucket_lookup(layer):
    distance = (-np.arange(ROWS)) % ROWS
    exact = BUCKETS // 2
    levels = np.arange(1, BUCKETS - exact)
    bounds = exact * REACH_RATIO ** (levels / exact)
    far = exact + np.sum(distance[:, None] >= bounds[None, :], axis=1)
    bucket = np.where(distance < exact, distance, far)
    place = (layer * BUCKETS + bucket) * 12
    return jnp.asarray(place[:, None] == np.arange(WIDTH)[None, :], BF)


OUTWARD = (("x", "z", "y"), ("z", "y", "x"), ("y", "x", "z"))
HOMEWARD = (("z", "y", "x"), ("y", "x", "z"), ("x", "z", "y"))


def regroup(got, put):
    got = [g.astype(F32) for g in got]
    for k in range(RING):
        parts = [g[CAPACITY * k:CAPACITY * k + CAPACITY] for g in got]
        put(k, jnp.concatenate(parts, axis=0).astype(BF))


def put_at(ref, index):
    def put(k, value):
        ref[index(k)] = value
    return put


def across_kernel(home, src, own_out, recv_out, start_buf, land1, land2, turned, land3, relays,
                  sends, recvs, pair_sends, pair_recvs):
    near = neighbours()
    x, z, y = places()
    t = lax.axis_index("tensor")
    pair = {"tensor": 1 - t}
    barrier = pltpu.get_barrier_semaphore()
    pl.semaphore_signal(barrier, inc=1, device_id=pair, device_id_type=MESH)
    for axis in "xzy":
        for peer in near[axis]:
            pl.semaphore_signal(barrier, inc=1, device_id={"expert": peer}, device_id_type=MESH)
    pl.semaphore_wait(barrier, 7)

    def to_peer(k, a, b):
        return pltpu.make_async_remote_copy(
            src_ref=a, dst_ref=b, send_sem=pair_sends.at[k], recv_sem=pair_recvs.at[k],
            device_id=pair, device_id_type=MESH)

    def ring(k, axis, block, land):
        m = {"x": x, "z": z, "y": y}[axis]
        up, down = near[axis]
        p, q, o = (m + 1) % RING, (m + 3) % RING, (m + 2) % RING
        left, right = pl.ds(0, LANES), pl.ds(LANES, LANES)

        def copy(n, a, b, peer):
            return pltpu.make_async_remote_copy(
                src_ref=a, dst_ref=b, send_sem=sends.at[6 * k + n], recv_sem=recvs.at[6 * k + n],
                device_id={"expert": peer}, device_id_type=MESH)

        c = [
            copy(0, block(o).at[:, :, left], relays.at[k, 0], up),
            copy(1, block(o).at[:, :, right], relays.at[k, 1], down),
            copy(2, block(p), land(m), up),
            copy(3, block(q), land(m), down),
            copy(4, relays.at[k, 0], land(q).at[:, :, left], up),
            copy(5, relays.at[k, 1], land(p).at[:, :, right], down),
        ]

        def start():
            for n in range(4):
                c[n].start()
            land(m)[...] = block(m)[...]

        def relay():
            c[0].wait_recv()
            c[4].start()
            c[1].wait_recv()
            c[5].start()

        def finish():
            for n in range(2, 6):
                c[n].wait_recv()
            for n in range(6):
                c[n].wait_send()

        return start, relay, finish

    def lockstep(rings):
        for step in range(3):
            for r in rings:
                r[step]()

    axes = HOMEWARD if home else OUTWARD
    if home:
        moves = [to_peer(3 + j, src.at[1 - t, j], land3.at[j]) for j in range(3)]
        for move in moves:
            move.start()
        for j, move in enumerate(moves):
            move.wait()
            for n in range(RING):
                total = src[t, j, n].astype(F32) + land3[j, n].astype(F32)
                start_buf[0 if j == 0 else 2 + j, n] = total.astype(BF)
        for n in range(RING):
            regroup([start_buf[3, i, n] for i in range(RING)], put_at(start_buf, lambda k: (1, n, k)))
            regroup([start_buf[4, n, i] for i in range(RING)], put_at(start_buf, lambda k: (2, k, n)))
        first = lambda j: start_buf.at[j]
    else:
        first = lambda j: src.at[j]
    lockstep([ring(j, axes[j][0], lambda i, j=j: first(j).at[i], lambda i, j=j: land1.at[j, i])
              for j in range(3)])
    lockstep([ring(3 + j, axes[j][1], lambda i, j=j: land1.at[j, :, i], lambda i, j=j: land2.at[j, i])
              for j in range(3)])
    for j in range(3):
        over_second = home or j == 2
        for n in range(RING):
            got = [land2[j, i, n] if over_second else land2[j, n, i] for i in range(RING)]
            regroup(got, put_at(turned, lambda k: (j, k, n)))
    if home:
        last = [lambda i, j=j: own_out.at[j, i] for j in range(3)]
    else:
        last = [lambda i: own_out.at[0, :, i], lambda i: land3.at[1, i], lambda i: own_out.at[2, i]]
    lockstep([ring(6 + j, axes[j][2], lambda i, j=j: turned.at[j, i], last[j]) for j in range(3)])
    if not home:
        for n in range(RING):
            regroup([land3[1, i, n] for i in range(RING)], put_at(own_out, lambda k: (1, k, n)))
    ends = [to_peer(j, own_out.at[j], recv_out.at[j]) for j in range(3)]
    for end in ends:
        end.start()
    for end in ends:
        end.wait()


def across(packed, home):
    block = (3, RING, RING, 48, 256)
    both = pl.pallas_call(
        functools.partial(across_kernel, home),
        out_shape=(shaped(block, BF), shaped(block, BF)),
        in_specs=[vm()],
        out_specs=(vm(), vm()),
        scratch_shapes=[
            pltpu.VMEM((5, *block[1:]), BF), pltpu.VMEM(block, BF), pltpu.VMEM(block, BF),
            pltpu.VMEM(block, BF), pltpu.VMEM(block, BF), pltpu.VMEM((9, 2, RING, 48, LANES), BF),
            pltpu.SemaphoreType.DMA((54,)), pltpu.SemaphoreType.DMA((54,)),
            pltpu.SemaphoreType.DMA((6,)), pltpu.SemaphoreType.DMA((6,))],
        compiler_params=joint(10 if home else 9),
    )(packed.reshape(*((2,) if home else ()), *block))
    return [a.reshape(3, SLOTS, 256) for a in both]


def feed_place(column):
    chunk, at = divmod(column, WIDTH)
    part, at = divmod(at, 256)
    return part, pl.ds(chunk * 256 + at, LANES)


def pack_kernel(qkv, proj, expander, reducer, small, own):
    own[...] = jnp.zeros_like(own)
    for column in range(0, 4608, LANES):
        part, place = feed_place(column)
        value = reducer[:, place] if part == 2 else expander[:, part, place]
        own[:12, pl.ds(column, LANES)] = value
    for layer in range(2):
        base = 4608 + 1536 * layer
        for k in range(3):
            own[:12, pl.ds(base + k * HALF, HALF)] = qkv[:, k, layer, :]
        own[:12, pl.ds(base + 3 * HALF, HALF)] = proj[:, layer, :]
    own[:12, pl.ds(7680, LANES)] = small[...]


def pack(*operands):
    return pl.pallas_call(
        pack_kernel,
        out_shape=shaped((16, COLS), BF),
        in_specs=[vm()] * 5,
        out_specs=vm(),
    )(*operands)


def unpack_kernel(rows, folded, qkv, proj, expander, reducer, router, gains, bias):
    for column in range(0, 4608, LANES):
        part, place = feed_place(column)
        if column < FOLDED:
            q, at = divmod(column, QUARTER)
            value = folded[:, pl.ds(at, LANES)][12 * q:12 * q + 12]
        else:
            value = rows[:12, pl.ds(column - FOLDED, LANES)]
        if part == 2:
            reducer[:, place] = value
        else:
            expander[:, part, place] = value
    for layer in range(2):
        base = 4608 + 1536 * layer - FOLDED
        for k in range(3):
            qkv[:, k, layer, :] = rows[:12, pl.ds(base + k * HALF, HALF)]
        proj[:, layer, :] = rows[:12, pl.ds(base + 3 * HALF, HALF)]
    side = rows[:, pl.ds(7680 - FOLDED, LANES)]
    router[...] = side[:12, :64]
    bias[...] = side[:1, 68:74]
    gains[...] = side.T[64:68, :12]


def unpack(rows, folded):
    return pl.pallas_call(
        unpack_kernel,
        out_shape=(
            shaped((12, 3, 2, HALF), F32), shaped((12, 2, HALF), F32), shaped((12, 2, 1536), F32),
            shaped((12, 1536), F32), shaped((12, 64), F32), shaped((4, 12), F32), shaped((1, 6), F32)),
        in_specs=[vm()] * 2,
        out_specs=(vm(),) * 7,
    )(rows, folded)


def local(tokens, cotangent, segment_ids, expert_ids, attention, combiner, expander, reducer,
          router, widener, narrower, norm_gains, rel_bias):
    small = jnp.concatenate(
        [router, norm_gains.T, jnp.pad(rel_bias, ((0, 11), (0, 0))), jnp.zeros((12, 54), BF)], axis=1)
    whole = gather_rows(pack(
        attention.transpose(1, 2, 0, 3), combiner.transpose(2, 0, 1), expander, reducer.T, small))
    sides = whole[:, 7680:].T
    seg_col, seg_row = segment_ids[:, None], segment_ids[None, :]
    ids_row = expert_ids.T
    look1, look2 = bucket_lookup(0), bucket_lookup(1)
    wide = widener[0].reshape(WIDTH, -1)

    x1, na1, qkv1, probs1, mixed1 = attend(0, tokens, whole, sides, look1, seg_col, seg_row)
    x2, n2, gate_up, hidden = dense(x1, whole, sides)
    x3, na2, qkv2, probs2, mixed2 = attend(1, x2, whole, sides, look2, seg_col, seg_row)
    n4, first, second, weights, packed = route(x3, sides, expert_ids, ids_row, cotangent)
    wide_grad, narrow_grad, back = expert(*across(packed, False), wide, narrower[0])
    layer_out, g3, gain3, router_back = combine(
        *across(back, True), first, second, weights, x3, n4, cotangent, expert_ids, sides)
    held, bias2, g2, gain2 = attend_back(
        1, g3, x2, blank(), whole, sides, look2, na2, qkv2, probs2, mixed2)
    held, g1, gain1 = dense_back(g2, x1, held, whole, sides, n2, gate_up, hidden)
    held, bias1, g0, gain0 = attend_back(
        0, g1, tokens, held, whole, sides, look1, na1, qkv1, probs1, mixed1)
    held, g0 = finish(held, g0, router_back, gain0, gain1, gain2, gain3, bias1, bias2)
    qkv, proj, expander, reducer, router, gains, bias = unpack(*scatter_rows(held))
    return (
        layer_out, g0, qkv.transpose(2, 0, 1, 3), proj.transpose(1, 2, 0), expander, reducer.T, router, wide_grad[None],
        narrow_grad[None], gains, bias)


def solution(mesh):
    in_specs = (
        P("expert", None),
        P("expert", None),
        P("expert"),
        P("expert", None),
        P(None, "expert", None, "tensor"),
        P(None, "tensor", "expert"),
        P("expert", None, "tensor"),
        P("tensor", "expert"),
        P("expert", None),
        P("expert", None, None, "tensor"),
        P("expert", "tensor", None),
        P(None, "expert"),
        P("expert", "tensor"),
    )
    out_specs = (
        P("expert", None),
        P("expert", None),
        P(None, "expert", None, "tensor"),
        P(None, "tensor", "expert"),
        P("expert", None, "tensor"),
        P("tensor", "expert"),
        P("expert", None),
        P("expert", None, None, "tensor"),
        P("expert", "tensor", None),
        P(None, "expert"),
        P("expert", "tensor"),
    )
    return jax.shard_map(local, mesh=mesh, in_specs=in_specs, out_specs=out_specs, check_vma=False)
```

```python
import functools

import jax
import jax.numpy as jnp
import numpy as np
from jax import lax
from jax.experimental import pallas as pl
from jax.experimental.pallas import tpu as pltpu
from jax.sharding import PartitionSpec as P

HEAD_DIM = 64
EPSILON = 1e-06
NEG_FILL = -1000000000.0
REACH_RATIO = 8.0
GELU_COEF = 0.7978845608028654

MESH = pl.DeviceIdType.MESH
RING = 4
LANES = 128
BF = jnp.bfloat16
F32 = jnp.float32


def places():
    e = lax.axis_index("expert")
    return e // 16, (e // 4) % 4, e % 4


def neighbours():
    x, z, y = places()
    up, down = lambda v: (v + 1) % RING, lambda v: (v + 3) % RING
    at = lambda a, b, c: a * 16 + b * 4 + c
    return {
        "x": (at(up(x), z, y), at(down(x), z, y)),
        "z": (at(x, up(z), y), at(x, down(z), y)),
        "y": (at(x, z, up(y)), at(x, z, down(y))),
    }


def greet(near):
    barrier = pltpu.get_barrier_semaphore()
    for axis in "xzy":
        for peer in near[axis]:
            pl.semaphore_signal(barrier, inc=1, device_id={"expert": peer}, device_id_type=MESH)
    pl.semaphore_wait(barrier, 6)


FOLDED = 3072
QUARTER = FOLDED // RING
SPLIT = 5376
FIRST = 512


def tile_at(t, base=0):
    return pl.ds(pl.multiple_of(base + t * LANES, LANES), LANES)


def gather_kernel(cols, own, out, ring, block, folded, whole_c, stage, sends, recvs, locals_):
    near = neighbours()
    x, z, y = places()
    greet(near)

    def copy(k, src, dst, peer):
        return pltpu.make_async_remote_copy(
            src_ref=src, dst_ref=dst, send_sem=sends.at[k], recv_sem=recvs.at[k],
            device_id={"expert": peer}, device_id_type=MESH)

    def both_ways(k, axis, src, at, lo, hi):
        m = {"x": x, "z": z, "y": y}[axis]
        up, down = near[axis]
        prev, nxt = (m + 3) % RING, (m + 1) % RING
        mid = (lo + hi) // 2 // LANES * LANES
        left, right, full = pl.ds(lo, mid - lo), pl.ds(mid, hi - mid), pl.ds(lo, hi - lo)
        first = copy(k, src, at(m, full), up)
        second = copy(k + 1, src, at(m, full), down)
        third = copy(k + 2, at(prev, left), at(prev, left), up)
        fourth = copy(k + 3, at(nxt, right), at(nxt, right), down)

        def start():
            first.start()
            second.start()

        def relay():
            first.wait_recv()
            third.start()
            second.wait_recv()
            fourth.start()

        def finish():
            third.wait_recv()
            fourth.wait_recv()
            for c in (first, second, third, fourth):
                c.wait_send()

        return start, relay, finish

    def run(*streams):
        for step in range(3):
            for stream in streams:
                stream[step]()

    ab_y = both_ways(0, "y", own.at[:, pl.ds(FOLDED, cols - FOLDED)],
                     lambda i, c: ring.at[i, :, c], 0, cols - FOLDED)
    ab_y[0]()
    for t in range(QUARTER // LANES):
        parts = [own[:, pl.ds(q * QUARTER + t * LANES, LANES)].astype(F32)[:12] for q in range(RING)]
        folded[:, pl.ds(t * LANES, LANES)] = jnp.concatenate(parts, axis=0).astype(BF)
    c1_cols, c2_cols = pl.ds(0, FIRST), pl.ds(FIRST, QUARTER - FIRST)
    c1_z = both_ways(4, "z", folded.at[:, c1_cols], lambda i, c: whole_c.at[x, i, y, :, c], 0, FIRST)
    c2_x = both_ways(8, "x", folded.at[:, c2_cols], lambda i, c: whole_c.at[i, z, y, :, c], FIRST, QUARTER)
    c1_z[0]()
    c2_x[0]()
    whole_c[x, z, y] = folded[...]
    ring[y] = own[:, FOLDED:]
    ab_y[1]()
    c1_z[1]()
    c2_x[1]()
    c1_z[2]()
    c1_x = both_ways(12, "x", whole_c.at[x, :, y, :, c1_cols], lambda i, c: whole_c.at[i, :, y, :, c], 0, FIRST)
    c1_x[0]()
    c2_x[2]()
    c2_z = both_ways(16, "z", whole_c.at[:, z, y, :, c2_cols], lambda i, c: whole_c.at[:, i, y, :, c],
                     FIRST, QUARTER)
    c2_z[0]()
    ab_y[2]()

    def assemble(t, carry):
        parts = [ring[i, :, tile_at(t)].astype(F32)[:12] for i in range(RING)]
        block[:, tile_at(t)] = jnp.concatenate(parts, axis=0).astype(BF)
        return carry

    lax.fori_loop(0, (cols - FOLDED) // LANES, assemble, 0)
    keep = pltpu.make_async_copy(block, out.at[x, z, :, pl.ds(FOLDED, cols - FOLDED)], locals_.at[2])
    keep.start()
    a_cols, b_cols = pl.ds(FOLDED, SPLIT - FOLDED), pl.ds(SPLIT, cols - SPLIT)
    a_z = both_ways(20, "z", block.at[:, pl.ds(0, SPLIT - FOLDED)], lambda i, c: out.at[x, i, :, c], FOLDED, SPLIT)
    b_x = both_ways(24, "x", block.at[:, pl.ds(SPLIT - FOLDED, cols - SPLIT)], lambda i, c: out.at[i, z, :, c],
                    SPLIT, cols)
    a_z[0]()
    b_x[0]()
    c1_x[1]()
    c2_z[1]()
    c1_x[2]()
    c2_z[2]()
    c_y = both_ways(28, "y", whole_c.at[:, :, y], lambda i, c: whole_c.at[:, :, i, :, c], 0, QUARTER)
    c_y[0]()
    a_z[1]()
    b_x[1]()
    keep.wait()
    a_z[2]()
    a_x = both_ways(32, "x", out.at[x, :, :, a_cols], lambda i, c: out.at[i, :, :, c], FOLDED, SPLIT)
    a_x[0]()
    b_x[2]()
    b_z = both_ways(36, "z", out.at[:, z, :, b_cols], lambda i, c: out.at[:, i, :, c], SPLIT, cols)
    b_z[0]()
    c_y[1]()
    a_x[1]()
    b_z[1]()
    c_y[2]()

    def unfold(n, slot):
        def one(t, carry):
            got = [whole_c[n // RING, n % RING, i, :, tile_at(t)].astype(F32) for i in range(RING)]
            for q in range(RING):
                parts = [g[12 * q:12 * q + 12] for g in got]
                stage[slot, :, tile_at(t, q * QUARTER)] = jnp.concatenate(parts, axis=0).astype(BF)
            return carry
        lax.fori_loop(0, QUARTER // LANES, one, 0)

    def write(n, slot):
        return pltpu.make_async_copy(
            stage.at[slot], out.at[n // RING, n % RING, :, pl.ds(0, FOLDED)], locals_.at[slot])

    def pair(j, carry):
        for slot in range(2):
            n = 2 * j + slot

            @pl.when(j > 0)
            def _():
                write(n, slot).wait()

            unfold(n, slot)
            write(n, slot).start()
        return carry

    lax.fori_loop(0, RING * RING // 2, pair, 0)
    for slot in range(2):
        write(slot, slot).wait()
    a_x[2]()
    b_z[2]()


def gather_rows(own):
    cols = own.shape[1]
    out = pl.pallas_call(
        functools.partial(gather_kernel, cols),
        out_shape=jax.ShapeDtypeStruct((RING, RING, 48, cols), BF),
        in_specs=[pl.BlockSpec(memory_space=pltpu.VMEM)],
        out_specs=pl.BlockSpec(memory_space=pltpu.HBM),
        scratch_shapes=[
            pltpu.VMEM((RING, 16, cols - FOLDED), BF),
            pltpu.VMEM((48, cols - FOLDED), BF),
            pltpu.VMEM((48, QUARTER), BF),
            pltpu.VMEM((RING, RING, RING, 48, QUARTER), BF),
            pltpu.VMEM((2, 48, FOLDED), BF),
            pltpu.SemaphoreType.DMA((40,)),
            pltpu.SemaphoreType.DMA((40,)),
            pltpu.SemaphoreType.DMA((3,)),
        ],
        compiler_params=pltpu.CompilerParams(
            collective_id=0, has_side_effects=True, vmem_limit_bytes=60 << 20),
    )(own)
    return out.reshape(768, cols)


def scatter_kernel(cols, held, out, out_c, grads, ra1, rb1, fa1, fb1, sa, sb, ra2, rb2, fa2, fb2,
                   sy, ry, fy, cf, rc1, fc1, sc1, rc2, fc2, sc2, rc3, fc3,
                   rd2, fd2, sd2, rd3, fd3, sends, recvs, loads):
    near = neighbours()
    x, z, y = places()
    loading = [pltpu.make_async_copy(held.at[:, :, :, c], grads.at[:, :, :, c], loads.at[n])
               for n, c in enumerate((pl.ds(0, FOLDED), pl.ds(FOLDED, SPLIT - FOLDED), pl.ds(SPLIT, cols - SPLIT)))]
    for load_part in loading:
        load_part.start()
    greet(near)

    def copy(k, src, dst, peer):
        return pltpu.make_async_remote_copy(
            src_ref=src, dst_ref=dst, send_sem=sends.at[k], recv_sem=recvs.at[k],
            device_id={"expert": peer}, device_id_type=MESH)

    def ring_sum(k, axis, at, load, relay_buf, final_buf, lead, lo, hi, store):
        width = hi - lo
        half = width // 2 // LANES * LANES
        m = {"x": x, "z": z, "y": y}[axis]
        up, down = near[axis]
        p, q, o = (m + 1) % RING, (m + 3) % RING, (m + 2) % RING
        left, right = pl.ds(0, half), pl.ds(half, width - half)
        g_left, g_right = pl.ds(lo, half), pl.ds(lo + half, width - half)
        c = [
            copy(k, at(o, g_left), relay_buf.at[..., left], up),
            copy(k + 1, at(o, g_right), relay_buf.at[..., right], down),
            copy(k + 2, at(p, g_right), final_buf.at[0, ..., right], up),
            copy(k + 3, at(q, g_left), final_buf.at[1, ..., left], down),
            copy(k + 4, relay_buf.at[..., left], final_buf.at[0, ..., left], up),
            copy(k + 5, relay_buf.at[..., right], final_buf.at[1, ..., right], down),
        ]

        def tiles(first, count, dest):
            def body(t, carry):
                off = pl.multiple_of(first + t * LANES, LANES)
                here, there = pl.ds(off, LANES), pl.ds(pl.multiple_of(lo + off, LANES), LANES)
                for i in range(lead or 1):
                    ix = (i,) if lead else ()
                    relay_buf[(*ix, slice(None), here)] = (
                        relay_buf[(*ix, slice(None), here)].astype(F32)
                        + load(dest, i, there).astype(F32)).astype(BF)
                return carry
            lax.fori_loop(0, count, body, 0)

        def start():
            for j in range(4):
                c[j].start()

        def relay():
            c[0].wait_recv()
            tiles(0, half // LANES, p)
            c[4].start()
            c[1].wait_recv()
            tiles(half, (width - half) // LANES, q)
            c[5].start()

        def finish():
            for j in range(2, 6):
                c[j].wait_recv()

            def body(t, carry):
                here = pl.ds(pl.multiple_of(t * LANES, LANES), LANES)
                there = pl.ds(pl.multiple_of(lo + t * LANES, LANES), LANES)
                for i in range(lead or 1):
                    ix = (i,) if lead else ()
                    total = (load(m, i, there).astype(F32)
                             + final_buf[(0, *ix, slice(None), here)].astype(F32)
                             + final_buf[(1, *ix, slice(None), here)].astype(F32))
                    store(i, here, there, total)
                return carry
            lax.fori_loop(0, width // LANES, body, 0)
            for j in range(6):
                c[j].wait_send()

        return start, relay, finish

    def store_to(ref):
        def store(i, here, there, total):
            ref[i, :, here] = total.astype(BF)
        return store

    def store_parts_at(base):
        def store(i, here, there, total):
            spot = pl.ds(pl.multiple_of(there.start - base, LANES), LANES)
            for k in range(RING):
                part = total[12 * k:12 * k + 12]
                sy[k, :, spot] = jnp.concatenate([part, jnp.zeros((4, LANES), F32)], axis=0).astype(BF)
        return store

    def store_out(i, here, there, total):
        out[:, there] = total

    def store_square(i, here, there, total):
        sc1[i // RING, i % RING, :, here] = total.astype(BF)

    def store_wide(ref):
        def store(i, here, there, total):
            ref[i, :, there] = total.astype(BF)
        return store

    def store_c(i, here, there, total):
        out_c[:, there] = total

    a1 = ring_sum(0, "x", lambda i, c: held.at[i, :, :, c], lambda d, i, c: grads[d, i, :, c],
                  ra1, fa1, RING, FOLDED, SPLIT, store_to(sa))
    b1 = ring_sum(6, "z", lambda i, c: held.at[:, i, :, c], lambda d, i, c: grads[i, d, :, c],
                  rb1, fb1, RING, SPLIT, cols, store_to(sb))
    c1 = ring_sum(12, "y", lambda i, c: cf.at[i, :, :, c], lambda d, i, c: cf[d, i, :, c],
                  rc1, fc1, RING * RING, 0, QUARTER, store_square)
    a1[0]()
    b1[0]()

    def fold(n, carry):
        for t in range(QUARTER // LANES):
            got = [grads[n // RING, n % RING, :, pl.ds(q * QUARTER + t * LANES, LANES)].astype(F32)
                   for q in range(RING)]
            for i in range(RING):
                parts = [g[12 * i:12 * i + 12] for g in got]
                cf[i, n, :, pl.ds(t * LANES, LANES)] = jnp.concatenate(parts, axis=0).astype(BF)
        return carry

    loading[0].wait()
    lax.fori_loop(0, RING * RING, fold, 0)
    c1[0]()
    loading[1].wait()
    loading[2].wait()
    for step in (1, 2):
        a1[step]()
        b1[step]()
        if step == 2:
            a2 = ring_sum(18, "z", lambda i, c: sa.at[i, :, pl.ds(c.start - FOLDED, c.size)],
                          lambda d, i, c: sa[d, :, pl.ds(pl.multiple_of(c.start - FOLDED, LANES), LANES)],
                          ra2, fa2, 0, FOLDED, SPLIT, store_parts_at(FOLDED))
            b2 = ring_sum(24, "x", lambda i, c: sb.at[i, :, pl.ds(c.start - SPLIT, c.size)],
                          lambda d, i, c: sb[d, :, pl.ds(pl.multiple_of(c.start - SPLIT, LANES), LANES)],
                          rb2, fb2, 0, SPLIT, cols, store_parts_at(FOLDED))
            a2[0]()
            b2[0]()
        c1[step]()
    c2 = ring_sum(30, "x", lambda i, c: sc1.at[i, :, :, c], lambda d, i, c: sc1[d, i, :, c],
                  rc2, fc2, RING, 0, FIRST, store_wide(sc2))
    d2 = ring_sum(36, "z", lambda i, c: sc1.at[:, i, :, c], lambda d, i, c: sc1[i, d, :, c],
                  rd2, fd2, RING, FIRST, QUARTER, store_wide(sd2))
    c2[0]()
    d2[0]()
    for stream in (a2, b2, c2, d2):
        stream[1]()
    a2[2]()
    b2[2]()
    last = ring_sum(54, "y", lambda i, c: sy.at[i, :, c], lambda d, i, c: sy[d, :, c],
                    ry, fy, 0, 0, cols - FOLDED, store_out)
    last[0]()
    c2[2]()
    c3 = ring_sum(42, "z", lambda i, c: sc2.at[i, :, c], lambda d, i, c: sc2[d, :, c],
                  rc3, fc3, 0, 0, FIRST, store_c)
    c3[0]()
    d2[2]()
    d3 = ring_sum(48, "x", lambda i, c: sd2.at[i, :, c], lambda d, i, c: sd2[d, :, c],
                  rd3, fd3, 0, FIRST, QUARTER, store_c)
    d3[0]()
    for step in (1, 2):
        for stream in (last, c3, d3):
            stream[step]()


def scatter_rows(grads):
    cols = grads.shape[1]
    wa, wb, wy = SPLIT - FOLDED, cols - SPLIT, cols - FOLDED
    vm = lambda *shape: pltpu.VMEM(shape, BF)
    return pl.pallas_call(
        functools.partial(scatter_kernel, cols),
        out_shape=(jax.ShapeDtypeStruct((16, wy), F32), jax.ShapeDtypeStruct((48, QUARTER), F32)),
        in_specs=[pl.BlockSpec(memory_space=pl.ANY)],
        out_specs=(pl.BlockSpec(memory_space=pltpu.VMEM),) * 2,
        scratch_shapes=[
            vm(RING, RING, 48, cols),
            vm(RING, 48, wa), vm(RING, 48, wb), vm(2, RING, 48, wa), vm(2, RING, 48, wb),
            vm(RING, 48, wa), vm(RING, 48, wb),
            vm(48, wa), vm(48, wb), vm(2, 48, wa), vm(2, 48, wb),
            vm(RING, 16, wy), vm(16, wy), vm(2, 16, wy),
            vm(RING, RING * RING, 48, QUARTER), vm(RING * RING, 48, QUARTER), vm(2, RING * RING, 48, QUARTER),
            vm(RING, RING, 48, QUARTER), vm(RING, 48, FIRST), vm(2, RING, 48, FIRST),
            vm(RING, 48, QUARTER), vm(48, FIRST), vm(2, 48, FIRST),
            vm(RING, 48, QUARTER - FIRST), vm(2, RING, 48, QUARTER - FIRST),
            vm(RING, 48, QUARTER), vm(48, QUARTER - FIRST), vm(2, 48, QUARTER - FIRST),
            pltpu.SemaphoreType.DMA((60,)),
            pltpu.SemaphoreType.DMA((60,)),
            pltpu.SemaphoreType.DMA((3,)),
        ],
        compiler_params=pltpu.CompilerParams(
            collective_id=1, has_side_effects=True, vmem_limit_bytes=56 << 20),
    )(grads.reshape(RING, RING, 48, cols))


ROWS = 256
WIDTH = 768
HALF = 384
HEADS = 6
COLS = 7808
CHUNKS = 6
SLOTS = 768
CAPACITY = 12
EXPERTS = 64
BUCKETS = 32
VMEM_BYTES = 56 << 20


def matmul(a, b):
    return jnp.dot(a, b, preferred_element_type=F32)


def matmul_nt(a, b):
    return lax.dot_general(a, b, (((1,), (1,)), ((), ())), preferred_element_type=F32)


def matmul_tn(a, b):
    return lax.dot_general(a, b, (((0,), (0,)), ((), ())), preferred_element_type=F32)


def norm_factor(v):
    return lax.rsqrt(jnp.mean(v * v, axis=-1, keepdims=True) + EPSILON)


def norm_back(v, gain, du):
    r = norm_factor(v)
    inner = jnp.sum(du * gain * v, axis=-1, keepdims=True) / WIDTH
    dgain = jnp.sum(du * v * r, axis=0, keepdims=True)
    return r * gain * du - v * (r * r * r) * inner, dgain


def greet_pair():
    barrier = pltpu.get_barrier_semaphore()
    peer = {"tensor": 1 - lax.axis_index("tensor")}
    pl.semaphore_signal(barrier, inc=1, device_id=peer, device_id_type=MESH)


def to_pair(src, dst, sems):
    return pltpu.make_async_remote_copy(
        src_ref=src, dst_ref=dst, send_sem=sems.at[0], recv_sem=sems.at[1],
        device_id={"tensor": 1 - lax.axis_index("tensor")}, device_id_type=MESH)


def pair_total(value, mine, theirs, sems):
    mine[...] = value.astype(BF)
    pl.semaphore_wait(pltpu.get_barrier_semaphore(), 1)
    move = to_pair(mine, theirs, sems)
    move.start()
    move.wait()
    return mine[...].astype(F32) + theirs[...].astype(F32)


def pair_scratch():
    return [pltpu.VMEM((ROWS, WIDTH), BF), pltpu.VMEM((ROWS, WIDTH), BF), pltpu.SemaphoreType.DMA((2,))]


def joint(number):
    return pltpu.CompilerParams(
        collective_id=number, has_side_effects=True, vmem_limit_bytes=VMEM_BYTES)


def gelu_parts(g):
    t = jnp.tanh(GELU_COEF * (g + 0.044715 * g * g * g))
    value = 0.5 * g * (1.0 + t)
    slope = 0.5 * (1.0 + t) + 0.5 * g * (1.0 - t * t) * GELU_COEF * (1.0 + 3 * 0.044715 * g * g)
    return value, slope


def vm():
    return pl.BlockSpec(memory_space=pltpu.VMEM)


def full(shape):
    return pl.BlockSpec(shape, lambda *_: (0,) * len(shape))


def shaped(shape, dtype):
    return jax.ShapeDtypeStruct(shape, dtype)


def params():
    return pltpu.CompilerParams(vmem_limit_bytes=VMEM_BYTES)


def attend_kernel(layer, base, weights, sides, lookup, seg_row, next_out, na, qkv, probs,
                  mixed, mine, theirs, sems):
    greet_pair()
    x = base[...].astype(F32)
    gain = sides[64 + 2 * layer:65 + 2 * layer, :].astype(F32)
    normed = (x * norm_factor(x) * gain).astype(BF)
    na[...] = normed
    qkv[...] = matmul(normed, weights[:, :1152]).astype(BF)
    offsets = matmul_nt(sides[...], lookup[...])
    row = lax.broadcasted_iota(jnp.int32, (ROWS, ROWS), 0)
    col = lax.broadcasted_iota(jnp.int32, (ROWS, ROWS), 1)
    segments = jnp.broadcast_to(seg_row[...].astype(F32), (ROWS, ROWS))
    allowed = (segments.T == segments) & (col <= row)
    outs = []
    for h in range(HEADS):
        at = h * HEAD_DIM
        q = qkv[:, at:at + HEAD_DIM]
        k = qkv[:, HALF + at:HALF + at + HEAD_DIM]
        v = qkv[:, 2 * HALF + at:2 * HALF + at + HEAD_DIM]
        rel = pltpu.roll(jnp.broadcast_to(offsets[68 + h:69 + h, :], (ROWS, ROWS)), 0, 1,
                         stride=1, stride_axis=0)
        s = jnp.where(allowed, matmul_nt(q, k) * HEAD_DIM ** (-0.5) + rel, NEG_FILL)
        e = jnp.exp(s - jnp.max(s, axis=-1, keepdims=True))
        p = (e / jnp.sum(e, axis=-1, keepdims=True)).astype(BF)
        probs[h] = p
        outs.append(matmul(p, v))
    o = jnp.concatenate(outs, axis=1).astype(BF)
    mixed[...] = o
    next_out[...] = x + pair_total(matmul_nt(o, weights[:, 1152:]), mine, theirs, sems)


def attend(layer, base, whole, sides, lookup, seg_row):
    return pl.pallas_call(
        functools.partial(attend_kernel, layer),
        grid=(1,),
        out_shape=(
            shaped((ROWS, WIDTH), F32), shaped((ROWS, WIDTH), BF), shaped((ROWS, 1152), BF),
            shaped((HEADS, ROWS, ROWS), BF), shaped((ROWS, HALF), BF)),
        in_specs=[
            full((ROWS, WIDTH)), pl.BlockSpec((WIDTH, 1536), lambda i: (0, 3 + layer)),
            full((128, WIDTH)), full((ROWS, WIDTH)), full((1, ROWS))],
        out_specs=(
            full((ROWS, WIDTH)), full((ROWS, WIDTH)), full((ROWS, 1152)),
            full((HEADS, ROWS, ROWS)), full((ROWS, HALF))),
        scratch_shapes=pair_scratch(),
        compiler_params=joint(2 + layer),
    )(base, whole, sides, lookup, seg_row)


def dense_kernel(base, weights, sides, next_out, normed_out, gate_up, hidden, acc, mine, theirs, sems):
    c = pl.program_id(0)

    @pl.when(c == 0)
    def _():
        greet_pair()
        x = base[...]
        normed_out[...] = (x * norm_factor(x) * sides[65:66, :].astype(F32)).astype(BF)
        acc[...] = jnp.zeros_like(acc)

    gu = matmul(normed_out[...], weights[:, :512])
    gate_up[...] = gu.astype(BF)
    g, u = gu[:, :256], gu[:, 256:]
    t = jnp.tanh(GELU_COEF * (g + 0.044715 * g * g * g))
    hid = (0.5 * g * (1.0 + t) * u).astype(BF)
    hidden[...] = hid
    acc[...] += matmul_nt(hid, weights[:, 512:])

    @pl.when(c == CHUNKS - 1)
    def _():
        next_out[...] = base[...] + pair_total(acc[...], mine, theirs, sems)


def dense(base, whole, sides):
    return pl.pallas_call(
        dense_kernel,
        grid=(CHUNKS,),
        out_shape=(
            shaped((ROWS, WIDTH), F32), shaped((ROWS, WIDTH), BF), shaped((ROWS, 3072), BF),
            shaped((ROWS, 1536), BF)),
        in_specs=[
            full((ROWS, WIDTH)), pl.BlockSpec((WIDTH, WIDTH), lambda c: (0, c)), full((128, WIDTH))],
        out_specs=(
            full((ROWS, WIDTH)), full((ROWS, WIDTH)),
            pl.BlockSpec((ROWS, 512), lambda c: (0, c)), pl.BlockSpec((ROWS, 256), lambda c: (0, c))),
        scratch_shapes=[pltpu.VMEM((ROWS, WIDTH), F32), *pair_scratch()],
        compiler_params=joint(4),
    )(base, whole, sides)


def columns_of(ids_row):
    wide = [jnp.broadcast_to(ids_row[k:k + 1, :].astype(F32), (LANES, ROWS)) for k in range(2)]
    return [w.T[:, 0:1].astype(jnp.int32) for w in wide]


def ordered(e, j):
    x, z, y = e >> 4, (e >> 2) & 3, e & 3
    first, second, third = ((x, z, y), (z, y, x), (y, x, z))[j]
    return first * 16 + second * 4 + third


def route_kernel(base, sides, ids_row, cot, normed_out, first, second,
                 weights_out, packed):
    t = lax.axis_index("tensor")
    x = base[...]
    normed = (x * norm_factor(x) * sides[67:68, :].astype(F32)).astype(BF)
    normed_out[...] = normed
    logits = matmul_nt(normed, sides[:64, :])
    experts_col = lax.broadcasted_iota(jnp.int32, (ROWS, EXPERTS), 1)
    ids_col = columns_of(ids_row)
    one, two = ids_col[0] == experts_col, ids_col[1] == experts_col
    pick = lambda mask, v: jnp.sum(jnp.where(mask, v, 0.0), axis=1, keepdims=True)
    margin = pick(one, logits) - pick(two, logits)
    w1 = 1.0 / (1.0 + jnp.exp(-margin))
    w2 = 1.0 / (1.0 + jnp.exp(margin))
    weights_out[...] = jnp.concatenate([w1, w2], axis=1)
    row = lax.broadcasted_iota(jnp.int32, (ROWS, ROWS), 0)
    col = lax.broadcasted_iota(jnp.int32, (ROWS, ROWS), 1)
    as_low = lambda mask: jnp.where(mask, 1.0, 0.0).astype(BF)
    counts = matmul(as_low(col < row), as_low(one | two))
    slots_col = lax.broadcasted_iota(jnp.int32, (ROWS, SLOTS), 1)
    for k, (mask, out) in enumerate(((one, first), (two, second))):
        seen = pick(mask, counts).astype(jnp.int32)
        for j in range(3):
            out[j] = as_low(ordered(ids_col[k], j) * CAPACITY + seen == slots_col)
    experts_row = lax.broadcasted_iota(jnp.int32, (EXPERTS, ROWS), 0)
    one, two = ids_row[0:1, :] == experts_row, ids_row[1:2, :] == experts_row
    counts = matmul(as_low(one | two), as_low(row < col))
    slots_row = lax.broadcasted_iota(jnp.int32, (SLOTS, ROWS), 0)
    half = pl.ds(pl.multiple_of(t * HALF, HALF), HALF)
    g4 = cot[:, half].astype(F32)
    low = normed_out[:, half]
    scaled = [(w * g4).astype(BF) for w in (w1, w2)]
    seen = [jnp.sum(jnp.where(mask, counts, 0.0), axis=0, keepdims=True).astype(jnp.int32)
            for mask in (one, two)]
    for j in range(3):
        here = [as_low(ordered(ids_row[k:k + 1, :], j) * CAPACITY + seen[k] == slots_row) for k in range(2)]
        if j < 2:
            taken = matmul(here[0] + here[1], low[:, 256 * j:min(256 * j + 256, HALF)]).astype(BF)
            packed[j, :, :taken.shape[1]] = taken
        if j > 0:
            cut = slice(0, LANES) if j == 1 else slice(LANES, HALF)
            back = sum(matmul(here[k], scaled[k][:, cut]) for k in range(2)).astype(BF)
            packed[j, :, 256 - back.shape[1]:] = back


def route(*operands):
    return pl.pallas_call(
        route_kernel,
        out_shape=(
            shaped((ROWS, WIDTH), BF), shaped((3, ROWS, SLOTS), BF),
            shaped((3, ROWS, SLOTS), BF), shaped((ROWS, 2), F32), shaped((3, SLOTS, 256), BF)),
        in_specs=[vm()] * 4,
        out_specs=(vm(),) * 5,
        compiler_params=params(),
    )(*operands)


def expert_kernel(own, recv, wide_gate, wide_up, narrow, wide_grad, narrow_grad, back, xin, dy, x_turned, y_acc, dx_acc):
    c = pl.program_id(0)
    t = lax.axis_index("tensor")

    @pl.when(c == 0)
    def _():
        for h in range(2):
            part = [jnp.where(t == h, own[j], recv[j]) for j in range(3)]
            at = h * HALF
            xin[:, at:at + 256] = part[0]
            xin[:, at + 256:at + HALF] = part[1][:, :LANES]
            dy[:, at:at + LANES] = part[1][:, LANES:]
            dy[:, at + LANES:at + HALF] = part[2]
        x_turned[...] = xin[...].T
        y_acc[...] = jnp.zeros_like(y_acc)
        dx_acc[...] = jnp.zeros_like(dx_acc)

    g, u = matmul(xin[...], wide_gate[...]), matmul(xin[...], wide_up[...])
    value, slope = gelu_parts(g)
    hid = (value * u).astype(BF)
    y_acc[...] += matmul(hid, narrow[...])
    narrow_grad[...] = matmul_tn(hid, dy[...])
    dh = matmul_nt(dy[...], narrow[...])
    dg, du = (dh * u * slope).astype(BF), (dh * value).astype(BF)
    dx_acc[...] += matmul_nt(dg, wide_gate[...]) + matmul_nt(du, wide_up[...])
    wide_grad[:, 0, :] = matmul(x_turned[...], dg)
    wide_grad[:, 1, :] = matmul(x_turned[...], du)

    @pl.when(c == CHUNKS - 1)
    def _():
        for h in range(2):
            at = h * HALF
            back[h, 0] = y_acc[:, at:at + 256].astype(BF)
            back[h, 1, :, :LANES] = y_acc[:, at + 256:at + HALF].astype(BF)
            back[h, 1, :, LANES:] = dx_acc[:, at:at + LANES].astype(BF)
            back[h, 2] = dx_acc[:, at + LANES:at + HALF].astype(BF)


def expert(own, recv, wide, narrow):
    return pl.pallas_call(
        expert_kernel,
        grid=(CHUNKS,),
        out_shape=(
            shaped((WIDTH, 2, 1536), F32), shaped((1536, WIDTH), F32), shaped((2, 3, SLOTS, 256), BF)),
        in_specs=[full((3, SLOTS, 256)), full((3, SLOTS, 256)),
                  pl.BlockSpec((WIDTH, 256), lambda c: (0, c)),
                  pl.BlockSpec((WIDTH, 256), lambda c: (0, CHUNKS + c)),
                  pl.BlockSpec((256, WIDTH), lambda c: (c, 0))],
        out_specs=(pl.BlockSpec((WIDTH, 2, 256), lambda c: (0, 0, c)), pl.BlockSpec((256, WIDTH), lambda c: (c, 0)),
                   full((2, 3, SLOTS, 256))),
        scratch_shapes=[pltpu.VMEM((SLOTS, WIDTH), BF), pltpu.VMEM((SLOTS, WIDTH), BF),
                        pltpu.VMEM((WIDTH, SLOTS), BF), pltpu.VMEM((SLOTS, WIDTH), F32),
                        pltpu.VMEM((SLOTS, WIDTH), F32)],
        compiler_params=params(),
    )(own, recv, wide, wide, narrow)


def combine_kernel(own, recv, first, second, weights, x, normed, cot, ids_row, sides,
                   out, g3, dgain, router_back):
    t = lax.axis_index("tensor")
    ys, dxs = [[], []], []
    for h in range(2):
        part = [jnp.where(t == h, own[j], recv[j]) for j in range(3)]
        for k, chosen in enumerate((first, second)):
            ys[k] += [matmul(chosen[0], part[0]), matmul(chosen[1], part[1][:, :LANES])]
        dxs += [matmul(first[1] + second[1], part[1][:, LANES:]), matmul(first[2] + second[2], part[2])]
    y1, y2 = jnp.concatenate(ys[0], axis=1), jnp.concatenate(ys[1], axis=1)
    g4 = cot[...].astype(F32)
    w1, w2 = weights[:, 0:1], weights[:, 1:2]
    v = x[...]
    out[...] = v + (w1 * y1 + w2 * y2)
    dot = lambda a: jnp.sum(a * g4, axis=1, keepdims=True)
    dm = w1 * w2 * (dot(y1) - dot(y2))
    experts = lax.broadcasted_iota(jnp.int32, (ROWS, EXPERTS), 1)
    ids_col = columns_of(ids_row)
    signs = jnp.where(ids_col[0] == experts, 1.0, 0.0) - jnp.where(ids_col[1] == experts, 1.0, 0.0)
    dlogits = (dm * signs).astype(BF)
    router_back[...] = matmul_tn(dlogits, normed[...])
    dn = matmul(dlogits, sides[:64, :]) + jnp.concatenate(dxs, axis=1)
    dv, dg = norm_back(v, sides[67:68, :].astype(F32), dn)
    g3[...] = g4 + dv
    dgain[...] = dg


def combine(*operands):
    return pl.pallas_call(
        combine_kernel,
        out_shape=(shaped((ROWS, WIDTH), F32), shaped((ROWS, WIDTH), F32), shaped((1, WIDTH), F32),
                   shaped((EXPERTS, WIDTH), F32)),
        in_specs=[vm()] * len(operands),
        out_specs=(vm(),) * 4,
        compiler_params=params(),
    )(*operands)


def attend_back_kernel(layer, grad, x, held, weights, sides, lookup, na, qkv, probs, mixed,
                       held_out, bias_back, g_out, dgain, mine, theirs, sems):
    greet_pair()
    g = grad[...]
    db = g.astype(BF)
    held_out[:, 1152:] = matmul_tn(db, mixed[...]).astype(BF)
    back = matmul(db, weights[:, 1152:]).astype(BF)
    row = lax.broadcasted_iota(jnp.int32, (ROWS, ROWS), 0)
    col = lax.broadcasted_iota(jnp.int32, (ROWS, ROWS), 1)
    reverse = jnp.where(row + col == ROWS - 1, 1.0, 0.0).astype(BF)
    dq, dk, dv, sums = [], [], [], []
    for h in range(HEADS):
        at = h * HEAD_DIM
        q = qkv[:, at:at + HEAD_DIM]
        k = qkv[:, HALF + at:HALF + at + HEAD_DIM]
        v = qkv[:, 2 * HALF + at:2 * HALF + at + HEAD_DIM]
        d = back[:, at:at + HEAD_DIM]
        low = probs[h]
        p = low.astype(F32)
        dp = matmul_nt(d, v)
        ds = (p * (dp - jnp.sum(p * dp, axis=-1, keepdims=True))).astype(BF)
        turned = pltpu.roll(matmul(reverse, ds), 1, 1, stride=1, stride_axis=0)
        sums.append(jnp.sum(turned, axis=0, keepdims=True))
        dq.append(matmul(ds, k) * HEAD_DIM ** (-0.5))
        dk.append(matmul_tn(ds, q) * HEAD_DIM ** (-0.5))
        dv.append(matmul_tn(low, d))
    sums = jnp.concatenate(sums + [jnp.zeros((2, ROWS), F32)], axis=0)
    high = sums.astype(BF)
    rest = (sums - high.astype(F32)).astype(BF)
    bias_back[...] = matmul(high, lookup[...]) + matmul(rest, lookup[...])
    dqkv = jnp.concatenate(dq + dk + dv, axis=1).astype(BF)
    held_out[:, :1152] = matmul_tn(na[...], dqkv).astype(BF)
    total = pair_total(matmul_nt(dqkv, weights[:, :1152]), mine, theirs, sems)
    back, dg = norm_back(x[...].astype(F32), sides[64 + 2 * layer:65 + 2 * layer, :].astype(F32), total)
    g_out[...] = g + back
    dgain[...] = dg


def attend_back(layer, grad, x, held, whole, sides, lookup, na, qkv, probs, mixed):
    block = pl.BlockSpec((WIDTH, 1536), lambda i: (0, 3 + layer))
    rows = full((ROWS, WIDTH))
    return pl.pallas_call(
        functools.partial(attend_back_kernel, layer),
        grid=(1,),
        out_shape=(shaped((WIDTH, COLS), BF), shaped((8, WIDTH), F32), shaped((ROWS, WIDTH), F32),
                   shaped((1, WIDTH), F32)),
        in_specs=[rows, rows, pl.BlockSpec(memory_space=pl.ANY), block, full((128, WIDTH)), rows, rows,
                  full((ROWS, 1152)), full((HEADS, ROWS, ROWS)), full((ROWS, HALF))],
        out_specs=(block, full((8, WIDTH)), rows, full((1, WIDTH))),
        scratch_shapes=pair_scratch(),
        input_output_aliases={2: 0},
        compiler_params=joint(6 + layer),
    )(grad, x, held, whole, sides, lookup, na, qkv, probs, mixed)


def dense_back_kernel(grad, x, held, weights, sides, normed, gate_up, hidden,
                      held_out, g_out, dgain, low, low_turned, normed_turned, acc, mine, theirs, sems):
    c = pl.program_id(0)

    @pl.when(c == 0)
    def _():
        greet_pair()
        low[...] = grad[...].astype(BF)
        low_turned[...] = low[...].T
        normed_turned[...] = normed[...].T
        acc[...] = jnp.zeros_like(acc)

    held_out[:, 512:] = matmul(low_turned[...], hidden[...]).astype(BF)
    dh = matmul(low[...], weights[:, 512:])
    gu = gate_up[...].astype(F32)
    g, u = gu[:, :256], gu[:, 256:]
    value, slope = gelu_parts(g)
    dgu = jnp.concatenate([(dh * u * slope).astype(BF), (dh * value).astype(BF)], axis=1)
    held_out[:, :512] = matmul(normed_turned[...], dgu).astype(BF)
    acc[...] += matmul_nt(dgu, weights[:, :512])

    @pl.when(c == CHUNKS - 1)
    def _():
        total = pair_total(acc[...], mine, theirs, sems)
        dv, dg = norm_back(x[...], sides[65:66, :].astype(F32), total)
        g_out[...] = grad[...] + dv
        dgain[...] = dg


def dense_back(grad, x, held, whole, sides, normed, gate_up, hidden):
    rows = full((ROWS, WIDTH))
    block = pl.BlockSpec((WIDTH, WIDTH), lambda c: (0, c))
    return pl.pallas_call(
        dense_back_kernel,
        grid=(CHUNKS,),
        out_shape=(shaped((WIDTH, COLS), BF), shaped((ROWS, WIDTH), F32), shaped((1, WIDTH), F32)),
        in_specs=[rows, rows, pl.BlockSpec(memory_space=pl.ANY), block,
                  full((128, WIDTH)), rows, pl.BlockSpec((ROWS, 512), lambda c: (0, c)),
                  pl.BlockSpec((ROWS, 256), lambda c: (0, c))],
        out_specs=(block, rows, full((1, WIDTH))),
        scratch_shapes=[pltpu.VMEM((ROWS, WIDTH), BF), pltpu.VMEM((WIDTH, ROWS), BF),
                        pltpu.VMEM((WIDTH, ROWS), BF), pltpu.VMEM((ROWS, WIDTH), F32), *pair_scratch()],
        input_output_aliases={2: 0},
        compiler_params=joint(8),
    )(grad, x, held, whole, sides, normed, gate_up, hidden)


def finish_kernel(held, g, router_back, gain0, gain1, gain2, gain3, bias1, bias2, held_out, g_out, turned):
    g_out[...] = g[...]
    turned[:64, :] = router_back[...]
    turned[64:68, :] = jnp.concatenate([gain0[...], gain1[...], gain2[...], gain3[...]], axis=0)
    turned[68:76, :] = bias1[...] + bias2[...]
    turned[76:, :] = jnp.zeros((52, WIDTH), F32)
    held_out[...] = turned[...].T.astype(BF)


def finish(held, *rest):
    return pl.pallas_call(
        finish_kernel,
        grid=(1,),
        out_shape=(shaped((WIDTH, COLS), BF), shaped((ROWS, WIDTH), F32)),
        in_specs=[pl.BlockSpec(memory_space=pl.ANY)] + [full(r.shape) for r in rest],
        out_specs=(pl.BlockSpec((WIDTH, 128), lambda i: (0, 60)), full((ROWS, WIDTH))),
        scratch_shapes=[pltpu.VMEM((128, WIDTH), F32)],
        input_output_aliases={0: 0},
        compiler_params=params(),
    )(held, *rest)


def blank_kernel(out):
    pass


def blank():
    return pl.pallas_call(
        blank_kernel,
        out_shape=shaped((WIDTH, COLS), BF),
        out_specs=pl.BlockSpec(memory_space=pl.ANY),
    )()


def bucket_lookup(layer):
    distance = (-np.arange(ROWS)) % ROWS
    exact = BUCKETS // 2
    levels = np.arange(1, BUCKETS - exact)
    bounds = exact * REACH_RATIO ** (levels / exact)
    far = exact + np.sum(distance[:, None] >= bounds[None, :], axis=1)
    bucket = np.where(distance < exact, distance, far)
    place = (layer * BUCKETS + bucket) * 12
    return jnp.asarray(place[:, None] == np.arange(WIDTH)[None, :], BF)


OUTWARD = (("x", "z", "y"), ("z", "y", "x"), ("y", "x", "z"))
HOMEWARD = (("z", "y", "x"), ("y", "x", "z"), ("x", "z", "y"))


def regroup(got, put):
    got = [g.astype(F32) for g in got]
    for k in range(RING):
        parts = [g[CAPACITY * k:CAPACITY * k + CAPACITY] for g in got]
        put(k, jnp.concatenate(parts, axis=0).astype(BF))


def put_at(ref, index):
    def put(k, value):
        ref[index(k)] = value
    return put


def across_kernel(home, src, own_out, recv_out, start_buf, land1, land2, turned, land3, relays,
                  sends, recvs, pair_sends, pair_recvs):
    near = neighbours()
    x, z, y = places()
    t = lax.axis_index("tensor")
    pair = {"tensor": 1 - t}
    barrier = pltpu.get_barrier_semaphore()
    pl.semaphore_signal(barrier, inc=1, device_id=pair, device_id_type=MESH)
    for axis in "xzy":
        for peer in near[axis]:
            pl.semaphore_signal(barrier, inc=1, device_id={"expert": peer}, device_id_type=MESH)
    pl.semaphore_wait(barrier, 7)

    def to_peer(k, a, b):
        return pltpu.make_async_remote_copy(
            src_ref=a, dst_ref=b, send_sem=pair_sends.at[k], recv_sem=pair_recvs.at[k],
            device_id=pair, device_id_type=MESH)

    def ring(k, axis, block, land):
        m = {"x": x, "z": z, "y": y}[axis]
        up, down = near[axis]
        p, q, o = (m + 1) % RING, (m + 3) % RING, (m + 2) % RING
        left, right = pl.ds(0, LANES), pl.ds(LANES, LANES)

        def copy(n, a, b, peer):
            return pltpu.make_async_remote_copy(
                src_ref=a, dst_ref=b, send_sem=sends.at[6 * k + n], recv_sem=recvs.at[6 * k + n],
                device_id={"expert": peer}, device_id_type=MESH)

        c = [
            copy(0, block(o).at[:, :, left], relays.at[k, 0], up),
            copy(1, block(o).at[:, :, right], relays.at[k, 1], down),
            copy(2, block(p), land(m), up),
            copy(3, block(q), land(m), down),
            copy(4, relays.at[k, 0], land(q).at[:, :, left], up),
            copy(5, relays.at[k, 1], land(p).at[:, :, right], down),
        ]

        def start():
            for n in range(4):
                c[n].start()
            land(m)[...] = block(m)[...]

        def relay():
            c[0].wait_recv()
            c[4].start()
            c[1].wait_recv()
            c[5].start()

        def finish():
            for n in range(2, 6):
                c[n].wait_recv()
            for n in range(6):
                c[n].wait_send()

        return start, relay, finish

    axes = HOMEWARD if home else OUTWARD
    begin = (lambda j: start_buf.at[j]) if home else (lambda j: src.at[j])
    if home:
        last = [lambda i, j=j: own_out.at[j, i] for j in range(3)]
    else:
        last = [lambda i: own_out.at[0, :, i], lambda i: land3.at[1, i], lambda i: own_out.at[2, i]]
    rings = [[
        ring(j, axes[j][0], lambda i, j=j: begin(j).at[i], lambda i, j=j: land1.at[j, i]),
        ring(3 + j, axes[j][1], lambda i, j=j: land1.at[j, :, i], lambda i, j=j: land2.at[j, i]),
        ring(6 + j, axes[j][2], lambda i, j=j: turned.at[j, i], last[j]),
    ] for j in range(3)]
    ends = [to_peer(j, own_out.at[j], recv_out.at[j]) for j in range(3)]
    if home:
        moves = [to_peer(3 + j, src.at[1 - t, j], land3.at[j]) for j in range(3)]
        for move in moves:
            move.start()
        for j, move in enumerate(moves):
            move.wait()
            for n in range(RING):
                total = src[t, j, n].astype(F32) + land3[j, n].astype(F32)
                start_buf[0 if j == 0 else 2 + j, n] = total.astype(BF)
            if j == 1:
                for n in range(RING):
                    regroup([start_buf[3, i, n] for i in range(RING)], put_at(start_buf, lambda k: (1, n, k)))
            if j == 2:
                for n in range(RING):
                    regroup([start_buf[4, n, i] for i in range(RING)], put_at(start_buf, lambda k: (2, k, n)))
            rings[j][0][0]()
    else:
        for j in range(3):
            rings[j][0][0]()
    for phase in range(3):
        for j in range(3):
            rings[j][phase][1]()
        for j in range(3):
            rings[j][phase][2]()
            if phase == 1:
                over_second = home or j == 2
                for n in range(RING):
                    got = [land2[j, i, n] if over_second else land2[j, n, i] for i in range(RING)]
                    regroup(got, put_at(turned, lambda k: (j, k, n)))
            if phase < 2:
                rings[j][phase + 1][0]()
            else:
                if j == 1 and not home:
                    for n in range(RING):
                        regroup([land3[1, i, n] for i in range(RING)], put_at(own_out, lambda k: (1, k, n)))
                ends[j].start()
    for end in ends:
        end.wait()


def across(packed, home):
    block = (3, RING, RING, 48, 256)
    both = pl.pallas_call(
        functools.partial(across_kernel, home),
        out_shape=(shaped(block, BF), shaped(block, BF)),
        in_specs=[vm()],
        out_specs=(vm(), vm()),
        scratch_shapes=[
            pltpu.VMEM((5, *block[1:]), BF), pltpu.VMEM(block, BF), pltpu.VMEM(block, BF),
            pltpu.VMEM(block, BF), pltpu.VMEM(block, BF), pltpu.VMEM((9, 2, RING, 48, LANES), BF),
            pltpu.SemaphoreType.DMA((54,)), pltpu.SemaphoreType.DMA((54,)),
            pltpu.SemaphoreType.DMA((6,)), pltpu.SemaphoreType.DMA((6,))],
        compiler_params=joint(10 if home else 9),
    )(packed.reshape(*((2,) if home else ()), *block))
    return [a.reshape(3, SLOTS, 256) for a in both]


def feed_place(column):
    chunk, at = divmod(column, WIDTH)
    part, at = divmod(at, 256)
    return part, pl.ds(chunk * 256 + at, LANES)


def pack_kernel(qkv, proj, expander, reducer, small, own):
    own[...] = jnp.zeros_like(own)
    for column in range(0, 4608, LANES):
        part, place = feed_place(column)
        value = reducer[:, place] if part == 2 else expander[:, part, place]
        own[:12, pl.ds(column, LANES)] = value
    for layer in range(2):
        base = 4608 + 1536 * layer
        for k in range(3):
            own[:12, pl.ds(base + k * HALF, HALF)] = qkv[:, k, layer, :]
        own[:12, pl.ds(base + 3 * HALF, HALF)] = proj[:, layer, :]
    own[:12, pl.ds(7680, LANES)] = small[...]


def pack(*operands):
    return pl.pallas_call(
        pack_kernel,
        out_shape=shaped((16, COLS), BF),
        in_specs=[vm()] * 5,
        out_specs=vm(),
    )(*operands)


def unpack_kernel(rows, folded, qkv, proj, expander, reducer, router, gains, bias):
    for column in range(0, 4608, LANES):
        part, place = feed_place(column)
        if column < FOLDED:
            q, at = divmod(column, QUARTER)
            value = folded[:, pl.ds(at, LANES)][12 * q:12 * q + 12]
        else:
            value = rows[:12, pl.ds(column - FOLDED, LANES)]
        if part == 2:
            reducer[:, place] = value
        else:
            expander[:, part, place] = value
    for layer in range(2):
        base = 4608 + 1536 * layer - FOLDED
        for k in range(3):
            qkv[:, k, layer, :] = rows[:12, pl.ds(base + k * HALF, HALF)]
        proj[:, layer, :] = rows[:12, pl.ds(base + 3 * HALF, HALF)]
    side = rows[:, pl.ds(7680 - FOLDED, LANES)]
    router[...] = side[:12, :64]
    bias[...] = side[:1, 68:74]
    gains[...] = side.T[64:68, :12]


def unpack(rows, folded):
    return pl.pallas_call(
        unpack_kernel,
        out_shape=(
            shaped((12, 3, 2, HALF), F32), shaped((12, 2, HALF), F32), shaped((12, 2, 1536), F32),
            shaped((12, 1536), F32), shaped((12, 64), F32), shaped((4, 12), F32), shaped((1, 6), F32)),
        in_specs=[vm()] * 2,
        out_specs=(vm(),) * 7,
    )(rows, folded)


def local(tokens, cotangent, segment_ids, expert_ids, attention, combiner, expander, reducer,
          router, widener, narrower, norm_gains, rel_bias):
    small = jnp.concatenate(
        [router, norm_gains.T, jnp.pad(rel_bias, ((0, 11), (0, 0))), jnp.zeros((12, 54), BF)], axis=1)
    whole = gather_rows(pack(
        attention.transpose(1, 2, 0, 3), combiner.transpose(2, 0, 1), expander, reducer.T, small))
    sides = whole[:, 7680:].T
    seg_row = segment_ids[None, :]
    ids_row = expert_ids.T
    look1, look2 = bucket_lookup(0), bucket_lookup(1)
    wide = widener[0].reshape(WIDTH, -1)

    x1, na1, qkv1, probs1, mixed1 = attend(0, tokens, whole, sides, look1, seg_row)
    x2, n2, gate_up, hidden = dense(x1, whole, sides)
    x3, na2, qkv2, probs2, mixed2 = attend(1, x2, whole, sides, look2, seg_row)
    n4, first, second, weights, packed = route(x3, sides, ids_row, cotangent)
    wide_grad, narrow_grad, back = expert(*across(packed, False), wide, narrower[0])
    layer_out, g3, gain3, router_back = combine(
        *across(back, True), first, second, weights, x3, n4, cotangent, ids_row, sides)
    held, bias2, g2, gain2 = attend_back(
        1, g3, x2, blank(), whole, sides, look2, na2, qkv2, probs2, mixed2)
    held, g1, gain1 = dense_back(g2, x1, held, whole, sides, n2, gate_up, hidden)
    held, bias1, g0, gain0 = attend_back(
        0, g1, tokens, held, whole, sides, look1, na1, qkv1, probs1, mixed1)
    held, g0 = finish(held, g0, router_back, gain0, gain1, gain2, gain3, bias1, bias2)
    qkv, proj, expander, reducer, router, gains, bias = unpack(*scatter_rows(held))
    return (
        layer_out, g0, qkv.transpose(2, 0, 1, 3), proj.transpose(1, 2, 0), expander, reducer.T, router, wide_grad[None],
        narrow_grad[None], gains, bias)


def solution(mesh):
    in_specs = (
        P("expert", None),
        P("expert", None),
        P("expert"),
        P("expert", None),
        P(None, "expert", None, "tensor"),
        P(None, "tensor", "expert"),
        P("expert", None, "tensor"),
        P("tensor", "expert"),
        P("expert", None),
        P("expert", None, None, "tensor"),
        P("expert", "tensor", None),
        P(None, "expert"),
        P("expert", "tensor"),
    )
    out_specs = (
        P("expert", None),
        P("expert", None),
        P(None, "expert", None, "tensor"),
        P(None, "tensor", "expert"),
        P("expert", None, "tensor"),
        P("tensor", "expert"),
        P("expert", None),
        P("expert", None, None, "tensor"),
        P("expert", "tensor", None),
        P(None, "expert"),
        P("expert", "tensor"),
    )
    return jax.shard_map(local, mesh=mesh, in_specs=in_specs, out_specs=out_specs, check_vma=False)
```

```python
import functools

import jax
import jax.numpy as jnp
import numpy as np
from jax import lax
from jax.experimental import pallas as pl
from jax.experimental.pallas import tpu as pltpu
from jax.sharding import PartitionSpec as P

HEAD_DIM = 64
EPSILON = 1e-06
NEG_FILL = -1000000000.0
REACH_RATIO = 8.0
GELU_COEF = 0.7978845608028654

MESH = pl.DeviceIdType.MESH
RING = 4
LANES = 128
BF = jnp.bfloat16
F32 = jnp.float32


def places():
    e = lax.axis_index("expert")
    return e // 16, (e // 4) % 4, e % 4


def neighbours():
    x, z, y = places()
    up, down = lambda v: (v + 1) % RING, lambda v: (v + 3) % RING
    at = lambda a, b, c: a * 16 + b * 4 + c
    return {
        "x": (at(up(x), z, y), at(down(x), z, y)),
        "z": (at(x, up(z), y), at(x, down(z), y)),
        "y": (at(x, z, up(y)), at(x, z, down(y))),
    }


def greet(near):
    barrier = pltpu.get_barrier_semaphore()
    for axis in "xzy":
        for peer in near[axis]:
            pl.semaphore_signal(barrier, inc=1, device_id={"expert": peer}, device_id_type=MESH)
    pl.semaphore_wait(barrier, 6)


FOLDED = 3072
QUARTER = FOLDED // RING
SPLIT = 5376
FIRST = 512


def tile_at(t, base=0):
    return pl.ds(pl.multiple_of(base + t * LANES, LANES), LANES)


def gather_kernel(cols, own, out, ring, block, folded, whole_c, stage, sends, recvs, locals_):
    near = neighbours()
    x, z, y = places()
    greet(near)

    def copy(k, src, dst, peer):
        return pltpu.make_async_remote_copy(
            src_ref=src, dst_ref=dst, send_sem=sends.at[k], recv_sem=recvs.at[k],
            device_id={"expert": peer}, device_id_type=MESH)

    def both_ways(k, axis, src, at, lo, hi):
        m = {"x": x, "z": z, "y": y}[axis]
        up, down = near[axis]
        prev, nxt = (m + 3) % RING, (m + 1) % RING
        mid = (lo + hi) // 2 // LANES * LANES
        left, right, full = pl.ds(lo, mid - lo), pl.ds(mid, hi - mid), pl.ds(lo, hi - lo)
        first = copy(k, src, at(m, full), up)
        second = copy(k + 1, src, at(m, full), down)
        third = copy(k + 2, at(prev, left), at(prev, left), up)
        fourth = copy(k + 3, at(nxt, right), at(nxt, right), down)

        def start():
            first.start()
            second.start()

        def relay():
            first.wait_recv()
            third.start()
            second.wait_recv()
            fourth.start()

        def finish():
            third.wait_recv()
            fourth.wait_recv()
            for c in (first, second, third, fourth):
                c.wait_send()

        return start, relay, finish

    def run(*streams):
        for step in range(3):
            for stream in streams:
                stream[step]()

    ab_y = both_ways(0, "y", own.at[:, pl.ds(FOLDED, cols - FOLDED)],
                     lambda i, c: ring.at[i, :, c], 0, cols - FOLDED)
    ab_y[0]()
    for t in range(QUARTER // LANES):
        parts = [own[:, pl.ds(q * QUARTER + t * LANES, LANES)].astype(F32)[:12] for q in range(RING)]
        folded[:, pl.ds(t * LANES, LANES)] = jnp.concatenate(parts, axis=0).astype(BF)
    c1_cols, c2_cols = pl.ds(0, FIRST), pl.ds(FIRST, QUARTER - FIRST)
    c1_z = both_ways(4, "z", folded.at[:, c1_cols], lambda i, c: whole_c.at[x, i, y, :, c], 0, FIRST)
    c2_x = both_ways(8, "x", folded.at[:, c2_cols], lambda i, c: whole_c.at[i, z, y, :, c], FIRST, QUARTER)
    c1_z[0]()
    c2_x[0]()
    whole_c[x, z, y] = folded[...]
    ring[y] = own[:, FOLDED:]
    ab_y[1]()
    c1_z[1]()
    c2_x[1]()
    c1_z[2]()
    c1_x = both_ways(12, "x", whole_c.at[x, :, y, :, c1_cols], lambda i, c: whole_c.at[i, :, y, :, c], 0, FIRST)
    c1_x[0]()
    c2_x[2]()
    c2_z = both_ways(16, "z", whole_c.at[:, z, y, :, c2_cols], lambda i, c: whole_c.at[:, i, y, :, c],
                     FIRST, QUARTER)
    c2_z[0]()
    ab_y[2]()

    def assemble(t, carry):
        parts = [ring[i, :, tile_at(t)].astype(F32)[:12] for i in range(RING)]
        block[:, tile_at(t)] = jnp.concatenate(parts, axis=0).astype(BF)
        return carry

    lax.fori_loop(0, (cols - FOLDED) // LANES, assemble, 0)
    keep = pltpu.make_async_copy(block, out.at[x, z, :, pl.ds(FOLDED, cols - FOLDED)], locals_.at[2])
    keep.start()
    a_cols, b_cols = pl.ds(FOLDED, SPLIT - FOLDED), pl.ds(SPLIT, cols - SPLIT)
    a_z = both_ways(20, "z", block.at[:, pl.ds(0, SPLIT - FOLDED)], lambda i, c: out.at[x, i, :, c], FOLDED, SPLIT)
    b_x = both_ways(24, "x", block.at[:, pl.ds(SPLIT - FOLDED, cols - SPLIT)], lambda i, c: out.at[i, z, :, c],
                    SPLIT, cols)
    a_z[0]()
    b_x[0]()
    c1_x[1]()
    c2_z[1]()
    c1_x[2]()
    c2_z[2]()
    c_y = both_ways(28, "y", whole_c.at[:, :, y], lambda i, c: whole_c.at[:, :, i, :, c], 0, QUARTER)
    c_y[0]()
    a_z[1]()
    b_x[1]()
    keep.wait()
    a_z[2]()
    a_x = both_ways(32, "x", out.at[x, :, :, a_cols], lambda i, c: out.at[i, :, :, c], FOLDED, SPLIT)
    a_x[0]()
    b_x[2]()
    b_z = both_ways(36, "z", out.at[:, z, :, b_cols], lambda i, c: out.at[:, i, :, c], SPLIT, cols)
    b_z[0]()
    c_y[1]()
    a_x[1]()
    b_z[1]()
    c_y[2]()

    def unfold(n, slot):
        def one(t, carry):
            got = [whole_c[n // RING, n % RING, i, :, tile_at(t)].astype(F32) for i in range(RING)]
            for q in range(RING):
                parts = [g[12 * q:12 * q + 12] for g in got]
                stage[slot, :, tile_at(t, q * QUARTER)] = jnp.concatenate(parts, axis=0).astype(BF)
            return carry
        lax.fori_loop(0, QUARTER // LANES, one, 0)

    def write(n, slot):
        return pltpu.make_async_copy(
            stage.at[slot], out.at[n // RING, n % RING, :, pl.ds(0, FOLDED)], locals_.at[slot])

    def pair(j, carry):
        for slot in range(2):
            n = 2 * j + slot

            @pl.when(j > 0)
            def _():
                write(n, slot).wait()

            unfold(n, slot)
            write(n, slot).start()
        return carry

    lax.fori_loop(0, RING * RING // 2, pair, 0)
    for slot in range(2):
        write(slot, slot).wait()
    a_x[2]()
    b_z[2]()


def gather_rows(own):
    cols = own.shape[1]
    out = pl.pallas_call(
        functools.partial(gather_kernel, cols),
        out_shape=jax.ShapeDtypeStruct((RING, RING, 48, cols), BF),
        in_specs=[pl.BlockSpec(memory_space=pltpu.VMEM)],
        out_specs=pl.BlockSpec(memory_space=pltpu.HBM),
        scratch_shapes=[
            pltpu.VMEM((RING, 16, cols - FOLDED), BF),
            pltpu.VMEM((48, cols - FOLDED), BF),
            pltpu.VMEM((48, QUARTER), BF),
            pltpu.VMEM((RING, RING, RING, 48, QUARTER), BF),
            pltpu.VMEM((2, 48, FOLDED), BF),
            pltpu.SemaphoreType.DMA((40,)),
            pltpu.SemaphoreType.DMA((40,)),
            pltpu.SemaphoreType.DMA((3,)),
        ],
        compiler_params=pltpu.CompilerParams(
            collective_id=0, has_side_effects=True, vmem_limit_bytes=60 << 20),
    )(own)
    return out.reshape(768, cols)


def scatter_kernel(cols, held, out, out_c, grads, ra1, rb1, fa1, fb1, sa, sb, ra2, rb2, fa2, fb2,
                   sy, ry, fy, cf, rc1, fc1, sc1, rc2, fc2, sc2, rc3, fc3,
                   rd2, fd2, sd2, rd3, fd3, sends, recvs, loads):
    near = neighbours()
    x, z, y = places()
    loading = [pltpu.make_async_copy(held.at[:, :, :, c], grads.at[:, :, :, c], loads.at[n])
               for n, c in enumerate((pl.ds(0, FOLDED), pl.ds(FOLDED, SPLIT - FOLDED), pl.ds(SPLIT, cols - SPLIT)))]
    for load_part in loading:
        load_part.start()
    greet(near)

    def copy(k, src, dst, peer):
        return pltpu.make_async_remote_copy(
            src_ref=src, dst_ref=dst, send_sem=sends.at[k], recv_sem=recvs.at[k],
            device_id={"expert": peer}, device_id_type=MESH)

    def ring_sum(k, axis, at, load, relay_buf, final_buf, lead, lo, hi, store):
        width = hi - lo
        half = width // 2 // LANES * LANES
        m = {"x": x, "z": z, "y": y}[axis]
        up, down = near[axis]
        p, q, o = (m + 1) % RING, (m + 3) % RING, (m + 2) % RING
        left, right = pl.ds(0, half), pl.ds(half, width - half)
        g_left, g_right = pl.ds(lo, half), pl.ds(lo + half, width - half)
        c = [
            copy(k, at(o, g_left), relay_buf.at[..., left], up),
            copy(k + 1, at(o, g_right), relay_buf.at[..., right], down),
            copy(k + 2, at(p, g_right), final_buf.at[0, ..., right], up),
            copy(k + 3, at(q, g_left), final_buf.at[1, ..., left], down),
            copy(k + 4, relay_buf.at[..., left], final_buf.at[0, ..., left], up),
            copy(k + 5, relay_buf.at[..., right], final_buf.at[1, ..., right], down),
        ]

        def tiles(first, count, dest):
            def body(t, carry):
                off = pl.multiple_of(first + t * LANES, LANES)
                here, there = pl.ds(off, LANES), pl.ds(pl.multiple_of(lo + off, LANES), LANES)
                for i in range(lead or 1):
                    ix = (i,) if lead else ()
                    relay_buf[(*ix, slice(None), here)] = (
                        relay_buf[(*ix, slice(None), here)].astype(F32)
                        + load(dest, i, there).astype(F32)).astype(BF)
                return carry
            lax.fori_loop(0, count, body, 0)

        def start():
            for j in range(4):
                c[j].start()

        def relay():
            c[0].wait_recv()
            tiles(0, half // LANES, p)
            c[4].start()
            c[1].wait_recv()
            tiles(half, (width - half) // LANES, q)
            c[5].start()

        def finish():
            for j in range(2, 6):
                c[j].wait_recv()

            def body(t, carry):
                here = pl.ds(pl.multiple_of(t * LANES, LANES), LANES)
                there = pl.ds(pl.multiple_of(lo + t * LANES, LANES), LANES)
                for i in range(lead or 1):
                    ix = (i,) if lead else ()
                    total = (load(m, i, there).astype(F32)
                             + final_buf[(0, *ix, slice(None), here)].astype(F32)
                             + final_buf[(1, *ix, slice(None), here)].astype(F32))
                    store(i, here, there, total)
                return carry
            lax.fori_loop(0, width // LANES, body, 0)
            for j in range(6):
                c[j].wait_send()

        return start, relay, finish

    def store_to(ref):
        def store(i, here, there, total):
            ref[i, :, here] = total.astype(BF)
        return store

    def store_parts_at(base):
        def store(i, here, there, total):
            spot = pl.ds(pl.multiple_of(there.start - base, LANES), LANES)
            for k in range(RING):
                part = total[12 * k:12 * k + 12]
                sy[k, :, spot] = jnp.concatenate([part, jnp.zeros((4, LANES), F32)], axis=0).astype(BF)
        return store

    def store_out(i, here, there, total):
        out[:, there] = total

    def store_square(i, here, there, total):
        sc1[i // RING, i % RING, :, here] = total.astype(BF)

    def store_wide(ref):
        def store(i, here, there, total):
            ref[i, :, there] = total.astype(BF)
        return store

    def store_c(i, here, there, total):
        out_c[:, there] = total

    a1 = ring_sum(0, "x", lambda i, c: held.at[i, :, :, c], lambda d, i, c: grads[d, i, :, c],
                  ra1, fa1, RING, FOLDED, SPLIT, store_to(sa))
    b1 = ring_sum(6, "z", lambda i, c: held.at[:, i, :, c], lambda d, i, c: grads[i, d, :, c],
                  rb1, fb1, RING, SPLIT, cols, store_to(sb))
    c1 = ring_sum(12, "y", lambda i, c: cf.at[i, :, :, c], lambda d, i, c: cf[d, i, :, c],
                  rc1, fc1, RING * RING, 0, QUARTER, store_square)
    a1[0]()
    b1[0]()

    def fold(n, carry):
        for t in range(QUARTER // LANES):
            got = [grads[n // RING, n % RING, :, pl.ds(q * QUARTER + t * LANES, LANES)].astype(F32)
                   for q in range(RING)]
            for i in range(RING):
                parts = [g[12 * i:12 * i + 12] for g in got]
                cf[i, n, :, pl.ds(t * LANES, LANES)] = jnp.concatenate(parts, axis=0).astype(BF)
        return carry

    loading[0].wait()
    lax.fori_loop(0, RING * RING, fold, 0)
    c1[0]()
    loading[1].wait()
    loading[2].wait()
    for step in (1, 2):
        a1[step]()
        b1[step]()
        if step == 2:
            a2 = ring_sum(18, "z", lambda i, c: sa.at[i, :, pl.ds(c.start - FOLDED, c.size)],
                          lambda d, i, c: sa[d, :, pl.ds(pl.multiple_of(c.start - FOLDED, LANES), LANES)],
                          ra2, fa2, 0, FOLDED, SPLIT, store_parts_at(FOLDED))
            b2 = ring_sum(24, "x", lambda i, c: sb.at[i, :, pl.ds(c.start - SPLIT, c.size)],
                          lambda d, i, c: sb[d, :, pl.ds(pl.multiple_of(c.start - SPLIT, LANES), LANES)],
                          rb2, fb2, 0, SPLIT, cols, store_parts_at(FOLDED))
            a2[0]()
            b2[0]()
        c1[step]()
    c2 = ring_sum(30, "x", lambda i, c: sc1.at[i, :, :, c], lambda d, i, c: sc1[d, i, :, c],
                  rc2, fc2, RING, 0, FIRST, store_wide(sc2))
    d2 = ring_sum(36, "z", lambda i, c: sc1.at[:, i, :, c], lambda d, i, c: sc1[i, d, :, c],
                  rd2, fd2, RING, FIRST, QUARTER, store_wide(sd2))
    c2[0]()
    d2[0]()
    for stream in (a2, b2, c2, d2):
        stream[1]()
    a2[2]()
    b2[2]()
    last = ring_sum(54, "y", lambda i, c: sy.at[i, :, c], lambda d, i, c: sy[d, :, c],
                    ry, fy, 0, 0, cols - FOLDED, store_out)
    last[0]()
    c2[2]()
    c3 = ring_sum(42, "z", lambda i, c: sc2.at[i, :, c], lambda d, i, c: sc2[d, :, c],
                  rc3, fc3, 0, 0, FIRST, store_c)
    c3[0]()
    d2[2]()
    d3 = ring_sum(48, "x", lambda i, c: sd2.at[i, :, c], lambda d, i, c: sd2[d, :, c],
                  rd3, fd3, 0, FIRST, QUARTER, store_c)
    d3[0]()
    for step in (1, 2):
        for stream in (last, c3, d3):
            stream[step]()


def scatter_rows(grads):
    cols = grads.shape[1]
    wa, wb, wy = SPLIT - FOLDED, cols - SPLIT, cols - FOLDED
    vm = lambda *shape: pltpu.VMEM(shape, BF)
    return pl.pallas_call(
        functools.partial(scatter_kernel, cols),
        out_shape=(jax.ShapeDtypeStruct((16, wy), F32), jax.ShapeDtypeStruct((48, QUARTER), F32)),
        in_specs=[pl.BlockSpec(memory_space=pl.ANY)],
        out_specs=(pl.BlockSpec(memory_space=pltpu.VMEM),) * 2,
        scratch_shapes=[
            vm(RING, RING, 48, cols),
            vm(RING, 48, wa), vm(RING, 48, wb), vm(2, RING, 48, wa), vm(2, RING, 48, wb),
            vm(RING, 48, wa), vm(RING, 48, wb),
            vm(48, wa), vm(48, wb), vm(2, 48, wa), vm(2, 48, wb),
            vm(RING, 16, wy), vm(16, wy), vm(2, 16, wy),
            vm(RING, RING * RING, 48, QUARTER), vm(RING * RING, 48, QUARTER), vm(2, RING * RING, 48, QUARTER),
            vm(RING, RING, 48, QUARTER), vm(RING, 48, FIRST), vm(2, RING, 48, FIRST),
            vm(RING, 48, QUARTER), vm(48, FIRST), vm(2, 48, FIRST),
            vm(RING, 48, QUARTER - FIRST), vm(2, RING, 48, QUARTER - FIRST),
            vm(RING, 48, QUARTER), vm(48, QUARTER - FIRST), vm(2, 48, QUARTER - FIRST),
            pltpu.SemaphoreType.DMA((60,)),
            pltpu.SemaphoreType.DMA((60,)),
            pltpu.SemaphoreType.DMA((3,)),
        ],
        compiler_params=pltpu.CompilerParams(
            collective_id=1, has_side_effects=True, vmem_limit_bytes=56 << 20),
    )(grads.reshape(RING, RING, 48, cols))


ROWS = 256
WIDTH = 768
HALF = 384
HEADS = 6
COLS = 7808
CHUNKS = 6
EXPERT_STEPS = 3
SLOTS = 768
CAPACITY = 12
EXPERTS = 64
BUCKETS = 32
VMEM_BYTES = 56 << 20


def matmul(a, b):
    return jnp.dot(a, b, preferred_element_type=F32)


def matmul_nt(a, b):
    return lax.dot_general(a, b, (((1,), (1,)), ((), ())), preferred_element_type=F32)


def matmul_tn(a, b):
    return lax.dot_general(a, b, (((0,), (0,)), ((), ())), preferred_element_type=F32)


def norm_factor(v):
    return lax.rsqrt(jnp.mean(v * v, axis=-1, keepdims=True) + EPSILON)


def norm_back(v, gain, du):
    r = norm_factor(v)
    inner = jnp.sum(du * gain * v, axis=-1, keepdims=True) / WIDTH
    dgain = jnp.sum(du * v * r, axis=0, keepdims=True)
    return r * gain * du - v * (r * r * r) * inner, dgain


def greet_pair():
    barrier = pltpu.get_barrier_semaphore()
    peer = {"tensor": 1 - lax.axis_index("tensor")}
    pl.semaphore_signal(barrier, inc=1, device_id=peer, device_id_type=MESH)


def to_pair(src, dst, sems):
    return pltpu.make_async_remote_copy(
        src_ref=src, dst_ref=dst, send_sem=sems.at[0], recv_sem=sems.at[1],
        device_id={"tensor": 1 - lax.axis_index("tensor")}, device_id_type=MESH)


def pair_total(value, mine, theirs, sems):
    mine[...] = value.astype(BF)
    pl.semaphore_wait(pltpu.get_barrier_semaphore(), 1)
    move = to_pair(mine, theirs, sems)
    move.start()
    move.wait()
    return mine[...].astype(F32) + theirs[...].astype(F32)


def pair_scratch():
    return [pltpu.VMEM((ROWS, WIDTH), BF), pltpu.VMEM((ROWS, WIDTH), BF), pltpu.SemaphoreType.DMA((2,))]


def joint(number):
    return pltpu.CompilerParams(
        collective_id=number, has_side_effects=True, vmem_limit_bytes=VMEM_BYTES)


def gelu_parts(g):
    t = jnp.tanh(GELU_COEF * (g + 0.044715 * g * g * g))
    value = 0.5 * g * (1.0 + t)
    slope = 0.5 * (1.0 + t) + 0.5 * g * (1.0 - t * t) * GELU_COEF * (1.0 + 3 * 0.044715 * g * g)
    return value, slope


def vm():
    return pl.BlockSpec(memory_space=pltpu.VMEM)


def full(shape):
    return pl.BlockSpec(shape, lambda *_: (0,) * len(shape))


def shaped(shape, dtype):
    return jax.ShapeDtypeStruct(shape, dtype)


def params():
    return pltpu.CompilerParams(vmem_limit_bytes=VMEM_BYTES)


def attend_kernel(layer, base, weights, sides, lookup, seg_row, next_out, na, qkv, probs,
                  mixed, mine, theirs, sems):
    greet_pair()
    x = base[...].astype(F32)
    gain = sides[64 + 2 * layer:65 + 2 * layer, :].astype(F32)
    normed = (x * norm_factor(x) * gain).astype(BF)
    na[...] = normed
    qkv[...] = matmul(normed, weights[:, :1152]).astype(BF)
    offsets = matmul_nt(sides[...], lookup[...])
    row = lax.broadcasted_iota(jnp.int32, (ROWS, ROWS), 0)
    col = lax.broadcasted_iota(jnp.int32, (ROWS, ROWS), 1)
    segments = jnp.broadcast_to(seg_row[...].astype(F32), (ROWS, ROWS))
    allowed = (segments.T == segments) & (col <= row)
    outs = []
    for h in range(HEADS):
        at = h * HEAD_DIM
        q = qkv[:, at:at + HEAD_DIM]
        k = qkv[:, HALF + at:HALF + at + HEAD_DIM]
        v = qkv[:, 2 * HALF + at:2 * HALF + at + HEAD_DIM]
        rel = pltpu.roll(jnp.broadcast_to(offsets[68 + h:69 + h, :], (ROWS, ROWS)), 0, 1,
                         stride=1, stride_axis=0)
        s = jnp.where(allowed, matmul_nt(q, k) * HEAD_DIM ** (-0.5) + rel, NEG_FILL)
        e = jnp.exp(s - jnp.max(s, axis=-1, keepdims=True))
        p = (e / jnp.sum(e, axis=-1, keepdims=True)).astype(BF)
        probs[h] = p
        outs.append(matmul(p, v))
    o = jnp.concatenate(outs, axis=1).astype(BF)
    mixed[...] = o
    next_out[...] = x + pair_total(matmul_nt(o, weights[:, 1152:]), mine, theirs, sems)


def attend(layer, base, whole, sides, lookup, seg_row):
    return pl.pallas_call(
        functools.partial(attend_kernel, layer),
        grid=(1,),
        out_shape=(
            shaped((ROWS, WIDTH), F32), shaped((ROWS, WIDTH), BF), shaped((ROWS, 1152), BF),
            shaped((HEADS, ROWS, ROWS), BF), shaped((ROWS, HALF), BF)),
        in_specs=[
            full((ROWS, WIDTH)), pl.BlockSpec((WIDTH, 1536), lambda i: (0, 3 + layer)),
            full((128, WIDTH)), full((ROWS, WIDTH)), full((1, ROWS))],
        out_specs=(
            full((ROWS, WIDTH)), full((ROWS, WIDTH)), full((ROWS, 1152)),
            full((HEADS, ROWS, ROWS)), full((ROWS, HALF))),
        scratch_shapes=pair_scratch(),
        compiler_params=joint(2 + layer),
    )(base, whole, sides, lookup, seg_row)


def dense_kernel(base, weights, sides, next_out, normed_out, gate_up, hidden, acc, mine, theirs, sems):
    c = pl.program_id(0)

    @pl.when(c == 0)
    def _():
        greet_pair()
        x = base[...]
        normed_out[...] = (x * norm_factor(x) * sides[65:66, :].astype(F32)).astype(BF)
        acc[...] = jnp.zeros_like(acc)

    gu = matmul(normed_out[...], weights[:, :512])
    gate_up[...] = gu.astype(BF)
    g, u = gu[:, :256], gu[:, 256:]
    t = jnp.tanh(GELU_COEF * (g + 0.044715 * g * g * g))
    hid = (0.5 * g * (1.0 + t) * u).astype(BF)
    hidden[...] = hid
    acc[...] += matmul_nt(hid, weights[:, 512:])

    @pl.when(c == CHUNKS - 1)
    def _():
        next_out[...] = base[...] + pair_total(acc[...], mine, theirs, sems)


def dense(base, whole, sides):
    return pl.pallas_call(
        dense_kernel,
        grid=(CHUNKS,),
        out_shape=(
            shaped((ROWS, WIDTH), F32), shaped((ROWS, WIDTH), BF), shaped((ROWS, 3072), BF),
            shaped((ROWS, 1536), BF)),
        in_specs=[
            full((ROWS, WIDTH)), pl.BlockSpec((WIDTH, WIDTH), lambda c: (0, c)), full((128, WIDTH))],
        out_specs=(
            full((ROWS, WIDTH)), full((ROWS, WIDTH)),
            pl.BlockSpec((ROWS, 512), lambda c: (0, c)), pl.BlockSpec((ROWS, 256), lambda c: (0, c))),
        scratch_shapes=[pltpu.VMEM((ROWS, WIDTH), F32), *pair_scratch()],
        compiler_params=joint(4),
    )(base, whole, sides)


def columns_of(ids_row):
    wide = [jnp.broadcast_to(ids_row[k:k + 1, :].astype(F32), (LANES, ROWS)) for k in range(2)]
    return [w.T[:, 0:1].astype(jnp.int32) for w in wide]


def ordered(e, j):
    x, z, y = e >> 4, (e >> 2) & 3, e & 3
    first, second, third = ((x, z, y), (z, y, x), (y, x, z))[j]
    return first * 16 + second * 4 + third


def route_kernel(base, sides, ids_row, cot, normed_out, first, second,
                 weights_out, packed):
    t = lax.axis_index("tensor")
    x = base[...]
    normed = (x * norm_factor(x) * sides[67:68, :].astype(F32)).astype(BF)
    normed_out[...] = normed
    logits = matmul_nt(normed, sides[:64, :])
    experts_col = lax.broadcasted_iota(jnp.int32, (ROWS, EXPERTS), 1)
    ids_col = columns_of(ids_row)
    one, two = ids_col[0] == experts_col, ids_col[1] == experts_col
    pick = lambda mask, v: jnp.sum(jnp.where(mask, v, 0.0), axis=1, keepdims=True)
    margin = pick(one, logits) - pick(two, logits)
    w1 = 1.0 / (1.0 + jnp.exp(-margin))
    w2 = 1.0 / (1.0 + jnp.exp(margin))
    weights_out[...] = jnp.concatenate([w1, w2], axis=1)
    row = lax.broadcasted_iota(jnp.int32, (ROWS, ROWS), 0)
    col = lax.broadcasted_iota(jnp.int32, (ROWS, ROWS), 1)
    as_low = lambda mask: jnp.where(mask, 1.0, 0.0).astype(BF)
    counts = matmul(as_low(col < row), as_low(one | two))
    slots_col = lax.broadcasted_iota(jnp.int32, (ROWS, SLOTS), 1)
    for k, (mask, out) in enumerate(((one, first), (two, second))):
        seen = pick(mask, counts).astype(jnp.int32)
        for j in range(3):
            out[j] = as_low(ordered(ids_col[k], j) * CAPACITY + seen == slots_col)
    experts_row = lax.broadcasted_iota(jnp.int32, (EXPERTS, ROWS), 0)
    one, two = ids_row[0:1, :] == experts_row, ids_row[1:2, :] == experts_row
    counts = matmul(as_low(one | two), as_low(row < col))
    slots_row = lax.broadcasted_iota(jnp.int32, (SLOTS, ROWS), 0)
    half = pl.ds(pl.multiple_of(t * HALF, HALF), HALF)
    g4 = cot[:, half].astype(F32)
    low = normed_out[:, half]
    scaled = [(w * g4).astype(BF) for w in (w1, w2)]
    seen = [jnp.sum(jnp.where(mask, counts, 0.0), axis=0, keepdims=True).astype(jnp.int32)
            for mask in (one, two)]
    for j in range(3):
        here = [as_low(ordered(ids_row[k:k + 1, :], j) * CAPACITY + seen[k] == slots_row) for k in range(2)]
        if j < 2:
            taken = matmul(here[0] + here[1], low[:, 256 * j:min(256 * j + 256, HALF)]).astype(BF)
            packed[j, :, :taken.shape[1]] = taken
        if j > 0:
            cut = slice(0, LANES) if j == 1 else slice(LANES, HALF)
            back = sum(matmul(here[k], scaled[k][:, cut]) for k in range(2)).astype(BF)
            packed[j, :, 256 - back.shape[1]:] = back


def route(*operands):
    return pl.pallas_call(
        route_kernel,
        out_shape=(
            shaped((ROWS, WIDTH), BF), shaped((3, ROWS, SLOTS), BF),
            shaped((3, ROWS, SLOTS), BF), shaped((ROWS, 2), F32), shaped((3, SLOTS, 256), BF)),
        in_specs=[vm()] * 4,
        out_specs=(vm(),) * 5,
        compiler_params=params(),
    )(*operands)


def expert_kernel(own, recv, wide_gate, wide_up, narrow, wide_grad, narrow_grad, back, xin, dy, x_turned, y_acc, dx_acc):
    c = pl.program_id(0)
    t = lax.axis_index("tensor")

    @pl.when(c == 0)
    def _():
        for h in range(2):
            part = [jnp.where(t == h, own[j], recv[j]) for j in range(3)]
            at = h * HALF
            xin[:, at:at + 256] = part[0]
            xin[:, at + 256:at + HALF] = part[1][:, :LANES]
            dy[:, at:at + LANES] = part[1][:, LANES:]
            dy[:, at + LANES:at + HALF] = part[2]
        x_turned[...] = xin[...].T
        y_acc[...] = jnp.zeros_like(y_acc)
        dx_acc[...] = jnp.zeros_like(dx_acc)

    g, u = matmul(xin[...], wide_gate[...]), matmul(xin[...], wide_up[...])
    value, slope = gelu_parts(g)
    hid = (value * u).astype(BF)
    y_acc[...] += matmul(hid, narrow[...])
    narrow_grad[...] = matmul_tn(hid, dy[...])
    dh = matmul_nt(dy[...], narrow[...])
    dg, du = (dh * u * slope).astype(BF), (dh * value).astype(BF)
    dx_acc[...] += matmul_nt(dg, wide_gate[...]) + matmul_nt(du, wide_up[...])
    wide_grad[:, 0, :] = matmul(x_turned[...], dg)
    wide_grad[:, 1, :] = matmul(x_turned[...], du)

    @pl.when(c == EXPERT_STEPS - 1)
    def _():
        for h in range(2):
            at = h * HALF
            back[h, 0] = y_acc[:, at:at + 256].astype(BF)
            back[h, 1, :, :LANES] = y_acc[:, at + 256:at + HALF].astype(BF)
            back[h, 1, :, LANES:] = dx_acc[:, at:at + LANES].astype(BF)
            back[h, 2] = dx_acc[:, at + LANES:at + HALF].astype(BF)


def expert(own, recv, wide, narrow):
    return pl.pallas_call(
        expert_kernel,
        grid=(EXPERT_STEPS,),
        out_shape=(
            shaped((WIDTH, 2, 1536), F32), shaped((1536, WIDTH), F32), shaped((2, 3, SLOTS, 256), BF)),
        in_specs=[full((3, SLOTS, 256)), full((3, SLOTS, 256)),
                  pl.BlockSpec((WIDTH, 512), lambda c: (0, c)),
                  pl.BlockSpec((WIDTH, 512), lambda c: (0, EXPERT_STEPS + c)),
                  pl.BlockSpec((512, WIDTH), lambda c: (c, 0))],
        out_specs=(pl.BlockSpec((WIDTH, 2, 512), lambda c: (0, 0, c)), pl.BlockSpec((512, WIDTH), lambda c: (c, 0)),
                   full((2, 3, SLOTS, 256))),
        scratch_shapes=[pltpu.VMEM((SLOTS, WIDTH), BF), pltpu.VMEM((SLOTS, WIDTH), BF),
                        pltpu.VMEM((WIDTH, SLOTS), BF), pltpu.VMEM((SLOTS, WIDTH), F32),
                        pltpu.VMEM((SLOTS, WIDTH), F32)],
        compiler_params=params(),
    )(own, recv, wide, wide, narrow)


def combine_kernel(own, recv, first, second, weights, x, normed, cot, ids_row, sides,
                   out, g3, dgain, router_back):
    t = lax.axis_index("tensor")
    ys, dxs = [[], []], []
    for h in range(2):
        part = [jnp.where(t == h, own[j], recv[j]) for j in range(3)]
        for k, chosen in enumerate((first, second)):
            ys[k] += [matmul(chosen[0], part[0]), matmul(chosen[1], part[1][:, :LANES])]
        dxs += [matmul(first[1] + second[1], part[1][:, LANES:]), matmul(first[2] + second[2], part[2])]
    y1, y2 = jnp.concatenate(ys[0], axis=1), jnp.concatenate(ys[1], axis=1)
    g4 = cot[...].astype(F32)
    w1, w2 = weights[:, 0:1], weights[:, 1:2]
    v = x[...]
    out[...] = v + (w1 * y1 + w2 * y2)
    dot = lambda a: jnp.sum(a * g4, axis=1, keepdims=True)
    dm = w1 * w2 * (dot(y1) - dot(y2))
    experts = lax.broadcasted_iota(jnp.int32, (ROWS, EXPERTS), 1)
    ids_col = columns_of(ids_row)
    signs = jnp.where(ids_col[0] == experts, 1.0, 0.0) - jnp.where(ids_col[1] == experts, 1.0, 0.0)
    dlogits = (dm * signs).astype(BF)
    router_back[...] = matmul_tn(dlogits, normed[...])
    dn = matmul(dlogits, sides[:64, :]) + jnp.concatenate(dxs, axis=1)
    dv, dg = norm_back(v, sides[67:68, :].astype(F32), dn)
    g3[...] = g4 + dv
    dgain[...] = dg


def combine(*operands):
    return pl.pallas_call(
        combine_kernel,
        out_shape=(shaped((ROWS, WIDTH), F32), shaped((ROWS, WIDTH), F32), shaped((1, WIDTH), F32),
                   shaped((EXPERTS, WIDTH), F32)),
        in_specs=[vm()] * len(operands),
        out_specs=(vm(),) * 4,
        compiler_params=params(),
    )(*operands)


def attend_back_kernel(layer, grad, x, held, weights, sides, lookup, na, qkv, probs, mixed,
                       held_out, bias_back, g_out, dgain, mine, theirs, sems):
    greet_pair()
    g = grad[...]
    db = g.astype(BF)
    held_out[:, 1152:] = matmul_tn(db, mixed[...]).astype(BF)
    back = matmul(db, weights[:, 1152:]).astype(BF)
    row = lax.broadcasted_iota(jnp.int32, (ROWS, ROWS), 0)
    col = lax.broadcasted_iota(jnp.int32, (ROWS, ROWS), 1)
    reverse = jnp.where(row + col == ROWS - 1, 1.0, 0.0).astype(BF)
    dq, dk, dv, sums = [], [], [], []
    for h in range(HEADS):
        at = h * HEAD_DIM
        q = qkv[:, at:at + HEAD_DIM]
        k = qkv[:, HALF + at:HALF + at + HEAD_DIM]
        v = qkv[:, 2 * HALF + at:2 * HALF + at + HEAD_DIM]
        d = back[:, at:at + HEAD_DIM]
        low = probs[h]
        p = low.astype(F32)
        dp = matmul_nt(d, v)
        ds = (p * (dp - jnp.sum(p * dp, axis=-1, keepdims=True))).astype(BF)
        turned = pltpu.roll(matmul(reverse, ds), 1, 1, stride=1, stride_axis=0)
        sums.append(jnp.sum(turned, axis=0, keepdims=True))
        dq.append(matmul(ds, k) * HEAD_DIM ** (-0.5))
        dk.append(matmul_tn(ds, q) * HEAD_DIM ** (-0.5))
        dv.append(matmul_tn(low, d))
    sums = jnp.concatenate(sums + [jnp.zeros((2, ROWS), F32)], axis=0)
    high = sums.astype(BF)
    rest = (sums - high.astype(F32)).astype(BF)
    bias_back[...] = matmul(high, lookup[...]) + matmul(rest, lookup[...])
    dqkv = jnp.concatenate(dq + dk + dv, axis=1).astype(BF)
    held_out[:, :1152] = matmul_tn(na[...], dqkv).astype(BF)
    total = pair_total(matmul_nt(dqkv, weights[:, :1152]), mine, theirs, sems)
    back, dg = norm_back(x[...].astype(F32), sides[64 + 2 * layer:65 + 2 * layer, :].astype(F32), total)
    g_out[...] = g + back
    dgain[...] = dg


def attend_back(layer, grad, x, held, whole, sides, lookup, na, qkv, probs, mixed):
    block = pl.BlockSpec((WIDTH, 1536), lambda i: (0, 3 + layer))
    rows = full((ROWS, WIDTH))
    return pl.pallas_call(
        functools.partial(attend_back_kernel, layer),
        grid=(1,),
        out_shape=(shaped((WIDTH, COLS), BF), shaped((8, WIDTH), F32), shaped((ROWS, WIDTH), F32),
                   shaped((1, WIDTH), F32)),
        in_specs=[rows, rows, pl.BlockSpec(memory_space=pl.ANY), block, full((128, WIDTH)), rows, rows,
                  full((ROWS, 1152)), full((HEADS, ROWS, ROWS)), full((ROWS, HALF))],
        out_specs=(block, full((8, WIDTH)), rows, full((1, WIDTH))),
        scratch_shapes=pair_scratch(),
        input_output_aliases={2: 0},
        compiler_params=joint(6 + layer),
    )(grad, x, held, whole, sides, lookup, na, qkv, probs, mixed)


def dense_back_kernel(grad, x, held, weights, sides, normed, gate_up, hidden,
                      held_out, g_out, dgain, low, low_turned, normed_turned, acc, mine, theirs, sems):
    c = pl.program_id(0)

    @pl.when(c == 0)
    def _():
        greet_pair()
        low[...] = grad[...].astype(BF)
        low_turned[...] = low[...].T
        normed_turned[...] = normed[...].T
        acc[...] = jnp.zeros_like(acc)

    held_out[:, 512:] = matmul(low_turned[...], hidden[...]).astype(BF)
    dh = matmul(low[...], weights[:, 512:])
    gu = gate_up[...].astype(F32)
    g, u = gu[:, :256], gu[:, 256:]
    value, slope = gelu_parts(g)
    dgu = jnp.concatenate([(dh * u * slope).astype(BF), (dh * value).astype(BF)], axis=1)
    held_out[:, :512] = matmul(normed_turned[...], dgu).astype(BF)
    acc[...] += matmul_nt(dgu, weights[:, :512])

    @pl.when(c == CHUNKS - 1)
    def _():
        total = pair_total(acc[...], mine, theirs, sems)
        dv, dg = norm_back(x[...], sides[65:66, :].astype(F32), total)
        g_out[...] = grad[...] + dv
        dgain[...] = dg


def dense_back(grad, x, held, whole, sides, normed, gate_up, hidden):
    rows = full((ROWS, WIDTH))
    block = pl.BlockSpec((WIDTH, WIDTH), lambda c: (0, c))
    return pl.pallas_call(
        dense_back_kernel,
        grid=(CHUNKS,),
        out_shape=(shaped((WIDTH, COLS), BF), shaped((ROWS, WIDTH), F32), shaped((1, WIDTH), F32)),
        in_specs=[rows, rows, pl.BlockSpec(memory_space=pl.ANY), block,
                  full((128, WIDTH)), rows, pl.BlockSpec((ROWS, 512), lambda c: (0, c)),
                  pl.BlockSpec((ROWS, 256), lambda c: (0, c))],
        out_specs=(block, rows, full((1, WIDTH))),
        scratch_shapes=[pltpu.VMEM((ROWS, WIDTH), BF), pltpu.VMEM((WIDTH, ROWS), BF),
                        pltpu.VMEM((WIDTH, ROWS), BF), pltpu.VMEM((ROWS, WIDTH), F32), *pair_scratch()],
        input_output_aliases={2: 0},
        compiler_params=joint(8),
    )(grad, x, held, whole, sides, normed, gate_up, hidden)


def finish_kernel(held, g, router_back, gain0, gain1, gain2, gain3, bias1, bias2, held_out, g_out, turned):
    g_out[...] = g[...]
    turned[:64, :] = router_back[...]
    turned[64:68, :] = jnp.concatenate([gain0[...], gain1[...], gain2[...], gain3[...]], axis=0)
    turned[68:76, :] = bias1[...] + bias2[...]
    turned[76:, :] = jnp.zeros((52, WIDTH), F32)
    held_out[...] = turned[...].T.astype(BF)


def finish(held, *rest):
    return pl.pallas_call(
        finish_kernel,
        grid=(1,),
        out_shape=(shaped((WIDTH, COLS), BF), shaped((ROWS, WIDTH), F32)),
        in_specs=[pl.BlockSpec(memory_space=pl.ANY)] + [full(r.shape) for r in rest],
        out_specs=(pl.BlockSpec((WIDTH, 128), lambda i: (0, 60)), full((ROWS, WIDTH))),
        scratch_shapes=[pltpu.VMEM((128, WIDTH), F32)],
        input_output_aliases={0: 0},
        compiler_params=params(),
    )(held, *rest)


def blank_kernel(out):
    pass


def blank():
    return pl.pallas_call(
        blank_kernel,
        out_shape=shaped((WIDTH, COLS), BF),
        out_specs=pl.BlockSpec(memory_space=pl.ANY),
    )()


def bucket_lookup(layer):
    distance = (-np.arange(ROWS)) % ROWS
    exact = BUCKETS // 2
    levels = np.arange(1, BUCKETS - exact)
    bounds = exact * REACH_RATIO ** (levels / exact)
    far = exact + np.sum(distance[:, None] >= bounds[None, :], axis=1)
    bucket = np.where(distance < exact, distance, far)
    place = (layer * BUCKETS + bucket) * 12
    return jnp.asarray(place[:, None] == np.arange(WIDTH)[None, :], BF)


OUTWARD = (("x", "z", "y"), ("z", "y", "x"), ("y", "x", "z"))
HOMEWARD = (("z", "y", "x"), ("y", "x", "z"), ("x", "z", "y"))


def regroup(got, put):
    got = [g.astype(F32) for g in got]
    for k in range(RING):
        parts = [g[CAPACITY * k:CAPACITY * k + CAPACITY] for g in got]
        put(k, jnp.concatenate(parts, axis=0).astype(BF))


def put_at(ref, index):
    def put(k, value):
        ref[index(k)] = value
    return put


def across_kernel(home, src, own_out, recv_out, start_buf, land1, land2, turned, land3, relays,
                  sends, recvs, pair_sends, pair_recvs):
    near = neighbours()
    x, z, y = places()
    t = lax.axis_index("tensor")
    pair = {"tensor": 1 - t}
    barrier = pltpu.get_barrier_semaphore()
    pl.semaphore_signal(barrier, inc=1, device_id=pair, device_id_type=MESH)
    for axis in "xzy":
        for peer in near[axis]:
            pl.semaphore_signal(barrier, inc=1, device_id={"expert": peer}, device_id_type=MESH)
    pl.semaphore_wait(barrier, 7)

    def to_peer(k, a, b):
        return pltpu.make_async_remote_copy(
            src_ref=a, dst_ref=b, send_sem=pair_sends.at[k], recv_sem=pair_recvs.at[k],
            device_id=pair, device_id_type=MESH)

    def ring(k, axis, block, land):
        m = {"x": x, "z": z, "y": y}[axis]
        up, down = near[axis]
        p, q, o = (m + 1) % RING, (m + 3) % RING, (m + 2) % RING
        left, right = pl.ds(0, LANES), pl.ds(LANES, LANES)

        def copy(n, a, b, peer):
            return pltpu.make_async_remote_copy(
                src_ref=a, dst_ref=b, send_sem=sends.at[6 * k + n], recv_sem=recvs.at[6 * k + n],
                device_id={"expert": peer}, device_id_type=MESH)

        c = [
            copy(0, block(o).at[:, :, left], relays.at[k, 0], up),
            copy(1, block(o).at[:, :, right], relays.at[k, 1], down),
            copy(2, block(p), land(m), up),
            copy(3, block(q), land(m), down),
            copy(4, relays.at[k, 0], land(q).at[:, :, left], up),
            copy(5, relays.at[k, 1], land(p).at[:, :, right], down),
        ]

        def start():
            for n in range(4):
                c[n].start()
            land(m)[...] = block(m)[...]

        def relay():
            c[0].wait_recv()
            c[4].start()
            c[1].wait_recv()
            c[5].start()

        def finish():
            for n in range(2, 6):
                c[n].wait_recv()
            for n in range(6):
                c[n].wait_send()

        return start, relay, finish

    axes = HOMEWARD if home else OUTWARD
    begin = (lambda j: start_buf.at[j]) if home else (lambda j: src.at[j])
    if home:
        last = [lambda i, j=j: own_out.at[j, i] for j in range(3)]
    else:
        last = [lambda i: own_out.at[0, :, i], lambda i: land3.at[1, i], lambda i: own_out.at[2, i]]
    rings = [[
        ring(j, axes[j][0], lambda i, j=j: begin(j).at[i], lambda i, j=j: land1.at[j, i]),
        ring(3 + j, axes[j][1], lambda i, j=j: land1.at[j, :, i], lambda i, j=j: land2.at[j, i]),
        ring(6 + j, axes[j][2], lambda i, j=j: turned.at[j, i], last[j]),
    ] for j in range(3)]
    ends = [to_peer(j, own_out.at[j], recv_out.at[j]) for j in range(3)]
    if home:
        moves = [to_peer(3 + j, src.at[1 - t, j], land3.at[j]) for j in range(3)]
        for move in moves:
            move.start()
        for j, move in enumerate(moves):
            move.wait()
            for n in range(RING):
                total = src[t, j, n].astype(F32) + land3[j, n].astype(F32)
                start_buf[0 if j == 0 else 2 + j, n] = total.astype(BF)
            if j == 1:
                for n in range(RING):
                    regroup([start_buf[3, i, n] for i in range(RING)], put_at(start_buf, lambda k: (1, n, k)))
            if j == 2:
                for n in range(RING):
                    regroup([start_buf[4, n, i] for i in range(RING)], put_at(start_buf, lambda k: (2, k, n)))
            rings[j][0][0]()
    else:
        for j in range(3):
            rings[j][0][0]()
    for phase in range(3):
        for j in range(3):
            rings[j][phase][1]()
        for j in range(3):
            rings[j][phase][2]()
            if phase == 1:
                over_second = home or j == 2
                for n in range(RING):
                    got = [land2[j, i, n] if over_second else land2[j, n, i] for i in range(RING)]
                    regroup(got, put_at(turned, lambda k: (j, k, n)))
            if phase < 2:
                rings[j][phase + 1][0]()
            else:
                if j == 1 and not home:
                    for n in range(RING):
                        regroup([land3[1, i, n] for i in range(RING)], put_at(own_out, lambda k: (1, k, n)))
                ends[j].start()
    for end in ends:
        end.wait()


def across(packed, home):
    block = (3, RING, RING, 48, 256)
    both = pl.pallas_call(
        functools.partial(across_kernel, home),
        out_shape=(shaped(block, BF), shaped(block, BF)),
        in_specs=[vm()],
        out_specs=(vm(), vm()),
        scratch_shapes=[
            pltpu.VMEM((5, *block[1:]), BF), pltpu.VMEM(block, BF), pltpu.VMEM(block, BF),
            pltpu.VMEM(block, BF), pltpu.VMEM(block, BF), pltpu.VMEM((9, 2, RING, 48, LANES), BF),
            pltpu.SemaphoreType.DMA((54,)), pltpu.SemaphoreType.DMA((54,)),
            pltpu.SemaphoreType.DMA((6,)), pltpu.SemaphoreType.DMA((6,))],
        compiler_params=joint(10 if home else 9),
    )(packed.reshape(*((2,) if home else ()), *block))
    return [a.reshape(3, SLOTS, 256) for a in both]


def feed_place(column):
    chunk, at = divmod(column, WIDTH)
    part, at = divmod(at, 256)
    return part, pl.ds(chunk * 256 + at, LANES)


def pack_kernel(qkv, proj, expander, reducer, small, own):
    own[...] = jnp.zeros_like(own)
    for column in range(0, 4608, LANES):
        part, place = feed_place(column)
        value = reducer[:, place] if part == 2 else expander[:, part, place]
        own[:12, pl.ds(column, LANES)] = value
    for layer in range(2):
        base = 4608 + 1536 * layer
        for k in range(3):
            own[:12, pl.ds(base + k * HALF, HALF)] = qkv[:, k, layer, :]
        own[:12, pl.ds(base + 3 * HALF, HALF)] = proj[:, layer, :]
    own[:12, pl.ds(7680, LANES)] = small[...]


def pack(*operands):
    return pl.pallas_call(
        pack_kernel,
        out_shape=shaped((16, COLS), BF),
        in_specs=[vm()] * 5,
        out_specs=vm(),
    )(*operands)


def unpack_kernel(rows, folded, qkv, proj, expander, reducer, router, gains, bias):
    for column in range(0, 4608, LANES):
        part, place = feed_place(column)
        if column < FOLDED:
            q, at = divmod(column, QUARTER)
            value = folded[:, pl.ds(at, LANES)][12 * q:12 * q + 12]
        else:
            value = rows[:12, pl.ds(column - FOLDED, LANES)]
        if part == 2:
            reducer[:, place] = value
        else:
            expander[:, part, place] = value
    for layer in range(2):
        base = 4608 + 1536 * layer - FOLDED
        for k in range(3):
            qkv[:, k, layer, :] = rows[:12, pl.ds(base + k * HALF, HALF)]
        proj[:, layer, :] = rows[:12, pl.ds(base + 3 * HALF, HALF)]
    side = rows[:, pl.ds(7680 - FOLDED, LANES)]
    router[...] = side[:12, :64]
    bias[...] = side[:1, 68:74]
    gains[...] = side.T[64:68, :12]


def unpack(rows, folded):
    return pl.pallas_call(
        unpack_kernel,
        out_shape=(
            shaped((12, 3, 2, HALF), F32), shaped((12, 2, HALF), F32), shaped((12, 2, 1536), F32),
            shaped((12, 1536), F32), shaped((12, 64), F32), shaped((4, 12), F32), shaped((1, 6), F32)),
        in_specs=[vm()] * 2,
        out_specs=(vm(),) * 7,
    )(rows, folded)


def local(tokens, cotangent, segment_ids, expert_ids, attention, combiner, expander, reducer,
          router, widener, narrower, norm_gains, rel_bias):
    small = jnp.concatenate(
        [router, norm_gains.T, jnp.pad(rel_bias, ((0, 11), (0, 0))), jnp.zeros((12, 54), BF)], axis=1)
    whole = gather_rows(pack(
        attention.transpose(1, 2, 0, 3), combiner.transpose(2, 0, 1), expander, reducer.T, small))
    sides = whole[:, 7680:].T
    seg_row = segment_ids[None, :]
    ids_row = expert_ids.T
    look1, look2 = bucket_lookup(0), bucket_lookup(1)
    wide = widener[0].reshape(WIDTH, -1)

    x1, na1, qkv1, probs1, mixed1 = attend(0, tokens, whole, sides, look1, seg_row)
    x2, n2, gate_up, hidden = dense(x1, whole, sides)
    x3, na2, qkv2, probs2, mixed2 = attend(1, x2, whole, sides, look2, seg_row)
    n4, first, second, weights, packed = route(x3, sides, ids_row, cotangent)
    wide_grad, narrow_grad, back = expert(*across(packed, False), wide, narrower[0])
    layer_out, g3, gain3, router_back = combine(
        *across(back, True), first, second, weights, x3, n4, cotangent, ids_row, sides)
    held, bias2, g2, gain2 = attend_back(
        1, g3, x2, blank(), whole, sides, look2, na2, qkv2, probs2, mixed2)
    held, g1, gain1 = dense_back(g2, x1, held, whole, sides, n2, gate_up, hidden)
    held, bias1, g0, gain0 = attend_back(
        0, g1, tokens, held, whole, sides, look1, na1, qkv1, probs1, mixed1)
    held, g0 = finish(held, g0, router_back, gain0, gain1, gain2, gain3, bias1, bias2)
    qkv, proj, expander, reducer, router, gains, bias = unpack(*scatter_rows(held))
    return (
        layer_out, g0, qkv.transpose(2, 0, 1, 3), proj.transpose(1, 2, 0), expander, reducer.T, router, wide_grad[None],
        narrow_grad[None], gains, bias)


def solution(mesh):
    in_specs = (
        P("expert", None),
        P("expert", None),
        P("expert"),
        P("expert", None),
        P(None, "expert", None, "tensor"),
        P(None, "tensor", "expert"),
        P("expert", None, "tensor"),
        P("tensor", "expert"),
        P("expert", None),
        P("expert", None, None, "tensor"),
        P("expert", "tensor", None),
        P(None, "expert"),
        P("expert", "tensor"),
    )
    out_specs = (
        P("expert", None),
        P("expert", None),
        P(None, "expert", None, "tensor"),
        P(None, "tensor", "expert"),
        P("expert", None, "tensor"),
        P("tensor", "expert"),
        P("expert", None),
        P("expert", None, None, "tensor"),
        P("expert", "tensor", None),
        P(None, "expert"),
        P("expert", "tensor"),
    )
    return jax.shard_map(local, mesh=mesh, in_specs=in_specs, out_specs=out_specs, check_vma=False)
```
